32 devices in a mesh: dp: 8 (over z, x), blk: 4 (over y, core).
Axes of the slice: x: 2, y: 2, z: 4, core: 2. Of those that a mesh axis runs over, the one named last changes fastest.
Arguments:
- patches: bfloat16 [32768, 768], P(('dp', 'blk')), may hold values from -6 to 6
- cotangent: bfloat16 [32768, 768], P(('dp', 'blk')), may hold values from -6 to 6
- short_lengths: int32 [32, 9], P(('dp', 'blk')), may hold values from 1 to 128, 896 in all within a row
- long_lengths: int32 [8], P('dp'), may hold values from 385 to 512, as said below
- w_qkv: float32 [768, 2304], P(('dp', 'blk')), may hold values from -0.21875 to 0.21875
- w_out: float32 [768, 768], P(('dp', 'blk')), may hold values from -0.625 to 0.625
- w_up: float32 [768, 3072], P(('dp', 'blk')), may hold values from -0.21875 to 0.21875
- w_down: float32 [3072, 768], P(('dp', 'blk')), may hold values from -0.109375 to 0.109375
- vectors: float32 [12, 768], P(None, ('dp', 'blk'))
- first_qkv: float32 [768, 2304], P(('dp', 'blk')), may hold values from -0.0024414062 to 0.0024414062
- first_out: float32 [768, 768], P(('dp', 'blk')), may hold values from -0.0024414062 to 0.0024414062
- first_up: float32 [768, 3072], P(('dp', 'blk')), may hold values from -0.0024414062 to 0.0024414062
- first_down: float32 [3072, 768], P(('dp', 'blk')), may hold values from -0.0024414062 to 0.0024414062
- first_vectors: float32 [12, 768], P(None, ('dp', 'blk')), may hold values from -0.0034179688 to 0.0034179688
- second_qkv: float32 [768, 2304], P(('dp', 'blk')), may hold values from 1.4128508e-07 to 5.6514034e-07
- second_out: float32 [768, 768], P(('dp', 'blk')), may hold values from 1.4128508e-07 to 5.6514034e-07
- second_up: float32 [768, 3072], P(('dp', 'blk')), may hold values from 1.4128508e-07 to 5.6514034e-07
- second_down: float32 [3072, 768], P(('dp', 'blk')), may hold values from 1.4128508e-07 to 5.6514034e-07
- second_vectors: float32 [12, 768], P(None, ('dp', 'blk')), may hold values from 2.8257017e-07 to 1.1302807e-06
Outputs:
- output: bfloat16 [32768, 768], P(('dp', 'blk'))
- input_grad: float32 [32768, 768], P(('dp', 'blk'))
- grad_norm: float32 [], replicated
- new_qkv: float32 [768, 2304], P(('dp', 'blk'))
- new_out: float32 [768, 768], P(('dp', 'blk'))
- new_up: float32 [768, 3072], P(('dp', 'blk'))
- new_down: float32 [3072, 768], P(('dp', 'blk'))
- new_vectors: float32 [12, 768], P(None, ('dp', 'blk'))
- new_first_qkv: float32 [768, 2304], P(('dp', 'blk'))
- new_first_out: float32 [768, 768], P(('dp', 'blk'))
- new_first_up: float32 [768, 3072], P(('dp', 'blk'))
- new_first_down: float32 [3072, 768], P(('dp', 'blk'))
- new_first_vectors: float32 [12, 768], P(None, ('dp', 'blk'))
- new_second_qkv: float32 [768, 2304], P(('dp', 'blk'))
- new_second_out: float32 [768, 768], P(('dp', 'blk'))
- new_second_up: float32 [768, 3072], P(('dp', 'blk'))
- new_second_down: float32 [3072, 768], P(('dp', 'blk'))
- new_second_vectors: float32 [12, 768], P(None, ('dp', 'blk'))
- copy_qkv: bfloat16 [768, 2304], P(('dp', 'blk'))
- copy_out: bfloat16 [768, 768], P(('dp', 'blk'))
- copy_up: bfloat16 [768, 3072], P(('dp', 'blk'))
- copy_down: bfloat16 [3072, 768], P(('dp', 'blk'))
- copy_vectors: bfloat16 [12, 768], P(None, ('dp', 'blk'))
The draws below stay inside these ranges and needn't reach their ends.
Inputs may be any that keep to these rules, and one draw needn't show every extreme that they name: `short_lengths`: each row holds the lengths of the 9 short clips packed in order into one device's 896 short rows; it sums to 896 and its largest entry is 128. `long_lengths`: the long clip of each index of dp spans its 4 devices along blk in order; some index has 512.
All inputs are finite; a program needn't handle non-finite values.
Results may differ from the reference program's by a relative error of at most 0.012.
The reference program's roundings to bfloat16 on the way count: a program that leaves them out, or rounds other values in their place, can miss the bound.
Values may be sent and summed in bfloat16 or wider, within the bound.
A program may use at most 256 MiB of HBM per device.

```python
import math
import jax
import jax.numpy as jnp
import numpy as np
from jax import lax

D = 768
FF = 3072
H = 12
HD = 64
SHORT_DEV = 896
LONG_DEV = 128
SHORT_MOST = 128
STEP = 10
SEGS = 9
TOKENS = 32768
N_DP = 8
N_BLK = 4


def draw_vectors(key, part):
    key = jax.random.fold_in(key, 11)
    key_gain, key_shift = jax.random.split(key)
    column = jnp.arange(D, dtype=jnp.float32)
    shard_step = (jnp.arange(D) // (D // (N_DP * N_BLK)) % N_BLK).astype(jnp.float32) / max(N_BLK - 1, 1)
    rise = (0.6 + 0.6 * column / D) * (1.0 + shard_step)
    rough = jnp.exp(0.2 * jax.random.truncated_normal(key_gain, -2.0, 2.0, (2, D), jnp.float32))
    shifts = 0.4 * jax.random.truncated_normal(key_shift, -3.0, 3.0, (10, D), jnp.float32)
    gains = rise[None, :] * rough
    return jnp.concatenate([gains[0:1], shifts[0:1], gains[1:2], shifts[1:10]], 0)


def draw_long_lengths(key, part):
    key = jax.random.fold_in(key, 23)
    key_len, key_top, key_low = jax.random.split(key, 3)
    lengths = jax.random.randint(key_len, (N_DP,), 3 * LONG_DEV + 1, 4 * LONG_DEV + 1, jnp.int32)
    top_group = jax.random.randint(key_top, (), 0, N_DP, jnp.int32)
    low_group = (top_group + jax.random.randint(key_low, (), 1, N_DP, jnp.int32)) % N_DP
    return lengths.at[top_group].set(4 * LONG_DEV).at[low_group].set(3 * LONG_DEV + 1)


def levels(key, shape, cuts, least, largest):
    factor_of, own = 1.0, jax.random.fold_in(key, 6)
    for dim, shards_of in cuts:
        draws = jnp.exp(jax.random.uniform(jax.random.fold_in(own, dim), (shards_of,), jnp.float32, least / len(cuts), largest / len(cuts)))
        factor_of = factor_of * jnp.repeat(draws, shape[dim] // shards_of).reshape([-1 if axis == dim else 1 for axis in range(len(shape))])
    return factor_of


def length_profile(number_of, total, limit, lean):
    loads = [(1 << 20) // math.isqrt(rank ** lean) + 1 for rank in range(2, number_of + 1)]
    rest, given = total - limit - (number_of - 1), [1] * (number_of - 1)
    while rest > 0:
        movable = [i for i in range(number_of - 1) if given[i] < limit]
        mass, left = sum([loads[i] for i in movable]), rest
        for i in movable:
            addition = min(limit - given[i], max(1, left * loads[i] // mass), rest)
            given[i] = given[i] + addition
            rest = rest - addition
    return np.array([limit] + given)


def ragged_sizes(rng, count, total, most, skew):
    if count == 2:
        one = jax.random.randint(rng, (), max(1, total - most), min(most, total - 1) + 1)
        return jnp.stack([one, total - one])
    sizes = jnp.asarray(length_profile(count, total, most, skew), jnp.int32)
    pairs = (count - 1) // 2
    source_of, taker = sizes[1:1 + 2 * pairs:2], sizes[2:2 + 2 * pairs:2]
    room = jnp.minimum(source_of - 1, most - taker)
    passed = jax.random.randint(jax.random.fold_in(rng, 1), (pairs,), 0, 1 << 20) % (room + 1)
    sizes = sizes.at[1:1 + 2 * pairs:2].set(source_of - passed).at[2:2 + 2 * pairs:2].set(taker + passed)
    return sizes[jax.random.permutation(jax.random.fold_in(rng, 2), count)]


def noise(rng, dims, width, reach, pieces=(), kind=jnp.bfloat16):
    level = levels(rng, dims, pieces, -0.22, 0.18) if pieces else 1.0
    values = jax.random.normal(rng, dims, jnp.float32) * width * level
    return jnp.minimum(jnp.maximum(values, -reach), reach).astype(kind)


def setup_inputs(seed: int = 0) -> dict:
    streams_of = jax.random.split(jax.random.key(seed), 20)
    return {
        "patches": noise(streams_of[0], (TOKENS, D), 1.0, 6.0, ((0, 32),)),
        "cotangent": noise(streams_of[1], (TOKENS, D), 1.0, 6.0, ((0, 32),)),
        "short_lengths": jax.vmap(lambda own: ragged_sizes(own, SEGS, SHORT_DEV, SHORT_MOST, 1))(jax.random.split(streams_of[2], (N_DP * N_BLK))).reshape((N_DP * N_BLK, SEGS)).astype(jnp.int32),
        "long_lengths": draw_long_lengths(jax.random.fold_in(streams_of[19], 71), 0),
        "w_qkv": noise(streams_of[4], (D, 3 * D), D ** -0.5, 0.21875, ((0, 32),), jnp.float32),
        "w_out": noise(streams_of[5], (D, D), (D // 8) ** -0.5, 0.625, ((0, 32),), jnp.float32),
        "w_up": noise(streams_of[6], (D, FF), D ** -0.5, 0.21875, ((0, 32),), jnp.float32),
        "w_down": noise(streams_of[7], (FF, D), FF ** -0.5, 0.109375, ((0, 32),), jnp.float32),
        "vectors": draw_vectors(jax.random.fold_in(streams_of[19], 71), 0),
        "first_qkv": noise(streams_of[9], (D, 3 * D), ((4 * D * D + 2 * D * FF) ** -0.5), 0.0024414062, ((0, 32),), jnp.float32),
        "first_out": noise(streams_of[10], (D, D), ((4 * D * D + 2 * D * FF) ** -0.5), 0.0024414062, ((0, 32),), jnp.float32),
        "first_up": noise(streams_of[11], (D, FF), ((4 * D * D + 2 * D * FF) ** -0.5), 0.0024414062, ((0, 32),), jnp.float32),
        "first_down": noise(streams_of[12], (FF, D), ((4 * D * D + 2 * D * FF) ** -0.5), 0.0024414062, ((0, 32),), jnp.float32),
        "first_vectors": noise(streams_of[13], (12, D), (1.5 * (4 * D * D + 2 * D * FF) ** -0.5), 0.0034179688, ((1, 32),), jnp.float32),
        "second_qkv": jnp.clip(jnp.exp(math.log(5.651403398587718e-07) - 1.3862944 * jax.random.uniform(streams_of[14], (D, 3 * D), jnp.float32) ** levels(streams_of[14], (D, 3 * D), ((0, 32),), -0.2, 0.2)), 1.4128508496469294e-07, 5.651403398587718e-07),
        "second_out": jnp.clip(jnp.exp(math.log(5.651403398587718e-07) - 1.3862944 * jax.random.uniform(streams_of[15], (D, D), jnp.float32) ** levels(streams_of[15], (D, D), ((0, 32),), -0.2, 0.2)), 1.4128508496469294e-07, 5.651403398587718e-07),
        "second_up": jnp.clip(jnp.exp(math.log(5.651403398587718e-07) - 1.3862944 * jax.random.uniform(streams_of[16], (D, FF), jnp.float32) ** levels(streams_of[16], (D, FF), ((0, 32),), -0.2, 0.2)), 1.4128508496469294e-07, 5.651403398587718e-07),
        "second_down": jnp.clip(jnp.exp(math.log(5.651403398587718e-07) - 1.3862944 * jax.random.uniform(streams_of[17], (FF, D), jnp.float32) ** levels(streams_of[17], (FF, D), ((0, 32),), -0.2, 0.2)), 1.4128508496469294e-07, 5.651403398587718e-07),
        "second_vectors": jnp.clip(jnp.exp(math.log(1.1302806797175435e-06) - 1.3862944 * jax.random.uniform(streams_of[18], (12, D), jnp.float32) ** levels(streams_of[18], (12, D), ((1, 32),), -0.2, 0.2)), 2.825701699293859e-07, 1.1302806797175435e-06),
    }


eps_norm = 1e-06
far_below = -1000000000.0
rate_matrix = 0.04
rate_vector = 0.5
beta_first = 0.5
beta_second = 0.5
eps_adam = 1e-08
decay_weight = 0.01

@jax.custom_vjp
def low(v):
    return lax.optimization_barrier(v.astype(jnp.bfloat16)).astype(jnp.float32)

@jax.custom_vjp
def low_back(v):
    return v

def low_keep(v):
    return (low(v), None)

def low_pass(kept, grad):
    return (grad,)

def back_keep(v):
    return (v, None)

def back_low(kept, grad):
    return (low(grad),)
low.defvjp(low_keep, low_pass)
low_back.defvjp(back_keep, back_low)

def highest(left_side, right_side):
    return jnp.dot(left_side, right_side, precision=lax.Precision.HIGHEST, preferred_element_type=jnp.float32)

def normalize(values, gain, shift):
    row_mean = lax.optimization_barrier(jnp.mean(values, -1, keepdims=True))
    centered = values - row_mean
    return centered * lax.rsqrt(lax.optimization_barrier(jnp.mean(centered * centered, -1, keepdims=True)) + eps_norm) * gain + shift

def attend(queries, key_rows, value_rows, allowed):
    raw_scores = jnp.einsum('qhd,khd->hqk', queries, key_rows, precision=lax.Precision.HIGHEST) * HD ** (-0.5)
    scores = jnp.where(allowed[None], low_back(raw_scores), far_below)
    attn_probs = low(jax.nn.softmax(scores, axis=-1))
    attn_out = jnp.einsum('hqk,khd->qhd', attn_probs, value_rows, precision=lax.Precision.HIGHEST)
    return attn_out.reshape(attn_out.shape[0], -1)

def forward(inputs, w_qkv, w_out, w_up, w_down, vectors, segment_ids, long_lengths):
    devices = N_DP * N_BLK
    per_device = SHORT_DEV + LONG_DEV
    params = low(vectors)
    gain_one, shift_one, gain_two, shift_two = (params[0], params[1], params[2], params[3])
    bias_qkv = jnp.concatenate([params[4], jnp.zeros_like(params[4]), params[5]])
    bias_out, bias_down = (params[6], params[7])
    bias_up = params[8:12].reshape(-1)
    hidden_one = low(normalize(inputs, gain_one, shift_one))
    projected = low(low_back(highest(hidden_one, low(w_qkv)) + bias_qkv))
    blocks = projected.reshape(devices, per_device, 3, H, HD)
    short_part = blocks[:, :SHORT_DEV]
    long_part = blocks[:, SHORT_DEV:].reshape(N_DP, N_BLK * LONG_DEV, 3, H, HD)

    def short_block(bundle):
        block_rows, segs = bundle
        allowed = segs[:, None] == segs[None, :]
        return attend(block_rows[:, 0], block_rows[:, 1], block_rows[:, 2], allowed)

    def long_block(bundle):
        block_rows, length = bundle
        key_ok = jnp.arange(N_BLK * LONG_DEV) < length
        allowed = jnp.broadcast_to(key_ok[None, :], (N_BLK * LONG_DEV, N_BLK * LONG_DEV))
        return attend(block_rows[:, 0], block_rows[:, 1], block_rows[:, 2], allowed)
    short_out = lax.map(jax.checkpoint(short_block), (short_part, segment_ids))
    long_out = lax.map(jax.checkpoint(long_block), (long_part, long_lengths))
    attended = jnp.concatenate([short_out, long_out.reshape(devices, LONG_DEV, D)], 1).reshape(-1, D)
    attended = low(low_back(attended))
    middle = inputs + low_back(highest(attended, low(w_out)) + bias_out)
    hidden_two = low(normalize(middle, gain_two, shift_two))
    pre_act = low_back(highest(hidden_two, low(w_up)) + bias_up)
    activated = low(jax.nn.gelu(pre_act))
    return middle + low_back(highest(activated, low(w_down)) + bias_down)

def adamw_step(weight, gradient, first_moment, second_moment, rate, decay):
    first_new = beta_first * first_moment + (1.0 - beta_first) * gradient
    second_new = beta_second * second_moment + (1.0 - beta_second) * gradient * gradient
    first_hat = first_new / (1.0 - beta_first ** STEP)
    second_hat = second_new / (1.0 - beta_second ** STEP)
    weight_new = weight - rate * (first_hat / (jnp.sqrt(second_hat) + eps_adam) + decay * weight)
    return (weight_new, first_new, second_new)

def reference(patches, cotangent, short_lengths, long_lengths, w_qkv, w_out, w_up, w_down, vectors, first_qkv, first_out, first_up, first_down, first_vectors, second_qkv, second_out, second_up, second_down, second_vectors):
    devices = N_DP * N_BLK
    seg_ends = jnp.cumsum(short_lengths, -1)
    positions = jnp.arange(SHORT_DEV, dtype=jnp.int32)
    segment_ids = lax.optimization_barrier(jnp.sum((positions[None, :, None] >= seg_ends[:, None, :]).astype(jnp.int32), -1))
    key_place = jnp.arange(N_BLK, dtype=jnp.int32)[:, None] * LONG_DEV + jnp.arange(LONG_DEV, dtype=jnp.int32)[None, :]
    long_keep = (key_place[None] < long_lengths[:, None, None]).astype(jnp.float32).reshape(devices, LONG_DEV)
    row_keep = jnp.concatenate([jnp.ones((devices, SHORT_DEV), jnp.float32), long_keep], 1).reshape(-1)
    inputs = patches.astype(jnp.float32)

    def whole_layer(values, qkv_weight, out_weight, up_weight, down_weight, vector_rows):
        return forward(values, qkv_weight, out_weight, up_weight, down_weight, vector_rows, segment_ids, long_lengths)
    result, pull_back = jax.vjp(whole_layer, inputs, w_qkv, w_out, w_up, w_down, vectors)
    all_grads = pull_back(cotangent.astype(jnp.float32) * row_keep[:, None])
    input_grad = all_grads[0]
    square_sum = sum((jnp.sum(gradient * gradient) for gradient in all_grads[1:]))
    grad_norm = jnp.sqrt(square_sum)
    clip_factor = 1.0 / jnp.maximum(grad_norm, 1.0)
    qkv_new = adamw_step(w_qkv, all_grads[1] * clip_factor, first_qkv, second_qkv, rate_matrix, decay_weight)
    out_new = adamw_step(w_out, all_grads[2] * clip_factor, first_out, second_out, rate_matrix, decay_weight)
    up_new = adamw_step(w_up, all_grads[3] * clip_factor, first_up, second_up, rate_matrix, decay_weight)
    down_new = adamw_step(w_down, all_grads[4] * clip_factor, first_down, second_down, rate_matrix, decay_weight)
    vec_new = adamw_step(vectors, all_grads[5] * clip_factor, first_vectors, second_vectors, rate_vector, 0.0)
    return (result.astype(jnp.bfloat16), input_grad, grad_norm, qkv_new[0], out_new[0], up_new[0], down_new[0], vec_new[0], qkv_new[1], out_new[1], up_new[1], down_new[1], vec_new[1], qkv_new[2], out_new[2], up_new[2], down_new[2], vec_new[2], qkv_new[0].astype(jnp.bfloat16), out_new[0].astype(jnp.bfloat16), up_new[0].astype(jnp.bfloat16), down_new[0].astype(jnp.bfloat16), vec_new[0].astype(jnp.bfloat16))
```

```python
import functools

import jax
import jax.numpy as jnp
from jax import lax
from jax.experimental import pallas as pl
from jax.experimental.pallas import tpu as pltpu
from jax.sharding import PartitionSpec as P

HD = 64
SHORT_DEV = 896
LONG_DEV = 128
STEP = 10
TILE = 128
BAND = 3 * TILE
PAIR = 2 * HD
ROWS = 256

eps_norm = 1e-06
far_below = -1000000000.0
rate_matrix = 0.04
rate_vector = 0.5
beta_first = 0.5
beta_second = 0.5
eps_adam = 1e-08
decay_weight = 0.01
score_scale = HD ** (-0.5)
gelu_root = 0.7978845608028654
gelu_cube = 0.044715
VMEM_MOST = 60 * 1024 * 1024
FUSED_VMEM = 63 * 1024 * 1024


def dot(left, right):
    return lax.dot_general(left, right, (((1,), (0,)), ((), ())), preferred_element_type=jnp.float32)


def dot_tr(left, right):
    return lax.dot_general(left, right, (((1,), (1,)), ((), ())), preferred_element_type=jnp.float32)


def dot_tl(left, right):
    return lax.dot_general(left, right, (((0,), (0,)), ((), ())), preferred_element_type=jnp.float32)


def standardize(values):
    centered = values - jnp.mean(values, -1, keepdims=True)
    inv_std = lax.rsqrt(jnp.mean(centered * centered, -1, keepdims=True) + eps_norm)
    return centered * inv_std, inv_std


def norm_back(upstream, standard, inv_std, gain):
    scaled = upstream * gain
    inner = (
        scaled
        - jnp.mean(scaled, -1, keepdims=True)
        - standard * jnp.mean(scaled * standard, -1, keepdims=True)
    )
    return inner * inv_std


def column_sum(values):
    return jnp.sum(values, 0, keepdims=True)


def rows_at(step):
    return pl.ds(pl.multiple_of(step * ROWS, ROWS), ROWS)


def qkv_phase(x_ref, vec_ref, w_ref, h1_ref, qkv_ref):
    width = x_ref.shape[1]

    @pl.loop(0, x_ref.shape[0] // ROWS)
    def _(step):
        here = rows_at(step)
        unit, _ = standardize(x_ref[here, :].astype(jnp.float32))
        hidden = (unit * vec_ref[0:1, :] + vec_ref[1:2, :]).astype(jnp.bfloat16)
        h1_ref[here, :] = hidden
        for part, bias in ((0, 4), (1, None), (2, 5)):
            columns = slice(part * width, (part + 1) * width)
            made = dot(hidden, w_ref[:, columns])
            if bias is not None:
                made = made + vec_ref[bias : bias + 1, :]
            qkv_ref[here, columns] = made.astype(jnp.bfloat16)


def stack_heads(values, scale):
    lane = lax.broadcasted_iota(jnp.int32, values.shape, 1)
    if scale is not None:
        values = values * jnp.asarray(scale, values.dtype)
    zero = jnp.zeros_like(values)
    return jnp.concatenate(
        [jnp.where(lane < HD, values, zero), jnp.where(lane < HD, zero, values)], 0
    )


def unstack_heads(values):
    return jnp.concatenate([values[:HD, :TILE], values[HD:, TILE:]], 0)


def softmax_of(scores, allowed):
    scores = jnp.where(allowed, scores, far_below)
    top = jnp.max(scores, 0, keepdims=True)
    exponent = jnp.exp(scores - top)
    total = jnp.sum(exponent, 0, keepdims=True)
    return (exponent * (1.0 / total)).astype(jnp.bfloat16), top + jnp.log(total)


def attend_forward(queries, keys, values_tr, allowed):
    probs, log_total = softmax_of(dot_tr(keys, stack_heads(queries, score_scale)), allowed)
    return unstack_heads(dot(values_tr, probs)).astype(jnp.bfloat16), log_total


def softmax_back(scores, allowed, log_total, grad_probs):
    probs = jnp.exp(jnp.where(allowed, scores, far_below) - log_total)
    delta = jnp.sum(probs * grad_probs, 0, keepdims=True)
    grad_scores = (probs * (grad_probs - delta)).astype(jnp.bfloat16)
    return probs.astype(jnp.bfloat16), grad_scores


def attend_back(queries, keys, keys_tr, values, allowed, log_total, upstream):
    stacked_q = stack_heads(queries, score_scale)
    stacked_up = stack_heads(upstream, None)
    probs, grad_scores = softmax_back(
        dot_tr(keys, stacked_q), allowed, log_total, dot_tr(values, stacked_up)
    )
    grad_keys = dot(grad_scores, stacked_q)
    grad_values = dot(probs, stacked_up)
    grad_queries = unstack_heads(dot(keys_tr, grad_scores)) * score_scale
    return grad_queries.astype(jnp.bfloat16).T, grad_keys, grad_values


def mark_segments(ends_ref, key_seg, query_seg):
    count = ends_ref.shape[1]
    for tile in range(SHORT_DEV // TILE):
        rows = lax.broadcasted_iota(jnp.int32, (TILE, TILE), 0) + tile * TILE
        lanes = lax.broadcasted_iota(jnp.int32, (1, TILE), 1) + tile * TILE
        by_row = jnp.zeros((TILE, TILE), jnp.float32)
        by_lane = jnp.zeros((1, TILE), jnp.float32)
        end = jnp.int32(0)
        for clip in range(count):
            end = end + ends_ref[0, clip]
            by_row = by_row + jnp.where(rows >= end, 1.0, 0.0)
            by_lane = by_lane + jnp.where(lanes >= end, 1.0, 0.0)
        key_seg[tile * TILE : (tile + 1) * TILE, :] = by_row
        query_seg[tile] = by_lane


def band_start(tile):
    most = SHORT_DEV - BAND
    return pl.multiple_of(jnp.clip((tile - 1) * TILE, 0, most), TILE)


def pair_lanes(pair, offset=0):
    return pl.ds(pl.multiple_of(offset + pair * PAIR, PAIR), PAIR)


def short_mask(tile, key_seg, query_seg):
    band = key_seg[pl.ds(band_start(tile), BAND), :]
    line = query_seg[tile]
    return jnp.concatenate([band, band], 1) == jnp.concatenate([line, line], 1)


def long_mask(length_ref, keys):
    place = lax.broadcasted_iota(jnp.int32, (keys, 2 * TILE), 0)
    return place < length_ref[0]


def attention_forward_phase(qkv_ref, far_ref, length_ref, key_seg, query_seg, out_ref, lse_ref):
    width = out_ref.shape[1]
    pairs = width // PAIR
    tiles = SHORT_DEV // TILE

    @pl.loop(0, tiles)
    def _(tile):
        rows = pl.ds(pl.multiple_of(tile * TILE, TILE), TILE)
        band = pl.ds(band_start(tile), BAND)
        allowed = short_mask(tile, key_seg, query_seg)
        for pair in range(pairs):
            made, lse = attend_forward(
                qkv_ref[rows, pair * PAIR : (pair + 1) * PAIR],
                qkv_ref[band, width + pair * PAIR : width + (pair + 1) * PAIR],
                qkv_ref[band, 2 * width + pair * PAIR : 2 * width + (pair + 1) * PAIR].T,
                allowed,
            )
            out_ref[rows, pair * PAIR : (pair + 1) * PAIR] = made.T
            lse_ref[tile, pair] = lse

    @pl.loop(0, pairs)
    def _(pair):
        allowed = long_mask(length_ref, far_ref.shape[0])
        made, lse = attend_forward(
            qkv_ref[SHORT_DEV:, pair_lanes(pair)],
            far_ref[:, pair_lanes(pair)],
            far_ref[:, pair_lanes(pair, width)].T,
            allowed,
        )
        out_ref[SHORT_DEV:, pair_lanes(pair)] = made.T
        lse_ref[tiles, pair] = lse


def attention_back_long(qkv_ref, far_ref, length_ref, lse_ref, up_ref, dqkv_ref, far_grad):
    width = up_ref.shape[1]
    tiles = SHORT_DEV // TILE

    @pl.loop(0, width // PAIR)
    def _(pair):
        allowed = long_mask(length_ref, far_ref.shape[0])
        dq, dk, dv = attend_back(
            qkv_ref[SHORT_DEV:, pair_lanes(pair)],
            far_ref[:, pair_lanes(pair)],
            far_ref[:, pair_lanes(pair)].T,
            far_ref[:, pair_lanes(pair, width)],
            allowed,
            lse_ref[tiles, pair],
            up_ref[SHORT_DEV:, pair_lanes(pair)],
        )
        dqkv_ref[SHORT_DEV:, pair_lanes(pair)] = dq
        far_grad[:, pair_lanes(pair)] = dk.astype(jnp.bfloat16)
        far_grad[:, pair_lanes(pair, width)] = dv.astype(jnp.bfloat16)


def attention_back_short(qkv_ref, key_seg, query_seg, lse_ref, up_ref, dqkv_ref, dk_acc, dv_acc):
    width = up_ref.shape[1]
    tiles = SHORT_DEV // TILE

    @pl.loop(0, width // (2 * PAIR))
    def _(group):
        dk_acc[...] = jnp.zeros_like(dk_acc)
        dv_acc[...] = jnp.zeros_like(dv_acc)

        @pl.loop(0, tiles)
        def _(tile):
            rows = pl.ds(pl.multiple_of(tile * TILE, TILE), TILE)
            band = pl.ds(band_start(tile), BAND)
            allowed = short_mask(tile, key_seg, query_seg)
            for half in range(2):
                pair = group * 2 + half
                dq, dk, dv = attend_back(
                    qkv_ref[rows, pair_lanes(pair)],
                    qkv_ref[band, pair_lanes(pair, width)],
                    qkv_ref[band, pair_lanes(pair, width)].T,
                    qkv_ref[band, pair_lanes(pair, 2 * width)],
                    allowed,
                    lse_ref[tile, pair],
                    up_ref[rows, pair_lanes(pair)],
                )
                dqkv_ref[rows, pair_lanes(pair)] = dq
                own = slice(half * PAIR, (half + 1) * PAIR)
                dk_acc[band, own] += dk
                dv_acc[band, own] += dv

        lanes = 2 * PAIR
        k_at = pl.ds(pl.multiple_of(width + group * lanes, lanes), lanes)
        v_at = pl.ds(pl.multiple_of(2 * width + group * lanes, lanes), lanes)
        dqkv_ref[:SHORT_DEV, k_at] = dk_acc[...].astype(jnp.bfloat16)
        dqkv_ref[:SHORT_DEV, v_at] = dv_acc[...].astype(jnp.bfloat16)


def middle_phase(x_ref, vec_ref, w_ref, att_ref, middle_ref, h2_ref):
    @pl.loop(0, x_ref.shape[0] // ROWS)
    def _(step):
        here = rows_at(step)
        made = dot(att_ref[here, :], w_ref[...]) + vec_ref[6:7, :]
        middle = x_ref[here, :].astype(jnp.float32) + made
        middle_ref[here, :] = middle
        unit, _ = standardize(middle)
        h2_ref[here, :] = (unit * vec_ref[2:3, :] + vec_ref[3:4, :]).astype(jnp.bfloat16)


def gelu_both(values):
    square = values * values
    inner = values * (gelu_root + (gelu_root * gelu_cube) * square)
    bent = jnp.tanh(inner)
    half_up = 0.5 + 0.5 * bent
    slope = half_up + (0.5 * values) * (1.0 - bent * bent) * (
        gelu_root + (3.0 * gelu_root * gelu_cube) * square
    )
    return values * half_up, slope


def mlp_rows(h2_ref, dy_ref, up_ref, down_ref, bias, act_ref, du_ref, out_acc, dh2_acc, first):
    def body(step, total):
        here = rows_at(step)
        pre = dot(h2_ref[here, :], up_ref[...]) + bias
        grad_act = dot_tr(dy_ref[here, :], down_ref[...])
        act, slope = gelu_both(pre)
        act_low = act.astype(jnp.bfloat16)
        du_low = (grad_act * slope).astype(jnp.bfloat16)
        act_ref[here, :] = act_low
        du_ref[here, :] = du_low
        made = dot(act_low, down_ref[...])
        grad_hidden = dot_tr(du_low, up_ref[...])
        if first is True:
            out_acc[here, :] = made
            dh2_acc[here, :] = grad_hidden
        else:
            out_acc[here, :] += made
            dh2_acc[here, :] += grad_hidden
        return total + column_sum(du_low.astype(jnp.float32))

    width = up_ref.shape[1]
    return lax.fori_loop(0, h2_ref.shape[0] // ROWS, body, jnp.zeros((1, width), jnp.float32))


def middle_back_phase(
    dy_ref, middle_ref, dh2_ref, vec_ref, w_ref, dmiddle_ref, da_ref, datt_ref, gvec_ref
):
    def body(step, totals):
        here = rows_at(step)
        dy_low = dy_ref[here, :].astype(jnp.float32)
        dh2 = dh2_ref[here, :]
        unit, inv_std = standardize(middle_ref[here, :])
        dmiddle = dy_low + norm_back(dh2, unit, inv_std, vec_ref[2:3, :])
        dmiddle_ref[here, :] = dmiddle
        da = dmiddle.astype(jnp.bfloat16)
        da_ref[here, :] = da
        datt_ref[here, :] = dot_tr(da, w_ref[...]).astype(jnp.bfloat16)
        return (
            totals[0] + column_sum(dh2 * unit),
            totals[1] + column_sum(dh2),
            totals[2] + column_sum(da.astype(jnp.float32)),
            totals[3] + column_sum(dy_low),
        )

    zero = jnp.zeros((1, dy_ref.shape[1]), jnp.float32)
    totals = lax.fori_loop(0, dy_ref.shape[0] // ROWS, body, (zero,) * 4)
    for place in range(4):
        gvec_ref[place : place + 1, :] = totals[place]


def input_back_phase(x_ref, dqkv_ref, vec_ref, w_ref, dmiddle_ref, grad_ref, gvec_ref):
    width = x_ref.shape[1]

    def body(step, totals):
        here = rows_at(step)
        dh1 = dot_tr(dqkv_ref[here, :], w_ref[...])
        unit, inv_std = standardize(x_ref[here, :].astype(jnp.float32))
        grad_ref[here, :] = dmiddle_ref[here, :] + norm_back(dh1, unit, inv_std, vec_ref[0:1, :])
        return (
            totals[0] + column_sum(dh1 * unit),
            totals[1] + column_sum(dh1),
            totals[2] + column_sum(dqkv_ref[here, :width].astype(jnp.float32)),
            totals[3] + column_sum(dqkv_ref[here, 2 * width :].astype(jnp.float32)),
        )

    zero = jnp.zeros((1, width), jnp.float32)
    totals = lax.fori_loop(0, x_ref.shape[0] // ROWS, body, (zero,) * 4)
    for place in range(4):
        gvec_ref[place : place + 1, :] = totals[place]


def call(body, outs, scratch=(), smem=()):
    def run(*arrays):
        specs = [
            pl.BlockSpec(memory_space=pltpu.SMEM if place in smem else pltpu.VMEM)
            for place in range(len(arrays))
        ]
        return pl.pallas_call(
            body,
            out_shape=[jax.ShapeDtypeStruct(shape, kind) for shape, kind in outs],
            in_specs=specs,
            out_specs=[pl.BlockSpec(memory_space=pltpu.VMEM)] * len(outs),
            scratch_shapes=list(scratch),
            compiler_params=pltpu.CompilerParams(vmem_limit_bytes=VMEM_MOST),
        )(*arrays)

    return run


def forward_kernel(
    ends_ref, length_ref, x_ref, vec_ref, qkv_ref, far_ref, w_ref,
    att_ref, lse_ref, middle_ref, h2_ref, key_seg, query_seg,
):
    mark_segments(ends_ref, key_seg, query_seg)
    attention_forward_phase(qkv_ref, far_ref, length_ref, key_seg, query_seg, att_ref, lse_ref)
    middle_phase(x_ref, vec_ref, w_ref, att_ref, middle_ref, h2_ref)


def mlp_kernel(
    h2_ref, dy_ref, middle_ref, up_ref, down_ref, bias_ref, last_ref,
    out_ref, dh2_ref, gup_ref, gdown_ref, gbu_ref, act_ref, du_ref, out_acc,
):
    block = pl.program_id(0)

    @pl.when(block == 0)
    def _():
        out_acc[...] = jnp.zeros_like(out_acc)
        dh2_ref[...] = jnp.zeros_like(dh2_ref)

    gbu_ref[0] = mlp_rows(
        h2_ref, dy_ref, up_ref, down_ref, bias_ref[0], act_ref, du_ref, out_acc, dh2_ref, None
    )
    gup_ref[...] = dot_tl(h2_ref[...], du_ref[...])
    gdown_ref[...] = dot_tl(act_ref[...], dy_ref[...])

    @pl.when(block == pl.num_programs(0) - 1)
    def _():
        out_ref[...] = (middle_ref[...] + (out_acc[...] + last_ref[...])).astype(jnp.bfloat16)


def run_mlp(h2, dy, middle, w_up, w_down, bias_up, bias_down):
    rows, width = h2.shape
    units = w_up.shape[1]
    blocks = units // width
    whole = lambda shape: pl.BlockSpec(shape, lambda b: (0, 0))
    return pl.pallas_call(
        mlp_kernel,
        grid=(blocks,),
        out_shape=[
            jax.ShapeDtypeStruct((rows, width), jnp.bfloat16),
            jax.ShapeDtypeStruct((rows, width), jnp.float32),
            jax.ShapeDtypeStruct((width, units), jnp.float32),
            jax.ShapeDtypeStruct((units, width), jnp.float32),
            jax.ShapeDtypeStruct((blocks, 1, width), jnp.float32),
        ],
        in_specs=[
            whole((rows, width)),
            whole((rows, width)),
            whole((rows, width)),
            pl.BlockSpec((width, width), lambda b: (0, b)),
            pl.BlockSpec((width, width), lambda b: (b, 0)),
            pl.BlockSpec((1, 1, width), lambda b: (b, 0, 0)),
            whole((1, width)),
        ],
        out_specs=[
            whole((rows, width)),
            whole((rows, width)),
            pl.BlockSpec((width, width), lambda b: (0, b)),
            pl.BlockSpec((width, width), lambda b: (b, 0)),
            pl.BlockSpec((1, 1, width), lambda b: (b, 0, 0)),
        ],
        scratch_shapes=[
            pltpu.VMEM((rows, width), jnp.bfloat16),
            pltpu.VMEM((rows, width), jnp.bfloat16),
            pltpu.VMEM((rows, width), jnp.float32),
        ],
        compiler_params=pltpu.CompilerParams(vmem_limit_bytes=VMEM_MOST),
    )(h2, dy, middle, w_up, w_down, bias_up, bias_down)


def middle_back_kernel(
    dy_ref, middle_ref, dh2_ref, vec_ref, w_ref, att_ref,
    dmiddle_ref, datt_ref, gvec_ref, gout_ref, da_ref,
):
    middle_back_phase(
        dy_ref, middle_ref, dh2_ref, vec_ref, w_ref, dmiddle_ref, da_ref, datt_ref, gvec_ref
    )
    gout_ref[...] = dot_tl(att_ref[...], da_ref[...])


def attention_back_kernel(
    ends_ref, length_ref, qkv_ref, far_ref, lse_ref, datt_ref,
    dqkv_ref, far_grad, key_seg, query_seg, dk_acc, dv_acc,
):
    mark_segments(ends_ref, key_seg, query_seg)
    attention_back_long(qkv_ref, far_ref, length_ref, lse_ref, datt_ref, dqkv_ref, far_grad)
    width = datt_ref.shape[1]
    dqkv_ref[SHORT_DEV:, width:] = jnp.zeros((LONG_DEV, 2 * width), jnp.bfloat16)
    attention_back_short(
        qkv_ref, key_seg, query_seg, lse_ref, datt_ref, dqkv_ref, dk_acc, dv_acc
    )


def input_back_kernel(
    x_ref, h1_ref, dqkv_ref, near_ref, vec_ref, w_ref, dmiddle_ref,
    grad_ref, gqkv_ref, gvec_ref, mixed_ref,
):
    width = x_ref.shape[1]
    mixed_ref[...] = dqkv_ref[...]
    mixed_ref[SHORT_DEV:, width:] = near_ref[...]
    input_back_phase(x_ref, mixed_ref, vec_ref, w_ref, dmiddle_ref, grad_ref, gvec_ref)
    for part in range(3):
        columns = slice(part * width, (part + 1) * width)
        gqkv_ref[:, columns] = dot_tl(h1_ref[...], mixed_ref[:, columns])


def when(condition, body):
    if isinstance(condition, bool):
        if condition:
            body()
    else:
        pl.when(condition)(body)


def both(left, right):
    if isinstance(left, bool) and isinstance(right, bool):
        return left and right
    return jnp.logical_and(left, right)


class Places:
    def __init__(self, depth):
        self.depth = depth
        dp, blk = lax.axis_index("dp"), lax.axis_index("blk")
        self.dp, self.blk = dp, blk
        z, x, y, c = dp // 2, lax.rem(dp, 2), blk // 2, lax.rem(blk, 2)
        self.z, self.x, self.y, self.c = z, x, y, c
        flip = lambda value, by: lax.rem(value + by, 2)
        self.core = (dp, y * 2 + 1 - c)
        self.x_peer = (z * 2 + 1 - x, blk)
        self.y_peer = (dp, (1 - y) * 2 + c)
        self.first = (z * 2 + flip(x, 1 - c), flip(y, c) * 2 + c)
        self.second = (z * 2 + flip(x, c), flip(y, 1 - c) * 2 + c)
        self.corner = x * 4 + blk
        self.s, self.f = jnp.where(c == 0, y, x), jnp.where(c == 0, x, y)
        self.own = self.s * 2 + self.f
        self.at_first = self.s * 2 + 1 - self.f
        self.near_two = pl.ds(2 * self.s, 2)
        self.far_two = pl.ds(2 - 2 * self.s, 2)
        self.core_near_two = pl.ds(2 * self.f, 2)
        self.core_far_two = pl.ds(2 - 2 * self.f, 2)

    def z_peer(self, step):
        return (lax.rem(self.z + step, self.depth) * 2 + self.x, self.blk)

    def z_from(self, step):
        return lax.rem(self.z - step + self.depth, self.depth)

    def z_to(self, step):
        return lax.rem(self.z + step, self.depth)

    def plane_from(self, step):
        return lax.rem(self.corner - step + 8, 8)

    def plane_peer(self, step):
        corner = lax.rem(self.corner + step, 8)
        return (self.z * 2 + corner // 4, lax.rem(corner, 4))


def remote(source, target, sends, recvs, device):
    return pltpu.make_async_remote_copy(
        src_ref=source,
        dst_ref=target,
        send_sem=sends,
        recv_sem=recvs,
        device_id=device,
        device_id_type=pl.DeviceIdType.MESH,
    )


class Gather:
    def __init__(self, at, pieces, sends, recvs, plane=None):
        self.at, self.pieces, self.sends, self.recvs, self.plane = at, pieces, sends, recvs, plane
        self.near = at.depth - 1

    def along_z(self, block, step, whole, incoming):
        at = self.at
        source = at.z_from(step) if incoming else at.z
        region = self.pieces(block, None if whole else source, at.own, True)
        index = step - 1
        return remote(
            region, region, self.sends.at[block, index], self.recvs.at[block, index],
            at.z_peer(step),
        )

    def copy(self, block, kind, incoming=False):
        at = self.at
        device = (at.first, at.second, at.core, at.core)[kind]
        going = (at.own, at.near_two, at.near_two, at.far_two)
        coming = (at.at_first, at.far_two, at.core_near_two, at.core_far_two)
        place = (coming if incoming else going)[kind]
        region = self.pieces(block, None, place, not (incoming and kind >= 2))
        index = self.near + kind
        return remote(
            region, region, self.sends.at[block, index], self.recvs.at[block, index], device
        )

    def start(self, block, *kinds):
        for kind in kinds:
            self.copy(block, kind).start()

    def arrive(self, block, *kinds):
        for kind in kinds:
            self.copy(block, kind, True).wait_recv()

    def split(self, block, every, one):
        if self.plane is None:
            every()
            return
        single, z = self.plane(block)
        if isinstance(single, bool):
            one(z) if single else every()
            return
        pl.when(single)(lambda: one(z))
        pl.when(jnp.logical_not(single))(every)

    def push(self, block):
        def every():
            for step in range(1, self.at.depth):
                self.along_z(block, step, False, False).start()

        def one(z):
            @pl.when(self.at.z == z)
            def _():
                for step in range(1, self.at.depth):
                    self.along_z(block, step, True, False).start()

        self.split(block, every, one)

    def stage_two(self, block):
        def every():
            for step in range(1, self.at.depth):
                self.along_z(block, step, False, True).wait_recv()

        def one(z):
            @pl.when(self.at.z != z)
            def _():
                away = lax.rem(self.at.z - z + self.at.depth, self.at.depth)
                self.along_z(block, away, True, True).wait_recv()

        self.split(block, every, one)
        self.start(block, 0)

    def stage_three(self, block):
        self.arrive(block, 0)
        self.start(block, 1, 2)

    def stage_four(self, block):
        self.arrive(block, 1)
        self.start(block, 3)

    def finish(self, block):
        self.arrive(block, 2, 3)

    def sent(self, block):
        def every():
            for step in range(1, self.at.depth):
                self.along_z(block, step, False, False).wait_send()

        def one(z):
            @pl.when(self.at.z == z)
            def _():
                for step in range(1, self.at.depth):
                    self.along_z(block, step, True, False).wait_send()

        self.split(block, every, one)
        for kind in range(4):
            self.copy(block, kind).wait_send()


class Exchange:
    def __init__(self, at, sent, got, got_z, sends, recvs, slot):
        self.at, self.sent, self.got, self.got_z = at, sent, got, got_z
        self.sends, self.recvs, self.slot = sends, recvs, slot
        self.stage, self.copies, self.value = 0, [], None

    def copy(self, source, target, index, device):
        return remote(
            source, target, self.sends.at[self.slot, index], self.recvs.at[self.slot, index], device
        )

    def begin(self, value):
        at, stage = self.at, self.stage
        self.value = value
        self.sent[stage] = value
        peers = (at.core, at.x_peer, at.y_peer)
        if stage < 3:
            copy = self.copy(self.sent.at[stage], self.got.at[stage], stage, peers[stage])
            self.copies = [(copy, copy)]
        else:
            self.got_z[at.z] = value
            self.copies = []
            for step in range(1, at.depth):
                ends = [self.got_z.at[at.z], self.got_z.at[at.z_from(step)]]
                self.copies.append(
                    tuple(self.copy(self.sent.at[3], end, 2 + step, at.z_peer(step)) for end in ends)
                )
        for going, _ in self.copies:
            going.start()

    def step(self):
        for going, coming in self.copies:
            going.wait_send()
            coming.wait_recv()
        if self.stage < 3:
            value = self.value + self.got[self.stage]
            self.stage += 1
            self.begin(value)
            return None
        value = self.got_z[0]
        for place in range(1, self.at.depth):
            value = value + self.got_z[place]
        return value


class ShortExchange:
    def __init__(self, at, sent, got_z, got_plane, sends, recvs):
        self.at, self.sent, self.got_z, self.got_plane = at, sent, got_z, got_plane
        self.sends, self.recvs = sends, recvs

    def start(self, stage, landing, mine, value, others):
        self.sent[stage] = value
        landing[mine] = value
        copies = []
        for device, slot, index in others:
            ends = [landing.at[mine], landing.at[slot]]
            copies.append(
                tuple(
                    remote(self.sent.at[stage], end, self.sends.at[index], self.recvs.at[index], device)
                    for end in ends
                )
            )
        for going, _ in copies:
            going.start()
        return copies

    def finish(self, landing, copies):
        for going, coming in copies:
            going.wait_send()
            coming.wait_recv()
        value = landing[0]
        for place in range(1, landing.shape[0]):
            value = value + landing[place]
        return value

    def along_z(self, value):
        at = self.at
        others = [(at.z_peer(step), at.z_from(step), step - 1) for step in range(1, at.depth)]
        return self.start(0, self.got_z, at.z, value, others)

    def in_plane(self, value):
        at = self.at
        others = [
            (at.plane_peer(step), at.plane_from(step), at.depth - 2 + step) for step in range(1, 8)
        ]
        return self.start(1, self.got_plane, at.corner, value, others)


def fused_kernel(
    depth, ends_ref, length_ref, wqkv_ref, wout_ref, wup_ref, wdown_ref, vectors_ref, x_hbm, cot_hbm,
    out_hbm, grad_hbm, rqkv_ref, rout_ref, rup_ref, rdown_ref, rvec_ref, norm_ref,
    w, vbuf, vpad, give_out, asm, asm_down, vec, qkv, att, middle, h2, act, du, out_acc, dh2, dy,
    far, far_got, lse, key_seg, query_seg, turned, h2_tr, flat_up, flat_down,
    got_a, got_b, got_z, got_zd, red, squares, gvec,
    v_sent, v_got, v_got_z, n_sent, n_got, n_got_z,
    swap_s, swap_r, ag_s, ag_r, vg_s, vg_r, kv_s, kv_r, fg_s, fg_r, rs_s, rs_r, ex_s, ex_r, no_s, no_r, local_s,
):
    bf16, f32 = jnp.bfloat16, jnp.float32
    at = Places(depth)
    rows, width = dy.shape
    spare = w.shape[0] - 2
    blocks = spare
    slab = w.shape[4]
    share = slab // 2
    half = width // 2
    lanes4 = 2 * PAIR
    groups = width // lanes4
    units = (blocks - groups - 1) // 2
    tiles = SHORT_DEV // TILE
    mine = pl.ds(pl.multiple_of(at.c * half, 128), half)
    other = pl.ds(pl.multiple_of((1 - at.c) * half, 128), half)
    my_rows = pl.ds(pl.multiple_of(at.c * share, 8), share)
    other_rows = pl.ds(pl.multiple_of((1 - at.c) * share, 8), share)
    tall = units * share
    my_tall = pl.ds(pl.multiple_of(at.c * tall, 8), tall)
    other_tall = pl.ds(pl.multiple_of((1 - at.c) * tall, 8), tall)
    wide = 2 * PAIR
    wide_at = lambda step: pl.ds(pl.multiple_of(step * wide, wide), wide)

    barrier = pltpu.get_barrier_semaphore()
    friends = [at.plane_peer(step) for step in range(1, 8)]
    friends += [at.z_peer(step) for step in range(1, depth)]
    for friend in friends:
        pl.semaphore_signal(barrier, inc=1, device_id=friend, device_id_type=pl.DeviceIdType.MESH)
    load_x = pltpu.make_async_copy(x_hbm, dy, local_s.at[0])
    load_x.start()

    def pair_part(part, pair):
        return pl.ds(pl.multiple_of(part * width + pair * PAIR, PAIR), PAIR)

    def own_slot(slot, side, columns):
        if slot < groups:
            parts = [lax.rem(place + side, 3) for place in range(3)]
            return [wqkv_ref[:, pair_part(part, 2 * slot + side)] for part in parts]
        if slot == groups:
            return [wout_ref[:, columns]]
        start = (slot - groups - 1) * width
        return [wup_ref[:, pl.ds(pl.multiple_of(start + side * half, 128), half)]]

    slots = groups + 1 + units
    for slot in range(slots):
        lane = 0
        for piece in own_slot(slot, 1 - at.c, other):
            give_out[slot, :, lane : lane + piece.shape[1]] = piece
            lane += piece.shape[1]
    vpad[...] = jnp.zeros_like(vpad)
    vpad[: vectors_ref.shape[0], : vectors_ref.shape[1]] = vectors_ref[...]
    vbuf[at.c, at.own, at.z] = vpad[...].astype(bf16)
    pl.semaphore_wait(barrier, len(friends))
    swaps = []
    for index, (low, high) in enumerate(((0, groups), (groups, slots))):
        swaps.append(
            remote(
                give_out.at[low:high], asm.at[low:high, my_rows, :],
                swap_s.at[index], swap_r.at[index], at.core,
            )
        )
    swaps.append(
        remote(wdown_ref.at[:, other], asm_down.at[my_tall, :], swap_s.at[2], swap_r.at[2], at.core)
    )
    for swap in swaps:
        swap.start()
    for slot in range(slots):
        lane = 0
        for piece in own_slot(slot, at.c, mine):
            asm[slot, my_rows, lane : lane + piece.shape[1]] = piece
            lane += piece.shape[1]
    asm_down[my_tall, :] = wdown_ref[:, mine]

    def weight_piece(block, z, place, own_half):
        side = at.c if own_half else 1 - at.c
        if z is None:
            return w.at[block, side, place]
        return w.at[block, side, place, z]

    def vector_piece(block, z, place, own_half):
        core = at.c if own_half else 1 - at.c
        if z is None:
            return vbuf.at[core, place]
        return vbuf.at[core, place, z]

    def plane(block):
        after = block - groups
        if isinstance(block, int):
            return after > 0 and after % 2 == 0, after // 2 - 1
        return jnp.logical_and(after > 0, lax.rem(after, 2) == 0), after // 2 - 1

    weights = Gather(at, weight_piece, ag_s, ag_r, plane)
    vectors = Gather(at, vector_piece, vg_s, vg_r)

    def push(block):
        def every():
            slot = jnp.where(block > groups, groups + 1 + (block - groups - 1) // 2, block)
            w[block, at.c, at.own, at.z] = asm[slot].astype(bf16)

        def one(z):
            @pl.when(at.z == z)
            def _():
                w[block, at.c, at.own] = asm_down[...].reshape(depth, slab, half).astype(bf16)

        weights.split(block, every, one)
        weights.push(block)

    def gather_even(turn):
        last, block = turn - 3, turn
        when(both(last >= 0, last < blocks), lambda: weights.stage_four(last))

        when(block < blocks, lambda: weights.stage_two(block))

    def gather_odd(turn):
        block = turn - 1
        when(both(block >= 0, block < blocks), lambda: weights.stage_three(block))

    vectors.push(0)
    swaps[0].wait_recv()
    for block in range(groups):
        push(block)
    mark_segments(ends_ref, key_seg, query_seg)
    swaps[1].wait_recv()
    swaps[2].wait_recv()
    vectors.stage_two(0)
    gather_even(0)
    for block in range(groups, 2 * groups):
        push(block)
    vectors.stage_three(0)
    gather_even(1)
    gather_odd(1)
    for block in range(2 * groups, blocks):
        push(block)
    vectors.stage_four(0)
    gather_even(2)
    gather_odd(2)
    vectors.finish(0)
    gather_even(3)

    per = vectors_ref.shape[1]
    lane_inverse = (1 << 16) // per + 1
    spread_row = lax.broadcasted_iota(jnp.int32, (128, width), 0)
    spread_col = lax.broadcasted_iota(jnp.int32, (128, width), 1)
    spread_place = spread_col - ((spread_col * lane_inverse) >> 16) * per
    spread = jnp.where(spread_row == spread_place, 1.0, 0.0).astype(bf16)
    whole = jnp.zeros((16, width), f32)
    row = lax.broadcasted_iota(jnp.int32, (8 * 16, width), 0)
    col = (lax.broadcasted_iota(jnp.int32, (8 * 16, width), 1) * lane_inverse) >> 16
    core, place = row >> 6, (row >> 4) & 3
    place = jnp.where(core == 0, ((place & 1) << 1) | (place >> 1), place)
    device = place * 2 + core
    for level in range(depth):
        values = dot(vbuf[:, :, level].reshape(8 * 16, 128), spread)
        values = jnp.where(col == device + level * 8, values, 0.0).reshape(8, 16, width)
        whole = whole + jnp.sum(values, 0)
    vec[...] = whole

    def first_norm(target, first_time):
        @pl.loop(0, rows // ROWS)
        def _(step):
            here = rows_at(step)
            value = dy[here, :].astype(f32)
            unit, _ = standardize(value)
            hidden = (unit * vec[0:1, :] + vec[1:2, :]).astype(bf16)
            if first_time:
                target[here, :] = hidden
                middle[here, :] = value
            else:
                target[:, here] = hidden.T

    load_x.wait()
    first_norm(act, True)
    load_dy = pltpu.make_async_copy(cot_hbm, dy, local_s.at[0])
    load_dy.start()

    third = 3 * PAIR

    def group_columns(group, offset, count):
        return pl.ds(pl.multiple_of(group * width + offset, 128), count)

    def lane_of(part, side):
        return side * third + (part - side) % 3 * PAIR

    def q_at(group, side):
        return group_columns(group, lane_of(0, side), PAIR)

    def k_at(group, side):
        return group_columns(group, lane_of(1, side), PAIR)

    def v_at(group, side):
        return group_columns(group, lane_of(2, side), PAIR)

    def kv_at(group, side):
        return group_columns(group, lane_of(1, side), 2 * PAIR)

    def far_columns(group, side):
        return pl.ds(pl.multiple_of((2 * group + side) * 2 * PAIR, 128), 2 * PAIR)

    y_blk, core_blk = (1 - at.y) * 2 + at.c, at.y * 2 + 1 - at.c
    both_blk = 3 - at.blk

    def keys_copy(group, role, incoming=False):
        columns = pl.ds(pl.multiple_of(group * 4 * PAIR, 128), 4 * PAIR)
        device = (at.y_peer, at.core, at.core)[role]
        if incoming:
            source = target = far.at[(y_blk, core_blk, both_blk)[role], :, columns]
        elif role == 2:
            source = target = far.at[y_blk, :, columns]
        else:
            source = qkv.at[SHORT_DEV:, group_columns(group, PAIR, 4 * PAIR)]
            target = far.at[at.blk, :, columns]
        return remote(source, target, kv_s.at[group, role], kv_r.at[group, role], device)

    def strips(natural):
        for side in range(2):
            for place in range(4):
                high, low = place // 2, place % 2
                chip = (low * 2 + high) if side == 0 else place
                for level in range(depth):
                    order = chip * depth + level if natural else level * 4 + chip
                    yield side, place, level, order * slab

    def flatten(target, block, natural=False):
        for side, place, level, start in strips(natural):
            target[start : start + slab, side * half : (side + 1) * half] = w[
                block, side, place, level
            ]

    @pl.loop(0, groups)
    def _(group):
        weights.finish(group)
        bias = []
        for side in range(2):
            lanes = pl.ds(pl.multiple_of((2 * group + side) * PAIR, PAIR), PAIR)
            three = [vec[4:5, lanes], jnp.zeros((1, PAIR), f32), vec[5:6, lanes]]
            bias += three[side:] + three[:side]
        flat_down[0:1, :] = jnp.concatenate(bias, 1).astype(bf16)
        flatten(flat_up, group)

        @pl.loop(0, width // wide)
        def _(step):
            made = dot(act[...], flat_up[:, wide_at(step)])
            made = made + flat_down[0:1, wide_at(step)].astype(f32)
            qkv[:, group_columns(group, step * wide, wide)] = made.astype(bf16)

        keys_copy(group, 0).start()
        keys_copy(group, 1).start()
        for side in range(2):
            far[at.blk, :, far_columns(group, side)] = qkv[SHORT_DEV:, kv_at(group, side)]
            turned[side * PAIR : (side + 1) * PAIR, :] = qkv[:SHORT_DEV, v_at(group, side)].T

        gather_odd(groups + 2 * group)

        def tile_rows(tile):
            return pl.ds(pl.multiple_of(tile * TILE, TILE), TILE)

        def slot_rows(slot):
            return slice(slot * BAND, (slot + 1) * BAND)

        def products(tile, side):
            made = unstack_heads(
                dot(
                    turned[side * PAIR : (side + 1) * PAIR, pl.ds(band_start(tile), BAND)],
                    flat_down[slot_rows(side), :wide],
                )
            )
            att[pair_lanes(group * 2 + side), tile_rows(tile)] = made.astype(bf16)

        def soften(tile, side):
            allowed = short_mask(tile, key_seg, query_seg)
            probs, log_total = softmax_of(out_acc[slot_rows(side), :wide], allowed)
            flat_down[slot_rows(side), :wide] = probs
            lse[tile, group * 2 + side] = log_total

        def compare(tile, side):
            queries = stack_heads(qkv[tile_rows(tile), q_at(group, side)], score_scale)
            keys = qkv[pl.ds(band_start(tile), BAND), k_at(group, side)]
            out_acc[slot_rows(side), :wide] = dot_tr(keys, queries)

        @pl.loop(0, tiles + 1)
        def _(turn):
            now, last = jnp.minimum(turn, tiles - 1), jnp.maximum(turn - 1, 0)
            products(last, 0)
            soften(last, 1)
            compare(now, 0)
            products(last, 1)
            soften(now, 0)
            compare(now, 1)
            pl.when(turn == 1)(lambda: gather_even(groups + 1 + 2 * group))

            @pl.when(turn == 3)
            def _():
                gather_odd(groups + 1 + 2 * group)
                keys_copy(group, 0, True).wait_recv()
                keys_copy(group, 2).start()

            pl.when(turn == 6)(lambda: gather_even(groups + 2 + 2 * group))

    def far_pair(pair, offset):
        return pl.ds(pl.multiple_of(pair * 2 * PAIR + offset, PAIR), PAIR)

    def far_block(pair, offset):
        return far[:, :, far_pair(pair, offset)].reshape(4 * LONG_DEV, PAIR)

    gather_odd(3 * groups)
    for group in range(groups):
        keys_copy(group, 1, True).wait_recv()
        keys_copy(group, 2, True).wait_recv()

    @pl.loop(0, groups)
    def _(group):
        allowed = long_mask(length_ref, 4 * LONG_DEV)
        for side in range(2):
            pair = 2 * group + side
            made, log_total = attend_forward(
                qkv[SHORT_DEV:, q_at(group, side)],
                far_block(pair, 0),
                far_block(pair, PAIR).T,
                allowed,
            )
            att[pair_lanes(pair), SHORT_DEV:] = made
            lse[tiles, pair] = log_total
        pl.when(group == 0)(lambda: gather_even(3 * groups + 1))
        pl.when(group == groups - 1)(lambda: gather_odd(3 * groups + 1))

    weights.finish(groups)
    for group in range(groups):
        for role in range(3):
            keys_copy(group, role).wait_send()

    load_dy.wait()
    place = lax.broadcasted_iota(jnp.int32, (LONG_DEV, width), 0) + at.blk * LONG_DEV
    keep = place < length_ref[0]
    dy[SHORT_DEV:, :] = jnp.where(keep, dy[SHORT_DEV:, :].astype(f32), 0.0).astype(bf16)

    act[...] = att[...].T
    flatten(flat_up, groups)
    gather_even(3 * groups + 2)

    @pl.loop(0, width // wide)
    def _(step):
        columns = wide_at(step)
        made = dot(act[...], flat_up[:, columns]) + vec[6:7, columns]
        middle[:, columns] = middle[:, columns] + made

    @pl.loop(0, rows // ROWS)
    def _(step):
        here = rows_at(step)
        unit, _ = standardize(middle[here, :])
        hidden = (unit * vec[2:3, :] + vec[3:4, :]).astype(bf16)
        h2[here, :] = hidden
        h2_tr[:, here] = hidden.T

    def piece(block, place):
        return w.at[block, at.c, place]

    turns = [*range(groups + 1, blocks), groups, *range(groups)]

    def landing(block, side):
        if isinstance(block, int) and block <= groups:
            return turns[turns.index(block) - 4], side
        order = block - groups - 1
        odd = jnp.logical_and(order < 4, lax.rem(order, 2) == 1)
        return (
            jnp.where(order < 4, spare + order // 2, block - 4),
            jnp.where(odd, 1 - side, side),
        )

    def to_core(block):
        place, side = landing(block, at.c)
        return remote(
            w.at[block, 1 - at.c], w.at[place, side], rs_s.at[block, 0], rs_r.at[block, 0], at.core
        )

    def going(block, index):
        sends, recvs = rs_s.at[block, index], rs_r.at[block, index]
        if index == 1:
            return remote(piece(block, at.far_two), got_a.at[block], sends, recvs, at.second)
        return remote(piece(block, at.at_first), got_b.at[block], sends, recvs, at.first)

    def along_z(block, step):
        index = 4 + step
        return remote(
            w.at[block, at.c, at.own, at.z_to(step)], got_z.at[block, step - 1],
            rs_s.at[block, index], rs_r.at[block, index], at.z_peer(step),
        )

    def to_plane(block, step):
        index = 4 + step
        return remote(
            piece(block, at.own), got_zd.at[step - 1],
            rs_s.at[block, index], rs_r.at[block, index], at.z_peer(step),
        )

    def swap_back(block, tall_one, incoming=False):
        sends, recvs = rs_s.at[block, 4], rs_r.at[block, 4]
        columns = other if incoming else mine
        if tall_one:
            return remote(
                asm_down.at[other_tall, :], red.at[pl.ds(blocks_low, tall), columns],
                sends, recvs, at.core,
            )
        return remote(
            asm.at[slot_of(block), other_rows, :], red.at[red_rows(block), columns],
            sends, recvs, at.core,
        )

    blocks_low = slots * share

    def slot_of(block):
        if isinstance(block, int):
            return block if block <= groups else groups + 1 + (block - groups - 1) // 2
        return jnp.where(block > groups, groups + 1 + (block - groups - 1) // 2, block)

    def red_rows(block):
        return pl.ds(pl.multiple_of(slot_of(block) * share, 8), share)

    def add_piece(block, place, got):
        w[block, at.c, place] = w[block, at.c, place] + got

    def scatter_one(block):
        to_core(block).wait_recv()
        where, side = landing(block, 1 - at.c)
        add_piece(block, at.far_two, w[where, side, at.far_two])
        going(block, 1).start()
        add_piece(block, at.near_two, w[where, side, at.near_two])

    def scatter_two(block):
        going(block, 1).wait_recv()
        add_piece(block, at.at_first, got_a[block, 1 - at.f])
        going(block, 3).start()
        add_piece(block, at.own, got_a[block, at.f])

    def scatter_three(block):
        going(block, 3).wait_recv()
        add_piece(block, at.own, got_b[block])

        def every():
            for step in range(1, depth):
                along_z(block, step).start()

        def one(z):
            @pl.when(at.z != z)
            def _():
                to_plane(block, lax.rem(z - at.z + depth, depth)).start()

        weights.split(block, every, one)

    def scatter_four(block):
        def every():
            total = w[block, at.c, at.own, at.z].astype(f32)
            for step in range(1, depth):
                along_z(block, step).wait_recv()
                total = total + got_z[block, step - 1].astype(f32)
            slot = slot_of(block)
            asm[slot] = total
            squares[...] += total * total
            swap_back(block, False).start()
            red[red_rows(block), mine] = asm[slot, my_rows, :]

        def one(z):
            @pl.when(at.z == z)
            def _():
                for step in range(1, depth):
                    to_plane(block, step).wait_recv()
                total = w[block, at.c, at.own].astype(f32)
                for step in range(1, depth):
                    total = total + got_zd[step - 1].astype(f32)
                asm_down[...] = total.reshape(2 * tall, half)
                squares[...] += jnp.sum(total * total, 0)
                swap_back(block, True).start()
                red[pl.ds(blocks_low, tall), mine] = asm_down[my_tall, :]

        weights.split(block, every, one)

    def scatter_end(block):
        def every():
            swap_back(block, False, True).wait_recv()
            swap_back(block, False).wait_send()
            for step in range(1, depth):
                along_z(block, step).wait_send()

        def one(z):
            @pl.when(at.z == z)
            def _():
                swap_back(block, True, True).wait_recv()
                swap_back(block, True).wait_send()

            @pl.when(at.z != z)
            def _():
                to_plane(block, lax.rem(z - at.z + depth, depth)).wait_send()

        weights.split(block, every, one)
        for index in (1, 3):
            going(block, index).wait_send()

    stages = (scatter_one, scatter_two, scatter_three, scatter_four)

    def scatter_pump(turn):
        for stage, first, pace in zip(stages, (4, 7, 11, 14), (2, 3, 3, 3)):
            if isinstance(turn, int):
                order = (turn - first) // pace
                if (turn - first) % pace == 0 and 0 <= order <= 2 * units:
                    stage(turns[order])
                continue
            late = turn - first
            due = jnp.logical_and(late >= 0, lax.rem(late, pace) == 0)
            pl.when(due)(functools.partial(stage, groups + 1 + lax.div(late, pace)))

    def give(block, gradient, natural=False):
        weights.sent(block)
        if isinstance(block, int) and block <= groups:
            to_core(turns[turns.index(block) - 2]).wait_send()
        else:
            pl.when(block > groups + 2)(lambda: to_core(block - 2).wait_send())
        low = gradient.astype(bf16)
        for side, place, level, start in strips(natural):
            w[block, side, place, level] = low[
                start : start + slab, side * half : (side + 1) * half
            ]
        to_core(block).start()

    squares[...] = jnp.zeros_like(squares)
    out_acc[...] = jnp.zeros_like(out_acc)
    dh2[...] = jnp.zeros_like(dh2)
    gvec[...] = jnp.zeros_like(gvec)

    @pl.loop(0, units)
    def _(unit):
        up, down = groups + 1 + 2 * unit, groups + 2 + 2 * unit
        weights.finish(up)
        weights.finish(down)
        flatten(flat_up, up)
        flatten(flat_down, down, True)

        @pl.loop(0, width // wide)
        def _(step):
            @pl.when(step == 0)
            def _():
                gather_odd(3 * groups + 2 + 2 * unit)
                scatter_pump(4 * unit)

            @pl.when(step == 2)
            def _():
                gather_even(3 * groups + 3 + 2 * unit)
                scatter_pump(4 * unit + 1)

            columns = wide_at(step)
            pre = dot(h2[...], flat_up[:, columns]) + vec[pl.ds(8 + unit, 1), columns]
            grad_act = dot_tr(dy[...], flat_down[columns, :])
            made, slope = gelu_both(pre)
            act[:, columns] = made.astype(bf16)
            du_low = (grad_act * slope).astype(bf16)
            du[:, columns] = du_low
            gvec[pl.ds(8 + unit, 1), columns] = column_sum(du_low.astype(f32))

        @pl.loop(0, width // wide)
        def _(step):
            @pl.when(step == 1)
            def _():
                gather_odd(3 * groups + 3 + 2 * unit)
                scatter_pump(4 * unit + 2)

            columns = wide_at(step)
            out_acc[:, columns] += dot(act[...], flat_down[:, columns])
            dh2[:, columns] += dot_tr(du[...], flat_up[columns, :])

        gather_even(3 * groups + 4 + 2 * unit)
        scatter_pump(4 * unit + 3)
        give(up, dot(h2_tr[...], du[...]))
        give(down, dot_tl(act[...], dy[...]), True)

    def body(step, totals):
        here = rows_at(step)
        for turn in range(rows // ROWS):
            pl.when(step == turn)(functools.partial(scatter_pump, 4 * units + turn))
        middle_here = middle[here, :]
        out = middle_here + (out_acc[here, :] + vec[7:8, :])
        h2[here, :] = out.astype(bf16)
        dy_here = dy[here, :].astype(f32)
        dh2_here = dh2[here, :]
        unit, inv_std = standardize(middle_here)
        dmiddle = dy_here + norm_back(dh2_here, unit, inv_std, vec[2:3, :])
        dh2[here, :] = dmiddle
        da = dmiddle.astype(bf16)
        act[here, :] = da
        return (
            totals[0] + column_sum(dh2_here * unit),
            totals[1] + column_sum(dh2_here),
            totals[2] + column_sum(da.astype(f32)),
            totals[3] + column_sum(dy_here),
        )

    zero = jnp.zeros((1, width), f32)
    sums = lax.fori_loop(0, rows // ROWS, body, (zero,) * 4)
    flatten(flat_up, groups)

    @pl.loop(0, width // wide)
    def _(step):
        columns = wide_at(step)
        du[:, columns] = dot_tr(act[...], flat_up[columns, :]).astype(bf16)

    for place, total in zip((2, 3, 6, 7), sums):
        gvec[place : place + 1, :] = total
    store_out = pltpu.make_async_copy(h2, out_hbm, local_s.at[0])
    store_out.start()
    load_again = pltpu.make_async_copy(x_hbm, dy, local_s.at[2])
    load_again.start()
    give(groups, dot(att[...], act[...]))
    load_again.wait()
    first_norm(h2_tr, False)

    after = 4 * units + rows // ROWS

    @pl.loop(0, groups)
    def _(group):
        allowed = long_mask(length_ref, 4 * LONG_DEV)
        for side in range(2):
            pair = 2 * group + side
            dq, dk, dv = attend_back(
                qkv[SHORT_DEV:, q_at(group, side)],
                far_block(pair, 0),
                far_block(pair, 0).T,
                far_block(pair, PAIR),
                allowed,
                lse[tiles, pair],
                du[SHORT_DEV:, pair_lanes(pair)],
            )
            qkv[SHORT_DEV:, q_at(group, side)] = dq
            far[:, :, far_pair(pair, 0)] = dk.astype(bf16).reshape(4, LONG_DEV, PAIR)
            far[:, :, far_pair(pair, PAIR)] = dv.astype(bf16).reshape(4, LONG_DEV, PAIR)
        for turn in range(groups):
            pl.when(group == turn)(functools.partial(scatter_pump, after + turn))

    flats = (flat_up, act.at[:width, :], att.at[:, :width])

    far_one = remote(far.at[core_blk], far_got.at[0], fg_s.at[0], fg_r.at[0], at.core)
    far_two = remote(far.at[both_blk], far_got.at[1], fg_s.at[1], fg_r.at[1], at.core)
    far_three = remote(far.at[y_blk], far_got.at[2], fg_s.at[2], fg_r.at[2], at.y_peer)
    far_two.start()
    far_one.start()
    store_out.wait()
    lse[tiles + 1] = jnp.full(lse.shape[1:], 1e30, f32)
    flat_down[...] = jnp.zeros_like(flat_down)

    @pl.loop(0, groups)
    def _(group):
        middle[:SHORT_DEV, 0 : 4 * PAIR] = jnp.zeros((SHORT_DEV, 4 * PAIR), f32)
        flat_down[:BAND, 0 : 2 * wide] = jnp.zeros((BAND, 2 * wide), bf16)
        before = group - 1

        def pump(place):
            for now in range(groups):
                turn = after + groups + 5 * now + place
                pl.when(group == now)(functools.partial(scatter_pump, turn))

            @pl.when(group > 0)
            def _():
                if place == 0:
                    pl.when(group > 1)(lambda: scatter_four(group - 2))
                if place == 1:
                    for block in range(groups - 1):
                        pl.when(before == block)(functools.partial(scatter_one, block))
                if place == 3:
                    scatter_two(before)
                if place == 4:
                    scatter_three(before)

        pump(0)
        for side in range(2):
            turned[side * PAIR : (side + 1) * PAIR, :] = qkv[:SHORT_DEV, k_at(group, side)].T

        def tile_rows(tile):
            return pl.ds(pl.multiple_of(tile * TILE, TILE), TILE)

        def slot_rows(slot):
            return slice(slot * BAND, (slot + 1) * BAND)

        def stacked(tile, side):
            here = tile_rows(tile)
            return (
                stack_heads(qkv[here, q_at(group, side)], score_scale),
                stack_heads(du[here, pair_lanes(group * 2 + side)], None),
            )

        def products(tile, side, target):
            queries, upstream = stacked(tile, side)
            band = pl.ds(band_start(tile), BAND)
            probs = flat_down[slot_rows(side), :wide]
            grad_scores = flat_down[slot_rows(side), wide : 2 * wide]
            start = side * 2 * PAIR
            middle[band, start : start + PAIR] += dot(grad_scores, queries)
            middle[band, start + PAIR : start + 2 * PAIR] += dot(probs, upstream)
            keys_tr = turned[side * PAIR : (side + 1) * PAIR, band]
            dq = unstack_heads(dot(keys_tr, grad_scores)) * score_scale
            h2[tile_rows(target), pair_lanes(group * 2 + side)] = dq.astype(bf16).T

        def soften(tile, side, source):
            allowed = short_mask(tile, key_seg, query_seg)
            probs, grad_scores = softmax_back(
                middle[slot_rows(side), 2 * wide : 3 * wide],
                allowed,
                lse[source, group * 2 + side],
                out_acc[slot_rows(side), :wide],
            )
            flat_down[slot_rows(side), :wide] = probs
            flat_down[slot_rows(side), wide : 2 * wide] = grad_scores

        def compare(tile, side):
            queries, upstream = stacked(tile, side)
            band = pl.ds(band_start(tile), BAND)
            middle[slot_rows(side), 2 * wide : 3 * wide] = dot_tr(
                qkv[band, k_at(group, side)], queries
            )
            out_acc[slot_rows(side), :wide] = dot_tr(qkv[band, v_at(group, side)], upstream)

        @pl.loop(0, tiles + 1)
        def _(turn):
            now, last = jnp.minimum(turn, tiles - 1), jnp.maximum(turn - 1, 0)
            target = jnp.where(turn == 0, tiles, last)
            products(last, 0, target)
            soften(last, 1, jnp.where(turn == 0, tiles + 1, last))
            compare(now, 0)
            products(last, 1, target)
            soften(now, 0, now)
            compare(now, 1)

            @pl.when(turn == 1)
            def _():
                pump(1)

                @pl.when(group == 0)
                def _():
                    far_two.wait_recv()
                    far[y_blk] = far[y_blk] + far_got[1]
                    far_three.start()

            pl.when(turn == 3)(lambda: pump(2))
            pl.when(turn == 6)(lambda: pump(3))

        for side in range(2):
            qkv[:SHORT_DEV, q_at(group, side)] = h2[:SHORT_DEV, pair_lanes(group * 2 + side)]

        @pl.when(group == 0)
        def _():
            far_one.wait_recv()
            far_three.wait_recv()

        for side in range(2):
            start = side * 2 * PAIR
            qkv[:SHORT_DEV, kv_at(group, side)] = middle[
                :SHORT_DEV, start : start + 2 * PAIR
            ].astype(bf16)
            near_at = far_columns(group, side)
            near = far[at.blk, :, near_at].astype(f32) + far_got[0, :, near_at].astype(f32)
            near = near + far_got[2, :, near_at].astype(f32)
            qkv[SHORT_DEV:, kv_at(group, side)] = near.astype(bf16)

        for block, target in enumerate(flats):
            pl.when(group == block)(functools.partial(flatten, target, block))
        gradient = dot(h2_tr[...], qkv[:, group_columns(group, 0, width)])
        for block in range(groups):
            pl.when(group == block)(functools.partial(give, block, gradient))

        pump(4)
        sums = column_sum(qkv[:, group_columns(group, 0, width)].astype(f32))
        for side in range(2):
            own = pl.ds(pl.multiple_of((2 * group + side) * PAIR, PAIR), PAIR)
            for part, line in ((0, 4), (2, 5)):
                lane = lane_of(part, side)
                gvec[line : line + 1, own] = sums[:, lane : lane + PAIR]

    def input_rows(step):
        here = pl.ds(step * (rows // 2), rows // 2)
        unit, inv_std = standardize(dy[here, :].astype(f32))
        dh1 = out_acc[here, :]
        middle[here, :] = dh2[here, :] + norm_back(dh1, unit, inv_std, vec[0:1, :])
        return column_sum(dh1 * unit), column_sum(dh1)

    latest = groups - 1
    scatter_one(latest)

    @pl.loop(0, width // wide)
    def _(step):
        columns = wide_at(step)
        made = jnp.zeros((rows, wide), f32)
        for group, flat in enumerate(flats):
            made = made + dot_tr(qkv[:, group * width : (group + 1) * width], flat[columns, :])
        out_acc[:, columns] = made

    gain_low, shift_low = input_rows(0)
    scatter_pump(after + 6 * groups)
    scatter_four(latest - 1)
    gain_high, shift_high = input_rows(1)
    store_grad = pltpu.make_async_copy(middle, grad_hbm, local_s.at[1])
    store_grad.start()
    gvec[0:1, :] = gain_low + gain_high
    gvec[1:2, :] = shift_low + shift_high
    exchange = Exchange(at, v_sent, v_got, v_got_z, ex_s, ex_r, 0)
    exchange.begin(gvec[...])
    scatter_two(latest)
    exchange.step()
    scatter_three(latest)
    exchange.step()
    exchange.step()
    scatter_four(latest)

    weight_square = jnp.sum(squares[...], keepdims=True)
    norms = ShortExchange(at, n_sent, n_got_z, n_got, no_s, no_r)
    norm_copies = norms.along_z(jnp.broadcast_to(weight_square, n_sent.shape[1:]))
    vector_sum = exchange.step()
    device = at.dp * 4 + at.blk
    turn_by = lax.rem(width - device * per, width)
    rvec_ref[...] = pltpu.roll(vector_sum, turn_by, 1)[:, :128]
    vector_square = jnp.sum(vector_sum * vector_sum, keepdims=True)
    norm_copies = norms.in_plane(norms.finish(n_got_z, norm_copies))

    @pl.loop(0, blocks)
    def _(block):
        @pl.when(block > groups)
        def _():
            scatter_end(block)

    for block in range(groups + 1):
        scatter_end(block)
    for block in turns[-2:]:
        to_core(block).wait_send()
    for group in range(groups):
        for side in range(2):
            for part in range(3):
                start = part * width + (2 * group + side) * PAIR
                lane = lane_of(part, side)
                rqkv_ref[:, start : start + PAIR] = red[
                    group * share : (group + 1) * share, lane : lane + PAIR
                ]
    rout_ref[...] = red[groups * share : (groups + 1) * share, :]
    for unit in range(units):
        start = (groups + 1 + unit) * share
        rup_ref[:, unit * width : (unit + 1) * width] = red[start : start + share, :]
    rdown_ref[...] = red[blocks_low : blocks_low + tall, :]
    far_one.wait_send()
    far_two.wait_send()
    far_three.wait_send()
    for swap in swaps:
        swap.wait_send()
    vectors.sent(0)
    norm_ref[...] = jnp.sqrt(norms.finish(n_got, norm_copies) + vector_square)
    store_grad.wait()


def run_fused(depth, patches, cotangent, ends, length, w_qkv, w_out, w_up, w_down, vectors):
    rows, width = patches.shape
    share = w_out.shape[0]
    tall = w_down.shape[0]
    bf16, f32 = jnp.bfloat16, jnp.float32
    slab = 2 * share
    lanes4 = 2 * PAIR
    groups = width // lanes4
    units = w_up.shape[1] // width
    slots = groups + 1 + units
    blocks = slots + units
    half = width // 2
    tiles = SHORT_DEV // TILE
    vmem = lambda shape, kind: pltpu.VMEM(shape, kind)
    dma = pltpu.SemaphoreType.DMA
    copies = depth + 3
    scratch = [
        vmem((blocks + 2, 2, 4, depth, slab, half), bf16),
        vmem((2, 4, depth, 16, 128), bf16),
        vmem((16, 128), f32),
        vmem((slots, share, half), f32),
        vmem((slots, slab, half), f32),
        vmem((2 * tall, half), f32),
        vmem((16, width), f32),
        vmem((rows, 3 * width), bf16),
        vmem((width, rows), bf16),
        vmem((rows, width), f32),
        vmem((rows, width), bf16),
        vmem((rows, width), bf16),
        vmem((rows, width), bf16),
        vmem((rows, width), f32),
        vmem((rows, width), f32),
        vmem((rows, width), bf16),
        vmem((4, LONG_DEV, 2 * width), bf16),
        vmem((3, LONG_DEV, 2 * width), bf16),
        vmem((tiles + 2, width // PAIR, 1, 2 * TILE), f32),
        vmem((SHORT_DEV, TILE), f32),
        vmem((tiles, 1, TILE), f32),
        vmem((lanes4, SHORT_DEV), bf16),
        vmem((width, rows), bf16),
        vmem((width, width), bf16),
        vmem((width, width), bf16),
        vmem((blocks, 2, depth, slab, half), bf16),
        vmem((blocks, depth, slab, half), bf16),
        vmem((blocks, depth - 1, slab, half), bf16),
        vmem((depth - 1, depth, slab, half), bf16),
        vmem((slots * share + tall, width), f32),
        vmem((slab, half), f32),
        vmem((16, width), f32),
        vmem((4, 16, width), f32),
        vmem((3, 16, width), f32),
        vmem((depth, 16, width), f32),
        vmem((2, 8, 128), f32),
        vmem((8, 8, 128), f32),
        vmem((depth, 8, 128), f32),
    ]
    scratch += [dma((3,))] * 2 + [dma((blocks, copies))] * 2 + [dma((1, copies))] * 2
    scratch += [dma((groups, 3))] * 2 + [dma((3,))] * 2 + [dma((blocks, 4 + depth))] * 2
    scratch += [dma((1, 3 + depth))] * 2 + [dma((depth + 6,))] * 2 + [dma((3,))]
    in_vmem = pl.BlockSpec(memory_space=pltpu.VMEM)
    in_smem = pl.BlockSpec(memory_space=pltpu.SMEM)
    anywhere = pl.BlockSpec(memory_space=pl.ANY)
    return pl.pallas_call(
        functools.partial(fused_kernel, depth),
        out_shape=[
            jax.ShapeDtypeStruct((rows, width), bf16),
            jax.ShapeDtypeStruct((rows, width), f32),
            jax.ShapeDtypeStruct(w_qkv.shape, f32),
            jax.ShapeDtypeStruct(w_out.shape, f32),
            jax.ShapeDtypeStruct(w_up.shape, f32),
            jax.ShapeDtypeStruct(w_down.shape, f32),
            jax.ShapeDtypeStruct((16, 128), f32),
            jax.ShapeDtypeStruct((8, 128), f32),
        ],
        in_specs=[in_smem] * 2 + [in_vmem] * 5 + [anywhere] * 2,
        out_specs=[anywhere] * 2 + [in_vmem] * 6,
        scratch_shapes=scratch,
        compiler_params=pltpu.CompilerParams(
            vmem_limit_bytes=FUSED_VMEM, collective_id=0, has_side_effects=True
        ),
    )(ends, length, w_qkv, w_out, w_up, w_down, vectors, patches, cotangent)


def adamw_kernel(*refs):
    out_in, grad_in, norm_ref, out_out, grad_out, total_ref = *refs[:3], *refs[23:26]
    sources = [refs[3 + 5 * kind : 8 + 5 * kind] for kind in range(4)]
    targets = [refs[26 + 5 * kind : 31 + 5 * kind] for kind in range(4)]
    through, sems = refs[46:48], refs[48]
    loads, stores = [], []
    for place, (source, target) in enumerate(((out_in, out_out), (grad_in, grad_out))):
        loads.append(pltpu.make_async_copy(source, through[place], sems.at[place]))
        stores.append(pltpu.make_async_copy(through[place], target, sems.at[2 + place]))
    for load in loads:
        load.start()
    total_ref[...] = norm_ref[0:1, 0:1]
    factor = 1.0 / jnp.maximum(norm_ref[0:1, 0:1], 1.0)
    for load, store in zip(loads, stores):
        load.wait()
        store.start()
    for place in range(5):
        weight, first, second, gradient = (source[place] for source in sources)
        rate, decay = (rate_vector, 0.0) if place == 4 else (rate_matrix, decay_weight)
        lines, columns = weight.shape
        new = adamw_step(
            weight[...], gradient[:lines, :columns] * factor, first[...], second[...], rate, decay
        )
        for target, value in zip(targets, (*new, new[0])):
            target[place][...] = value.astype(target[place].dtype)
    for store in stores:
        store.wait()


def run_adamw(result, input_grad, norm, weights, firsts, seconds, gradients):
    f32 = jnp.float32
    outs = [jax.ShapeDtypeStruct(part.shape, part.dtype) for part in (result, input_grad)]
    outs.append(jax.ShapeDtypeStruct((1, 1), f32))
    for kind in (f32, f32, f32, jnp.bfloat16):
        outs += [jax.ShapeDtypeStruct(part.shape, kind) for part in weights]
    in_vmem, anywhere = pl.BlockSpec(memory_space=pltpu.VMEM), pl.BlockSpec(memory_space=pl.ANY)
    found = pl.pallas_call(
        adamw_kernel,
        out_shape=outs,
        in_specs=[anywhere] * 2 + [in_vmem] * 21,
        out_specs=[anywhere] * 2 + [in_vmem] * 21,
        scratch_shapes=[
            pltpu.VMEM(result.shape, result.dtype),
            pltpu.VMEM(input_grad.shape, input_grad.dtype),
            pltpu.SemaphoreType.DMA((4,)),
        ],
        compiler_params=pltpu.CompilerParams(vmem_limit_bytes=VMEM_MOST),
    )(result, input_grad, norm, *weights, *firsts, *seconds, *gradients)
    return found[0], found[1], found[2].reshape(()), *found[3:]


def adamw_step(weight, gradient, first_moment, second_moment, rate, decay):
    first_new = beta_first * first_moment + (1.0 - beta_first) * gradient
    second_new = beta_second * second_moment + (1.0 - beta_second) * gradient * gradient
    first_hat = first_new / (1.0 - beta_first**STEP)
    second_hat = second_new / (1.0 - beta_second**STEP)
    weight_new = weight - rate * (first_hat / (jnp.sqrt(second_hat) + eps_adam) + decay * weight)
    return (weight_new, first_new, second_new)


def gather_parameters(weights, vectors):
    low = [w.astype(jnp.bfloat16) for w in weights] + [vectors.astype(jnp.bfloat16)]
    flat = jnp.concatenate([part.reshape(-1) for part in low])
    flat = jnp.pad(flat, (0, -flat.size % 4096)).reshape(-1, 128)
    whole = lax.all_gather(flat, ("dp", "blk"), axis=0, tiled=True)
    whole = whole.reshape(-1, flat.size)
    found, at = [], 0
    for part in low[:-1]:
        piece = whole[:, at : at + part.size]
        found.append(piece.reshape(-1, part.shape[1]))
        at += part.size
    piece = whole[:, at : at + vectors.size].reshape(-1, *vectors.shape)
    found.append(piece.transpose(1, 0, 2).reshape(vectors.shape[0], -1))
    return found


def layer_by_parts(
    patches, cotangent, short_lengths, long_lengths, w_qkv, w_out, w_up, w_down, vectors
):
    rows, width = patches.shape
    bf16, f32 = jnp.bfloat16, jnp.float32
    full_qkv, full_out, full_up, full_down, full_vec = gather_parameters(
        (w_qkv, w_out, w_up, w_down), vectors
    )
    params = full_vec.astype(f32)

    hidden_one, projected = call(
        qkv_phase, [((rows, width), bf16), ((rows, 3 * width), bf16)]
    )(patches, params, full_qkv)
    far = lax.all_gather(projected[SHORT_DEV:, width:], "blk", axis=0, tiled=True)
    tiles, pairs = SHORT_DEV // TILE, width // PAIR
    marks = [pltpu.VMEM((SHORT_DEV, TILE), f32), pltpu.VMEM((tiles, 1, TILE), f32)]
    attended, lse, middle, hidden_two = call(
        forward_kernel,
        [
            ((rows, width), bf16),
            ((tiles + 1, pairs, 1, 2 * TILE), f32),
            ((rows, width), f32),
            ((rows, width), bf16),
        ],
        scratch=marks,
        smem=(0, 1),
    )(short_lengths, long_lengths, patches, params, projected, far, full_out)

    long_place = lax.axis_index("blk") * LONG_DEV + jnp.arange(LONG_DEV, dtype=jnp.int32)
    keep = jnp.concatenate([jnp.ones((SHORT_DEV,), bool), long_place < long_lengths[0]])
    grad_low = jnp.where(keep[:, None], cotangent, jnp.zeros_like(cotangent))
    blocks = full_up.shape[1] // width
    result, grad_hidden_two, grad_up, grad_down, grad_bias_up = run_mlp(
        hidden_two, grad_low, middle, full_up, full_down,
        params[8 : 8 + blocks].reshape(blocks, 1, width), params[7:8],
    )
    scatter = functools.partial(
        lax.psum_scatter, axis_name=("dp", "blk"), scatter_dimension=0, tiled=True
    )
    red_up = scatter(grad_up)
    red_down = scatter(grad_down)

    grad_middle, grad_att, sums_two, grad_out = call(
        middle_back_kernel,
        [
            ((rows, width), f32),
            ((rows, width), bf16),
            ((4, width), f32),
            ((width, width), f32),
        ],
        scratch=[pltpu.VMEM((rows, width), bf16)],
    )(grad_low, middle, grad_hidden_two, params, full_out, attended)
    red_out = scatter(grad_out)

    mixed, far_grad = call(
        attention_back_kernel,
        [((rows, 3 * width), bf16), ((far.shape[0], 2 * width), bf16)],
        scratch=marks + [pltpu.VMEM((SHORT_DEV, 2 * PAIR), f32)] * 2,
        smem=(0, 1),
    )(short_lengths, long_lengths, projected, far, lse, grad_att)
    near = lax.psum_scatter(far_grad, "blk", scatter_dimension=0, tiled=True)
    input_grad, grad_qkv, sums_one = call(
        input_back_kernel,
        [((rows, width), f32), ((width, 3 * width), f32), ((4, width), f32)],
        scratch=[pltpu.VMEM((rows, 3 * width), bf16)],
    )(patches, hidden_one, mixed, near, params, full_qkv, grad_middle)
    red_qkv = scatter(grad_qkv)

    grad_vec = jnp.concatenate(
        [sums_one[0:2], sums_two[0:2], sums_one[2:4], sums_two[2:4], grad_bias_up.reshape(-1, width)], 0
    )
    red_vec = lax.psum_scatter(grad_vec, ("dp", "blk"), scatter_dimension=1, tiled=True)
    reduced = (red_qkv, red_out, red_up, red_down, red_vec)
    grad_norm = jnp.sqrt(
        lax.psum(sum(jnp.sum(part * part) for part in reduced), ("dp", "blk"))
    )
    return result, input_grad, grad_norm, reduced


def fits_one(patches, w_out):
    dp, blk = lax.axis_size("dp"), lax.axis_size("blk")
    share, width = w_out.shape
    return blk == 4 and dp % 2 == 0 and 2 * share % 16 == 0 and dp * blk * share == width


def per_device(
    patches, cotangent, short_lengths, long_lengths,
    w_qkv, w_out, w_up, w_down, vectors,
    first_qkv, first_out, first_up, first_down, first_vectors,
    second_qkv, second_out, second_up, second_down, second_vectors,
):
    layer = (patches, cotangent, short_lengths, long_lengths)
    weights = (w_qkv, w_out, w_up, w_down, vectors)
    if fits_one(patches, w_out):
        depth = lax.axis_size("dp") // 2
        result, input_grad, *gradients, norm = run_fused(depth, *layer, *weights)
    else:
        result, input_grad, grad_norm, gradients = layer_by_parts(*layer, *weights)
        norm = jnp.broadcast_to(grad_norm, (8, 128))
    firsts = (first_qkv, first_out, first_up, first_down, first_vectors)
    seconds = (second_qkv, second_out, second_up, second_down, second_vectors)
    return run_adamw(result, input_grad, norm, weights, firsts, seconds, gradients)


def solution(mesh):
    rows = P(("dp", "blk"), None)
    columns = P(None, ("dp", "blk"))
    group = (rows,) * 4 + (columns,)
    return jax.shard_map(
        per_device,
        mesh=mesh,
        in_specs=(rows, rows, rows, P("dp")) + group * 3,
        out_specs=(rows, rows, P()) + group * 4,
        check_vma=False,
    )
```

```python
import functools

import jax
import jax.numpy as jnp
from jax import lax
from jax.experimental import pallas as pl
from jax.experimental.pallas import tpu as pltpu
from jax.sharding import PartitionSpec as P

HD = 64
SHORT_DEV = 896
LONG_DEV = 128
STEP = 10
TILE = 128
BAND = 3 * TILE
PAIR = 2 * HD
ROWS = 256
CHUNK = 32

eps_norm = 1e-06
far_below = -1000000000.0
rate_matrix = 0.04
rate_vector = 0.5
beta_first = 0.5
beta_second = 0.5
eps_adam = 1e-08
decay_weight = 0.01
score_scale = HD ** (-0.5)
gelu_root = 0.7978845608028654
gelu_cube = 0.044715
VMEM_MOST = 60 * 1024 * 1024
FUSED_VMEM = 63 * 1024 * 1024


def dot(left, right):
    return lax.dot_general(left, right, (((1,), (0,)), ((), ())), preferred_element_type=jnp.float32)


def dot_tr(left, right):
    return lax.dot_general(left, right, (((1,), (1,)), ((), ())), preferred_element_type=jnp.float32)


def dot_tl(left, right):
    return lax.dot_general(left, right, (((0,), (0,)), ((), ())), preferred_element_type=jnp.float32)


def standardize(values):
    centered = values - jnp.mean(values, -1, keepdims=True)
    inv_std = lax.rsqrt(jnp.mean(centered * centered, -1, keepdims=True) + eps_norm)
    return centered * inv_std, inv_std


def norm_back(upstream, standard, inv_std, gain):
    scaled = upstream * gain
    inner = (
        scaled
        - jnp.mean(scaled, -1, keepdims=True)
        - standard * jnp.mean(scaled * standard, -1, keepdims=True)
    )
    return inner * inv_std


def column_sum(values):
    return jnp.sum(values, 0, keepdims=True)


def rows_at(step):
    return pl.ds(pl.multiple_of(step * ROWS, ROWS), ROWS)


def qkv_phase(x_ref, vec_ref, w_ref, h1_ref, qkv_ref):
    width = x_ref.shape[1]

    @pl.loop(0, x_ref.shape[0] // ROWS)
    def _(step):
        here = rows_at(step)
        unit, _ = standardize(x_ref[here, :].astype(jnp.float32))
        hidden = (unit * vec_ref[0:1, :] + vec_ref[1:2, :]).astype(jnp.bfloat16)
        h1_ref[here, :] = hidden
        for part, bias in ((0, 4), (1, None), (2, 5)):
            columns = slice(part * width, (part + 1) * width)
            made = dot(hidden, w_ref[:, columns])
            if bias is not None:
                made = made + vec_ref[bias : bias + 1, :]
            qkv_ref[here, columns] = made.astype(jnp.bfloat16)


def stack_heads(values, scale):
    lane = lax.broadcasted_iota(jnp.int32, values.shape, 1)
    if scale is not None:
        values = values * jnp.asarray(scale, values.dtype)
    zero = jnp.zeros_like(values)
    return jnp.concatenate(
        [jnp.where(lane < HD, values, zero), jnp.where(lane < HD, zero, values)], 0
    )


def unstack_heads(values):
    return jnp.concatenate([values[:HD, :TILE], values[HD:, TILE:]], 0)


def softmax_of(scores, allowed):
    scores = jnp.where(allowed, scores, far_below)
    top = jnp.max(scores, 0, keepdims=True)
    exponent = jnp.exp(scores - top)
    total = jnp.sum(exponent, 0, keepdims=True)
    return (exponent * (1.0 / total)).astype(jnp.bfloat16), top + jnp.log(total)


def attend_forward(queries, keys, values_tr, allowed):
    probs, log_total = softmax_of(dot_tr(keys, stack_heads(queries, score_scale)), allowed)
    return unstack_heads(dot(values_tr, probs)).astype(jnp.bfloat16), log_total


def softmax_back(scores, allowed, log_total, grad_probs):
    probs = jnp.exp(jnp.where(allowed, scores, far_below) - log_total)
    delta = jnp.sum(probs * grad_probs, 0, keepdims=True)
    grad_scores = (probs * (grad_probs - delta)).astype(jnp.bfloat16)
    return probs.astype(jnp.bfloat16), grad_scores


def attend_back(queries, keys, keys_tr, values, allowed, log_total, upstream):
    stacked_q = stack_heads(queries, score_scale)
    stacked_up = stack_heads(upstream, None)
    probs, grad_scores = softmax_back(
        dot_tr(keys, stacked_q), allowed, log_total, dot_tr(values, stacked_up)
    )
    grad_keys = dot(grad_scores, stacked_q)
    grad_values = dot(probs, stacked_up)
    grad_queries = unstack_heads(dot(keys_tr, grad_scores)) * score_scale
    return grad_queries.astype(jnp.bfloat16).T, grad_keys, grad_values


def mark_segments(ends_ref, key_seg, query_seg):
    count = ends_ref.shape[1]
    for tile in range(SHORT_DEV // TILE):
        rows = lax.broadcasted_iota(jnp.int32, (TILE, TILE), 0) + tile * TILE
        lanes = lax.broadcasted_iota(jnp.int32, (1, TILE), 1) + tile * TILE
        by_row = jnp.zeros((TILE, TILE), jnp.float32)
        by_lane = jnp.zeros((1, TILE), jnp.float32)
        end = jnp.int32(0)
        for clip in range(count):
            end = end + ends_ref[0, clip]
            by_row = by_row + jnp.where(rows >= end, 1.0, 0.0)
            by_lane = by_lane + jnp.where(lanes >= end, 1.0, 0.0)
        key_seg[tile * TILE : (tile + 1) * TILE, :] = by_row
        query_seg[tile] = by_lane


def band_start(tile):
    most = SHORT_DEV - BAND
    return pl.multiple_of(jnp.clip((tile - 1) * TILE, 0, most), TILE)


def pair_lanes(pair, offset=0):
    return pl.ds(pl.multiple_of(offset + pair * PAIR, PAIR), PAIR)


def short_mask(tile, key_seg, query_seg):
    band = key_seg[pl.ds(band_start(tile), BAND), :]
    line = query_seg[tile]
    return jnp.concatenate([band, band], 1) == jnp.concatenate([line, line], 1)


def long_mask(length_ref, keys):
    place = lax.broadcasted_iota(jnp.int32, (keys, 2 * TILE), 0)
    return place < length_ref[0]


def attention_forward_phase(qkv_ref, far_ref, length_ref, key_seg, query_seg, out_ref, lse_ref):
    width = out_ref.shape[1]
    pairs = width // PAIR
    tiles = SHORT_DEV // TILE

    @pl.loop(0, tiles)
    def _(tile):
        rows = pl.ds(pl.multiple_of(tile * TILE, TILE), TILE)
        band = pl.ds(band_start(tile), BAND)
        allowed = short_mask(tile, key_seg, query_seg)
        for pair in range(pairs):
            made, lse = attend_forward(
                qkv_ref[rows, pair * PAIR : (pair + 1) * PAIR],
                qkv_ref[band, width + pair * PAIR : width + (pair + 1) * PAIR],
                qkv_ref[band, 2 * width + pair * PAIR : 2 * width + (pair + 1) * PAIR].T,
                allowed,
            )
            out_ref[rows, pair * PAIR : (pair + 1) * PAIR] = made.T
            lse_ref[tile, pair] = lse

    @pl.loop(0, pairs)
    def _(pair):
        allowed = long_mask(length_ref, far_ref.shape[0])
        made, lse = attend_forward(
            qkv_ref[SHORT_DEV:, pair_lanes(pair)],
            far_ref[:, pair_lanes(pair)],
            far_ref[:, pair_lanes(pair, width)].T,
            allowed,
        )
        out_ref[SHORT_DEV:, pair_lanes(pair)] = made.T
        lse_ref[tiles, pair] = lse


def attention_back_long(qkv_ref, far_ref, length_ref, lse_ref, up_ref, dqkv_ref, far_grad):
    width = up_ref.shape[1]
    tiles = SHORT_DEV // TILE

    @pl.loop(0, width // PAIR)
    def _(pair):
        allowed = long_mask(length_ref, far_ref.shape[0])
        dq, dk, dv = attend_back(
            qkv_ref[SHORT_DEV:, pair_lanes(pair)],
            far_ref[:, pair_lanes(pair)],
            far_ref[:, pair_lanes(pair)].T,
            far_ref[:, pair_lanes(pair, width)],
            allowed,
            lse_ref[tiles, pair],
            up_ref[SHORT_DEV:, pair_lanes(pair)],
        )
        dqkv_ref[SHORT_DEV:, pair_lanes(pair)] = dq
        far_grad[:, pair_lanes(pair)] = dk.astype(jnp.bfloat16)
        far_grad[:, pair_lanes(pair, width)] = dv.astype(jnp.bfloat16)


def attention_back_short(qkv_ref, key_seg, query_seg, lse_ref, up_ref, dqkv_ref, dk_acc, dv_acc):
    width = up_ref.shape[1]
    tiles = SHORT_DEV // TILE

    @pl.loop(0, width // (2 * PAIR))
    def _(group):
        dk_acc[...] = jnp.zeros_like(dk_acc)
        dv_acc[...] = jnp.zeros_like(dv_acc)

        @pl.loop(0, tiles)
        def _(tile):
            rows = pl.ds(pl.multiple_of(tile * TILE, TILE), TILE)
            band = pl.ds(band_start(tile), BAND)
            allowed = short_mask(tile, key_seg, query_seg)
            for half in range(2):
                pair = group * 2 + half
                dq, dk, dv = attend_back(
                    qkv_ref[rows, pair_lanes(pair)],
                    qkv_ref[band, pair_lanes(pair, width)],
                    qkv_ref[band, pair_lanes(pair, width)].T,
                    qkv_ref[band, pair_lanes(pair, 2 * width)],
                    allowed,
                    lse_ref[tile, pair],
                    up_ref[rows, pair_lanes(pair)],
                )
                dqkv_ref[rows, pair_lanes(pair)] = dq
                own = slice(half * PAIR, (half + 1) * PAIR)
                dk_acc[band, own] += dk
                dv_acc[band, own] += dv

        lanes = 2 * PAIR
        k_at = pl.ds(pl.multiple_of(width + group * lanes, lanes), lanes)
        v_at = pl.ds(pl.multiple_of(2 * width + group * lanes, lanes), lanes)
        dqkv_ref[:SHORT_DEV, k_at] = dk_acc[...].astype(jnp.bfloat16)
        dqkv_ref[:SHORT_DEV, v_at] = dv_acc[...].astype(jnp.bfloat16)


def middle_phase(x_ref, vec_ref, w_ref, att_ref, middle_ref, h2_ref):
    @pl.loop(0, x_ref.shape[0] // ROWS)
    def _(step):
        here = rows_at(step)
        made = dot(att_ref[here, :], w_ref[...]) + vec_ref[6:7, :]
        middle = x_ref[here, :].astype(jnp.float32) + made
        middle_ref[here, :] = middle
        unit, _ = standardize(middle)
        h2_ref[here, :] = (unit * vec_ref[2:3, :] + vec_ref[3:4, :]).astype(jnp.bfloat16)


def gelu_both(values):
    square = values * values
    inner = values * (gelu_root + (gelu_root * gelu_cube) * square)
    bent = jnp.tanh(inner)
    half_up = 0.5 + 0.5 * bent
    slope = half_up + (0.5 * values) * (1.0 - bent * bent) * (
        gelu_root + (3.0 * gelu_root * gelu_cube) * square
    )
    return values * half_up, slope


def mlp_rows(h2_ref, dy_ref, up_ref, down_ref, bias, act_ref, du_ref, out_acc, dh2_acc, first):
    def body(step, total):
        here = rows_at(step)
        pre = dot(h2_ref[here, :], up_ref[...]) + bias
        grad_act = dot_tr(dy_ref[here, :], down_ref[...])
        act, slope = gelu_both(pre)
        act_low = act.astype(jnp.bfloat16)
        du_low = (grad_act * slope).astype(jnp.bfloat16)
        act_ref[here, :] = act_low
        du_ref[here, :] = du_low
        made = dot(act_low, down_ref[...])
        grad_hidden = dot_tr(du_low, up_ref[...])
        if first is True:
            out_acc[here, :] = made
            dh2_acc[here, :] = grad_hidden
        else:
            out_acc[here, :] += made
            dh2_acc[here, :] += grad_hidden
        return total + column_sum(du_low.astype(jnp.float32))

    width = up_ref.shape[1]
    return lax.fori_loop(0, h2_ref.shape[0] // ROWS, body, jnp.zeros((1, width), jnp.float32))


def middle_back_phase(
    dy_ref, middle_ref, dh2_ref, vec_ref, w_ref, dmiddle_ref, da_ref, datt_ref, gvec_ref
):
    def body(step, totals):
        here = rows_at(step)
        dy_low = dy_ref[here, :].astype(jnp.float32)
        dh2 = dh2_ref[here, :]
        unit, inv_std = standardize(middle_ref[here, :])
        dmiddle = dy_low + norm_back(dh2, unit, inv_std, vec_ref[2:3, :])
        dmiddle_ref[here, :] = dmiddle
        da = dmiddle.astype(jnp.bfloat16)
        da_ref[here, :] = da
        datt_ref[here, :] = dot_tr(da, w_ref[...]).astype(jnp.bfloat16)
        return (
            totals[0] + column_sum(dh2 * unit),
            totals[1] + column_sum(dh2),
            totals[2] + column_sum(da.astype(jnp.float32)),
            totals[3] + column_sum(dy_low),
        )

    zero = jnp.zeros((1, dy_ref.shape[1]), jnp.float32)
    totals = lax.fori_loop(0, dy_ref.shape[0] // ROWS, body, (zero,) * 4)
    for place in range(4):
        gvec_ref[place : place + 1, :] = totals[place]


def input_back_phase(x_ref, dqkv_ref, vec_ref, w_ref, dmiddle_ref, grad_ref, gvec_ref):
    width = x_ref.shape[1]

    def body(step, totals):
        here = rows_at(step)
        dh1 = dot_tr(dqkv_ref[here, :], w_ref[...])
        unit, inv_std = standardize(x_ref[here, :].astype(jnp.float32))
        grad_ref[here, :] = dmiddle_ref[here, :] + norm_back(dh1, unit, inv_std, vec_ref[0:1, :])
        return (
            totals[0] + column_sum(dh1 * unit),
            totals[1] + column_sum(dh1),
            totals[2] + column_sum(dqkv_ref[here, :width].astype(jnp.float32)),
            totals[3] + column_sum(dqkv_ref[here, 2 * width :].astype(jnp.float32)),
        )

    zero = jnp.zeros((1, width), jnp.float32)
    totals = lax.fori_loop(0, x_ref.shape[0] // ROWS, body, (zero,) * 4)
    for place in range(4):
        gvec_ref[place : place + 1, :] = totals[place]


def call(body, outs, scratch=(), smem=()):
    def run(*arrays):
        specs = [
            pl.BlockSpec(memory_space=pltpu.SMEM if place in smem else pltpu.VMEM)
            for place in range(len(arrays))
        ]
        return pl.pallas_call(
            body,
            out_shape=[jax.ShapeDtypeStruct(shape, kind) for shape, kind in outs],
            in_specs=specs,
            out_specs=[pl.BlockSpec(memory_space=pltpu.VMEM)] * len(outs),
            scratch_shapes=list(scratch),
            compiler_params=pltpu.CompilerParams(vmem_limit_bytes=VMEM_MOST),
        )(*arrays)

    return run


def forward_kernel(
    ends_ref, length_ref, x_ref, vec_ref, qkv_ref, far_ref, w_ref,
    att_ref, lse_ref, middle_ref, h2_ref, key_seg, query_seg,
):
    mark_segments(ends_ref, key_seg, query_seg)
    attention_forward_phase(qkv_ref, far_ref, length_ref, key_seg, query_seg, att_ref, lse_ref)
    middle_phase(x_ref, vec_ref, w_ref, att_ref, middle_ref, h2_ref)


def mlp_kernel(
    h2_ref, dy_ref, middle_ref, up_ref, down_ref, bias_ref, last_ref,
    out_ref, dh2_ref, gup_ref, gdown_ref, gbu_ref, act_ref, du_ref, out_acc,
):
    block = pl.program_id(0)

    @pl.when(block == 0)
    def _():
        out_acc[...] = jnp.zeros_like(out_acc)
        dh2_ref[...] = jnp.zeros_like(dh2_ref)

    gbu_ref[0] = mlp_rows(
        h2_ref, dy_ref, up_ref, down_ref, bias_ref[0], act_ref, du_ref, out_acc, dh2_ref, None
    )
    gup_ref[...] = dot_tl(h2_ref[...], du_ref[...])
    gdown_ref[...] = dot_tl(act_ref[...], dy_ref[...])

    @pl.when(block == pl.num_programs(0) - 1)
    def _():
        out_ref[...] = (middle_ref[...] + (out_acc[...] + last_ref[...])).astype(jnp.bfloat16)


def run_mlp(h2, dy, middle, w_up, w_down, bias_up, bias_down):
    rows, width = h2.shape
    units = w_up.shape[1]
    blocks = units // width
    whole = lambda shape: pl.BlockSpec(shape, lambda b: (0, 0))
    return pl.pallas_call(
        mlp_kernel,
        grid=(blocks,),
        out_shape=[
            jax.ShapeDtypeStruct((rows, width), jnp.bfloat16),
            jax.ShapeDtypeStruct((rows, width), jnp.float32),
            jax.ShapeDtypeStruct((width, units), jnp.float32),
            jax.ShapeDtypeStruct((units, width), jnp.float32),
            jax.ShapeDtypeStruct((blocks, 1, width), jnp.float32),
        ],
        in_specs=[
            whole((rows, width)),
            whole((rows, width)),
            whole((rows, width)),
            pl.BlockSpec((width, width), lambda b: (0, b)),
            pl.BlockSpec((width, width), lambda b: (b, 0)),
            pl.BlockSpec((1, 1, width), lambda b: (b, 0, 0)),
            whole((1, width)),
        ],
        out_specs=[
            whole((rows, width)),
            whole((rows, width)),
            pl.BlockSpec((width, width), lambda b: (0, b)),
            pl.BlockSpec((width, width), lambda b: (b, 0)),
            pl.BlockSpec((1, 1, width), lambda b: (b, 0, 0)),
        ],
        scratch_shapes=[
            pltpu.VMEM((rows, width), jnp.bfloat16),
            pltpu.VMEM((rows, width), jnp.bfloat16),
            pltpu.VMEM((rows, width), jnp.float32),
        ],
        compiler_params=pltpu.CompilerParams(vmem_limit_bytes=VMEM_MOST),
    )(h2, dy, middle, w_up, w_down, bias_up, bias_down)


def middle_back_kernel(
    dy_ref, middle_ref, dh2_ref, vec_ref, w_ref, att_ref,
    dmiddle_ref, datt_ref, gvec_ref, gout_ref, da_ref,
):
    middle_back_phase(
        dy_ref, middle_ref, dh2_ref, vec_ref, w_ref, dmiddle_ref, da_ref, datt_ref, gvec_ref
    )
    gout_ref[...] = dot_tl(att_ref[...], da_ref[...])


def attention_back_kernel(
    ends_ref, length_ref, qkv_ref, far_ref, lse_ref, datt_ref,
    dqkv_ref, far_grad, key_seg, query_seg, dk_acc, dv_acc,
):
    mark_segments(ends_ref, key_seg, query_seg)
    attention_back_long(qkv_ref, far_ref, length_ref, lse_ref, datt_ref, dqkv_ref, far_grad)
    width = datt_ref.shape[1]
    dqkv_ref[SHORT_DEV:, width:] = jnp.zeros((LONG_DEV, 2 * width), jnp.bfloat16)
    attention_back_short(
        qkv_ref, key_seg, query_seg, lse_ref, datt_ref, dqkv_ref, dk_acc, dv_acc
    )


def input_back_kernel(
    x_ref, h1_ref, dqkv_ref, near_ref, vec_ref, w_ref, dmiddle_ref,
    grad_ref, gqkv_ref, gvec_ref, mixed_ref,
):
    width = x_ref.shape[1]
    mixed_ref[...] = dqkv_ref[...]
    mixed_ref[SHORT_DEV:, width:] = near_ref[...]
    input_back_phase(x_ref, mixed_ref, vec_ref, w_ref, dmiddle_ref, grad_ref, gvec_ref)
    for part in range(3):
        columns = slice(part * width, (part + 1) * width)
        gqkv_ref[:, columns] = dot_tl(h1_ref[...], mixed_ref[:, columns])


def when(condition, body):
    if isinstance(condition, bool):
        if condition:
            body()
    else:
        pl.when(condition)(body)


def both(left, right):
    if isinstance(left, bool) and isinstance(right, bool):
        return left and right
    return jnp.logical_and(left, right)


def fold(values):
    return jnp.sum(values.reshape(-1, 8, values.shape[1]), 0)


def chunks_of(count, size):
    return [slice(start, start + size) for start in range(0, count, size)]


def softmax_into(scores, allowed_at, probs):
    parts = chunks_of(scores.shape[0], 64)
    top = None
    for part in parts:
        value = jnp.where(allowed_at(part), scores[part, :], far_below)
        scores[part, :] = value
        high = jnp.max(value.reshape(-1, 8, value.shape[1]), 0)
        top = high if top is None else jnp.maximum(top, high)
    top = jnp.max(top, 0, keepdims=True)
    total = None
    for part in parts:
        value = jnp.exp(scores[part, :] - top)
        scores[part, :] = value
        total = fold(value) if total is None else total + fold(value)
    total = jnp.sum(total, 0, keepdims=True)
    scale = 1.0 / total
    for part in parts:
        probs[part, :] = (scores[part, :] * scale).astype(jnp.bfloat16)
    return top + jnp.log(total)


def softmax_back_into(scores, grad_probs, allowed_at, log_total, probs, grad_scores):
    parts = chunks_of(scores.shape[0], 32)
    delta = None
    for part in parts:
        value = jnp.exp(jnp.where(allowed_at(part), scores[part, :], far_below) - log_total)
        scores[part, :] = value
        probs[part, :] = value.astype(jnp.bfloat16)
        share = fold(value * grad_probs[part, :])
        delta = share if delta is None else delta + share
    delta = jnp.sum(delta, 0, keepdims=True)
    for part in parts:
        grad = scores[part, :] * (grad_probs[part, :] - delta)
        grad_scores[part, :] = grad.astype(jnp.bfloat16)


class Places:
    def __init__(self, depth):
        self.depth = depth
        dp, blk = lax.axis_index("dp"), lax.axis_index("blk")
        self.dp, self.blk = dp, blk
        z, x, y, c = dp // 2, lax.rem(dp, 2), blk // 2, lax.rem(blk, 2)
        self.z, self.x, self.y, self.c = z, x, y, c
        flip = lambda value, by: lax.rem(value + by, 2)
        self.core = (dp, y * 2 + 1 - c)
        self.x_peer = (z * 2 + 1 - x, blk)
        self.y_peer = (dp, (1 - y) * 2 + c)
        self.first = (z * 2 + flip(x, 1 - c), flip(y, c) * 2 + c)
        self.second = (z * 2 + flip(x, c), flip(y, 1 - c) * 2 + c)
        self.corner = x * 4 + blk
        self.s, self.f = jnp.where(c == 0, y, x), jnp.where(c == 0, x, y)
        self.own = self.s * 2 + self.f
        self.at_first = self.s * 2 + 1 - self.f
        self.near_two = pl.ds(2 * self.s, 2)
        self.far_two = pl.ds(2 - 2 * self.s, 2)
        self.core_near_two = pl.ds(2 * self.f, 2)
        self.core_far_two = pl.ds(2 - 2 * self.f, 2)

    def z_peer(self, step):
        return (lax.rem(self.z + step, self.depth) * 2 + self.x, self.blk)

    def z_from(self, step):
        return lax.rem(self.z - step + self.depth, self.depth)

    def z_to(self, step):
        return lax.rem(self.z + step, self.depth)

    def plane_from(self, step):
        return lax.rem(self.corner - step + 8, 8)

    def plane_peer(self, step):
        corner = lax.rem(self.corner + step, 8)
        return (self.z * 2 + corner // 4, lax.rem(corner, 4))


def remote(source, target, sends, recvs, device):
    return pltpu.make_async_remote_copy(
        src_ref=source,
        dst_ref=target,
        send_sem=sends,
        recv_sem=recvs,
        device_id=device,
        device_id_type=pl.DeviceIdType.MESH,
    )


class Gather:
    def __init__(self, at, pieces, sends, recvs, plane=None):
        self.at, self.pieces, self.sends, self.recvs, self.plane = at, pieces, sends, recvs, plane
        self.near = at.depth - 1

    def along_z(self, block, step, whole, incoming):
        at = self.at
        source = at.z_from(step) if incoming else at.z
        region = self.pieces(block, None if whole else source, at.own, True)
        index = step - 1
        return remote(
            region, region, self.sends.at[block, index], self.recvs.at[block, index],
            at.z_peer(step),
        )

    def copy(self, block, kind, incoming=False):
        at = self.at
        device = (at.first, at.second, at.core, at.core)[kind]
        going = (at.own, at.near_two, at.near_two, at.far_two)
        coming = (at.at_first, at.far_two, at.core_near_two, at.core_far_two)
        place = (coming if incoming else going)[kind]
        region = self.pieces(block, None, place, not (incoming and kind >= 2))
        index = self.near + kind
        return remote(
            region, region, self.sends.at[block, index], self.recvs.at[block, index], device
        )

    def start(self, block, *kinds):
        for kind in kinds:
            self.copy(block, kind).start()

    def arrive(self, block, *kinds):
        for kind in kinds:
            self.copy(block, kind, True).wait_recv()

    def split(self, block, every, one):
        if self.plane is None:
            every()
            return
        single, z = self.plane(block)
        if isinstance(single, bool):
            one(z) if single else every()
            return
        pl.when(single)(lambda: one(z))
        pl.when(jnp.logical_not(single))(every)

    def push(self, block):
        def every():
            for step in range(1, self.at.depth):
                self.along_z(block, step, False, False).start()

        def one(z):
            @pl.when(self.at.z == z)
            def _():
                for step in range(1, self.at.depth):
                    self.along_z(block, step, True, False).start()

        self.split(block, every, one)

    def stage_two(self, block):
        def every():
            for step in range(1, self.at.depth):
                self.along_z(block, step, False, True).wait_recv()

        def one(z):
            @pl.when(self.at.z != z)
            def _():
                away = lax.rem(self.at.z - z + self.at.depth, self.at.depth)
                self.along_z(block, away, True, True).wait_recv()

        self.split(block, every, one)
        self.start(block, 0)

    def stage_three(self, block):
        self.arrive(block, 0)
        self.start(block, 1, 2)

    def stage_four(self, block):
        self.arrive(block, 1)
        self.start(block, 3)

    def finish(self, block):
        self.arrive(block, 2, 3)

    def sent(self, block):
        def every():
            for step in range(1, self.at.depth):
                self.along_z(block, step, False, False).wait_send()

        def one(z):
            @pl.when(self.at.z == z)
            def _():
                for step in range(1, self.at.depth):
                    self.along_z(block, step, True, False).wait_send()

        self.split(block, every, one)
        for kind in range(4):
            self.copy(block, kind).wait_send()


class Exchange:
    def __init__(self, at, sent, got, got_z, sends, recvs, slot):
        self.at, self.sent, self.got, self.got_z = at, sent, got, got_z
        self.sends, self.recvs, self.slot = sends, recvs, slot
        self.stage, self.copies, self.value = 0, [], None

    def copy(self, source, target, index, device):
        return remote(
            source, target, self.sends.at[self.slot, index], self.recvs.at[self.slot, index], device
        )

    def begin(self, value):
        at, stage = self.at, self.stage
        self.value = value
        self.sent[stage] = value
        peers = (at.core, at.x_peer, at.y_peer)
        if stage < 3:
            copy = self.copy(self.sent.at[stage], self.got.at[stage], stage, peers[stage])
            self.copies = [(copy, copy)]
        else:
            self.got_z[at.z] = value
            self.copies = []
            for step in range(1, at.depth):
                ends = [self.got_z.at[at.z], self.got_z.at[at.z_from(step)]]
                self.copies.append(
                    tuple(self.copy(self.sent.at[3], end, 2 + step, at.z_peer(step)) for end in ends)
                )
        for going, _ in self.copies:
            going.start()

    def step(self):
        for going, coming in self.copies:
            going.wait_send()
            coming.wait_recv()
        if self.stage < 3:
            value = self.value + self.got[self.stage]
            self.stage += 1
            self.begin(value)
            return None
        value = self.got_z[0]
        for place in range(1, self.at.depth):
            value = value + self.got_z[place]
        return value


class ShortExchange:
    def __init__(self, at, sent, got_z, got_plane, sends, recvs):
        self.at, self.sent, self.got_z, self.got_plane = at, sent, got_z, got_plane
        self.sends, self.recvs = sends, recvs

    def start(self, stage, landing, mine, value, others):
        self.sent[stage] = value
        landing[mine] = value
        copies = []
        for device, slot, index in others:
            ends = [landing.at[mine], landing.at[slot]]
            copies.append(
                tuple(
                    remote(self.sent.at[stage], end, self.sends.at[index], self.recvs.at[index], device)
                    for end in ends
                )
            )
        for going, _ in copies:
            going.start()
        return copies

    def finish(self, landing, copies):
        for going, coming in copies:
            going.wait_send()
            coming.wait_recv()
        value = landing[0]
        for place in range(1, landing.shape[0]):
            value = value + landing[place]
        return value

    def along_z(self, value):
        at = self.at
        others = [(at.z_peer(step), at.z_from(step), step - 1) for step in range(1, at.depth)]
        return self.start(0, self.got_z, at.z, value, others)

    def in_plane(self, value):
        at = self.at
        others = [
            (at.plane_peer(step), at.plane_from(step), at.depth - 2 + step) for step in range(1, 8)
        ]
        return self.start(1, self.got_plane, at.corner, value, others)


def fused_kernel(
    depth, ends_ref, length_ref, wqkv_ref, wout_ref, wup_ref, wdown_ref, vectors_ref, x_hbm, cot_hbm,
    out_hbm, grad_hbm, rqkv_ref, rout_ref, rup_ref, rdown_ref, rvec_ref, norm_ref,
    w, vbuf, vpad, give_out, asm, asm_down, vec, qkv, att, middle, h2, act, du, out_acc, dh2, dy,
    far, far_got, lse, key_seg, query_seg, turned, h2_tr, flat_up, flat_down, pre_grad,
    got_a, got_b, got_z, got_zd, red, squares, gvec, sums_two,
    v_sent, v_got, v_got_z, n_sent, n_got, n_got_z,
    swap_s, swap_r, ag_s, ag_r, vg_s, vg_r, kv_s, kv_r, fg_s, fg_r, rs_s, rs_r, ex_s, ex_r, no_s, no_r, local_s,
):
    bf16, f32 = jnp.bfloat16, jnp.float32
    at = Places(depth)
    rows, width = dy.shape
    spare = w.shape[0] - 2
    blocks = spare
    slab = w.shape[4]
    share = slab // 2
    half = width // 2
    lanes4 = 2 * PAIR
    groups = width // lanes4
    units = (blocks - groups - 1) // 2
    tiles = SHORT_DEV // TILE
    mine = pl.ds(pl.multiple_of(at.c * half, 128), half)
    other = pl.ds(pl.multiple_of((1 - at.c) * half, 128), half)
    my_rows = pl.ds(pl.multiple_of(at.c * share, 8), share)
    other_rows = pl.ds(pl.multiple_of((1 - at.c) * share, 8), share)
    tall = units * share
    my_tall = pl.ds(pl.multiple_of(at.c * tall, 8), tall)
    other_tall = pl.ds(pl.multiple_of((1 - at.c) * tall, 8), tall)
    wide = 2 * PAIR
    wide_at = lambda step: pl.ds(pl.multiple_of(step * wide, wide), wide)

    barrier = pltpu.get_barrier_semaphore()
    friends = [at.plane_peer(step) for step in range(1, 8)]
    friends += [at.z_peer(step) for step in range(1, depth)]
    for friend in friends:
        pl.semaphore_signal(barrier, inc=1, device_id=friend, device_id_type=pl.DeviceIdType.MESH)
    load_x = pltpu.make_async_copy(x_hbm, dy, local_s.at[0])
    load_x.start()

    def pair_part(part, pair):
        return pl.ds(pl.multiple_of(part * width + pair * PAIR, PAIR), PAIR)

    def own_slot(slot, side, columns):
        if slot < groups:
            parts = [lax.rem(place + side, 3) for place in range(3)]
            return [wqkv_ref[:, pair_part(part, 2 * slot + side)] for part in parts]
        if slot == groups:
            return [wout_ref[:, columns]]
        start = (slot - groups - 1) * width
        return [wup_ref[:, pl.ds(pl.multiple_of(start + side * half, 128), half)]]

    slots = groups + 1 + units
    for slot in range(slots):
        lane = 0
        for piece in own_slot(slot, 1 - at.c, other):
            give_out[slot, :, lane : lane + piece.shape[1]] = piece
            lane += piece.shape[1]
    vpad[...] = jnp.zeros_like(vpad)
    vpad[: vectors_ref.shape[0], : vectors_ref.shape[1]] = vectors_ref[...]
    vbuf[at.c, at.own, at.z] = vpad[...].astype(bf16)
    pl.semaphore_wait(barrier, len(friends))
    swaps = []
    for index, (low, high) in enumerate(((0, groups), (groups, slots))):
        swaps.append(
            remote(
                give_out.at[low:high], asm.at[low:high, my_rows, :],
                swap_s.at[index], swap_r.at[index], at.core,
            )
        )
    swaps.append(
        remote(wdown_ref.at[:, other], asm_down.at[my_tall, :], swap_s.at[2], swap_r.at[2], at.core)
    )
    for swap in swaps:
        swap.start()
    for slot in range(slots):
        lane = 0
        for piece in own_slot(slot, at.c, mine):
            asm[slot, my_rows, lane : lane + piece.shape[1]] = piece
            lane += piece.shape[1]
    asm_down[my_tall, :] = wdown_ref[:, mine]

    def weight_piece(block, z, place, own_half):
        side = at.c if own_half else 1 - at.c
        if z is None:
            return w.at[block, side, place]
        return w.at[block, side, place, z]

    def vector_piece(block, z, place, own_half):
        core = at.c if own_half else 1 - at.c
        if z is None:
            return vbuf.at[core, place]
        return vbuf.at[core, place, z]

    def plane(block):
        after = block - groups
        if isinstance(block, int):
            return after > 0 and after % 2 == 0, after // 2 - 1
        return jnp.logical_and(after > 0, lax.rem(after, 2) == 0), after // 2 - 1

    weights = Gather(at, weight_piece, ag_s, ag_r, plane)
    vectors = Gather(at, vector_piece, vg_s, vg_r)

    def push(block):
        def every():
            slot = jnp.where(block > groups, groups + 1 + (block - groups - 1) // 2, block)
            w[block, at.c, at.own, at.z] = asm[slot].astype(bf16)

        def one(z):
            @pl.when(at.z == z)
            def _():
                w[block, at.c, at.own] = asm_down[...].reshape(depth, slab, half).astype(bf16)

        weights.split(block, every, one)
        weights.push(block)

    def gather_even(turn):
        last, block = turn - 3, turn
        when(both(last >= 0, last < blocks), lambda: weights.stage_four(last))

        when(block < blocks, lambda: weights.stage_two(block))

    def gather_odd(turn):
        block = turn - 1
        when(both(block >= 0, block < blocks), lambda: weights.stage_three(block))

    vectors.push(0)
    swaps[0].wait_recv()
    for block in range(groups):
        push(block)
    mark_segments(ends_ref, key_seg, query_seg)
    swaps[1].wait_recv()
    swaps[2].wait_recv()
    vectors.stage_two(0)
    gather_even(0)
    for block in range(groups, 2 * groups):
        push(block)
    vectors.stage_three(0)
    gather_even(1)
    gather_odd(1)
    for block in range(2 * groups, blocks):
        push(block)
    vectors.stage_four(0)
    gather_even(2)
    gather_odd(2)
    vectors.finish(0)
    gather_even(3)

    per = vectors_ref.shape[1]
    lane_inverse = (1 << 16) // per + 1
    spread_row = lax.broadcasted_iota(jnp.int32, (128, width), 0)
    spread_col = lax.broadcasted_iota(jnp.int32, (128, width), 1)
    spread_place = spread_col - ((spread_col * lane_inverse) >> 16) * per
    spread = jnp.where(spread_row == spread_place, 1.0, 0.0).astype(bf16)
    whole = jnp.zeros((16, width), f32)
    row = lax.broadcasted_iota(jnp.int32, (8 * 16, width), 0)
    col = (lax.broadcasted_iota(jnp.int32, (8 * 16, width), 1) * lane_inverse) >> 16
    core, place = row >> 6, (row >> 4) & 3
    place = jnp.where(core == 0, ((place & 1) << 1) | (place >> 1), place)
    device = place * 2 + core
    for level in range(depth):
        values = dot(vbuf[:, :, level].reshape(8 * 16, 128), spread)
        values = jnp.where(col == device + level * 8, values, 0.0).reshape(8, 16, width)
        whole = whole + jnp.sum(values, 0)
    vec[...] = whole

    def row_chunks(step):
        return [
            pl.ds(pl.multiple_of(step * ROWS + start, CHUNK), CHUNK)
            for start in range(0, ROWS, CHUNK)
        ]

    def first_norm(target, first_time):
        @pl.loop(0, rows // ROWS)
        def _(step):
            for here in row_chunks(step):
                value = dy[here, :].astype(f32)
                unit, _ = standardize(value)
                act[here, :] = (unit * vec[0:1, :] + vec[1:2, :]).astype(bf16)
                if first_time:
                    middle[here, :] = value
            if not first_time:
                target[:, rows_at(step)] = act[rows_at(step), :].T

    load_x.wait()
    first_norm(act, True)
    load_dy = pltpu.make_async_copy(cot_hbm, dy, local_s.at[0])
    load_dy.start()

    def allowed_short(tile):
        start, line = band_start(tile), query_seg[tile]

        def allowed(part):
            count = part.stop - part.start
            band = key_seg[pl.ds(pl.multiple_of(start + part.start, 32), count), :]
            return jnp.concatenate([band, band], 1) == jnp.concatenate([line, line], 1)

        return allowed

    def allowed_long(part):
        shape = (part.stop - part.start, 2 * TILE)
        return lax.broadcasted_iota(jnp.int32, shape, 0) + part.start < length_ref[0]

    third = 3 * PAIR

    def group_columns(group, offset, count):
        return pl.ds(pl.multiple_of(group * width + offset, 128), count)

    def lane_of(part, side):
        return side * third + (part - side) % 3 * PAIR

    def q_at(group, side):
        return group_columns(group, lane_of(0, side), PAIR)

    def k_at(group, side):
        return group_columns(group, lane_of(1, side), PAIR)

    def v_at(group, side):
        return group_columns(group, lane_of(2, side), PAIR)

    def kv_at(group, side):
        return group_columns(group, lane_of(1, side), 2 * PAIR)

    def far_columns(group, side):
        return pl.ds(pl.multiple_of((2 * group + side) * 2 * PAIR, 128), 2 * PAIR)

    y_blk, core_blk = (1 - at.y) * 2 + at.c, at.y * 2 + 1 - at.c
    both_blk = 3 - at.blk

    def keys_copy(group, role, incoming=False):
        columns = pl.ds(pl.multiple_of(group * 4 * PAIR, 128), 4 * PAIR)
        device = (at.y_peer, at.core, at.core)[role]
        if incoming:
            source = target = far.at[(y_blk, core_blk, both_blk)[role], :, columns]
        elif role == 2:
            source = target = far.at[y_blk, :, columns]
        else:
            source = qkv.at[SHORT_DEV:, group_columns(group, PAIR, 4 * PAIR)]
            target = far.at[at.blk, :, columns]
        return remote(source, target, kv_s.at[group, role], kv_r.at[group, role], device)

    def strips(natural):
        for side in range(2):
            for place in range(4):
                high, low = place // 2, place % 2
                chip = (low * 2 + high) if side == 0 else place
                for level in range(depth):
                    order = chip * depth + level if natural else level * 4 + chip
                    yield side, place, level, order * slab

    def flatten(target, block, natural=False):
        for side, place, level, start in strips(natural):
            target[start : start + slab, side * half : (side + 1) * half] = w[
                block, side, place, level
            ]

    @pl.loop(0, groups)
    def _(group):
        weights.finish(group)
        bias = []
        for side in range(2):
            lanes = pl.ds(pl.multiple_of((2 * group + side) * PAIR, PAIR), PAIR)
            three = [vec[4:5, lanes], jnp.zeros((1, PAIR), f32), vec[5:6, lanes]]
            bias += three[side:] + three[:side]
        flat_down[0:1, :] = jnp.concatenate(bias, 1).astype(bf16)
        flatten(flat_up, group)

        @pl.loop(0, width // wide)
        def _(step):
            made = dot(act[...], flat_up[:, wide_at(step)])
            made = made + flat_down[0:1, wide_at(step)].astype(f32)
            qkv[:, group_columns(group, step * wide, wide)] = made.astype(bf16)

        keys_copy(group, 0).start()
        keys_copy(group, 1).start()
        for side in range(2):
            far[at.blk, :, far_columns(group, side)] = qkv[SHORT_DEV:, kv_at(group, side)]
            turned[side * PAIR : (side + 1) * PAIR, :] = qkv[:SHORT_DEV, v_at(group, side)].T

        gather_odd(groups + 2 * group)

        def tile_rows(tile):
            return pl.ds(pl.multiple_of(tile * TILE, TILE), TILE)

        def slot_rows(slot):
            return slice(slot * BAND, (slot + 1) * BAND)

        def products(tile, side):
            made = unstack_heads(
                dot(
                    turned[side * PAIR : (side + 1) * PAIR, pl.ds(band_start(tile), BAND)],
                    flat_down[slot_rows(side), :wide],
                )
            )
            att[pair_lanes(group * 2 + side), tile_rows(tile)] = made.astype(bf16)

        def soften(tile, side):
            lse[tile, group * 2 + side] = softmax_into(
                out_acc.at[slot_rows(side), :wide],
                allowed_short(tile),
                flat_down.at[slot_rows(side), :wide],
            )

        def compare(tile, side):
            queries = stack_heads(qkv[tile_rows(tile), q_at(group, side)], score_scale)
            keys = qkv[pl.ds(band_start(tile), BAND), k_at(group, side)]
            out_acc[slot_rows(side), :wide] = dot_tr(keys, queries)

        @pl.loop(0, tiles + 1)
        def _(turn):
            now, last = jnp.minimum(turn, tiles - 1), jnp.maximum(turn - 1, 0)
            products(last, 0)
            soften(last, 1)
            compare(now, 0)
            products(last, 1)
            soften(now, 0)
            compare(now, 1)
            pl.when(turn == 1)(lambda: gather_even(groups + 1 + 2 * group))

            @pl.when(turn == 3)
            def _():
                gather_odd(groups + 1 + 2 * group)
                keys_copy(group, 0, True).wait_recv()
                keys_copy(group, 2).start()

            pl.when(turn == 6)(lambda: gather_even(groups + 2 + 2 * group))

    def far_pair(pair, offset):
        return pl.ds(pl.multiple_of(pair * 2 * PAIR + offset, PAIR), PAIR)

    def far_block(pair, offset):
        return far[:, :, far_pair(pair, offset)].reshape(4 * LONG_DEV, PAIR)

    gather_odd(3 * groups)
    for group in range(groups):
        keys_copy(group, 1, True).wait_recv()
        keys_copy(group, 2, True).wait_recv()

    @pl.loop(0, groups)
    def _(group):
        long_rows = lambda side: slice(side * 4 * LONG_DEV, (side + 1) * 4 * LONG_DEV)
        for side in range(2):
            queries = stack_heads(qkv[SHORT_DEV:, q_at(group, side)], score_scale)
            out_acc[long_rows(side), :wide] = dot_tr(far_block(2 * group + side, 0), queries)
        for side in range(2):
            pair = 2 * group + side
            probs = flat_down.at[: 4 * LONG_DEV, side * wide : (side + 1) * wide]
            lse[tiles, pair] = softmax_into(
                out_acc.at[long_rows(side), :wide], allowed_long, probs
            )
            made = unstack_heads(dot(far_block(pair, PAIR).T, probs[...]))
            att[pair_lanes(pair), SHORT_DEV:] = made.astype(bf16)
        pl.when(group == 0)(lambda: gather_even(3 * groups + 1))
        pl.when(group == groups - 1)(lambda: gather_odd(3 * groups + 1))

    weights.finish(groups)
    for group in range(groups):
        for role in range(3):
            keys_copy(group, role).wait_send()

    load_dy.wait()
    place = lax.broadcasted_iota(jnp.int32, (LONG_DEV, width), 0) + at.blk * LONG_DEV
    keep = place < length_ref[0]
    dy[SHORT_DEV:, :] = jnp.where(keep, dy[SHORT_DEV:, :].astype(f32), 0.0).astype(bf16)

    act[...] = att[...].T
    flatten(flat_up, groups)
    gather_even(3 * groups + 2)

    @pl.loop(0, width // wide)
    def _(step):
        columns = wide_at(step)
        made = dot(act[...], flat_up[:, columns]) + vec[6:7, columns]
        middle[:, columns] = middle[:, columns] + made

    @pl.loop(0, rows // ROWS)
    def _(step):
        for here in row_chunks(step):
            unit, _ = standardize(middle[here, :])
            h2[here, :] = (unit * vec[2:3, :] + vec[3:4, :]).astype(bf16)
        h2_tr[:, rows_at(step)] = h2[rows_at(step), :].T

    def piece(block, place):
        return w.at[block, at.c, place]

    turns = [*range(groups + 1, blocks), groups, *range(groups)]

    def landing(block, side):
        if isinstance(block, int) and block <= groups:
            return turns[turns.index(block) - 4], side
        order = block - groups - 1
        odd = jnp.logical_and(order < 4, lax.rem(order, 2) == 1)
        return (
            jnp.where(order < 4, spare + order // 2, block - 4),
            jnp.where(odd, 1 - side, side),
        )

    def to_core(block):
        place, side = landing(block, at.c)
        return remote(
            w.at[block, 1 - at.c], w.at[place, side], rs_s.at[block, 0], rs_r.at[block, 0], at.core
        )

    def going(block, index):
        sends, recvs = rs_s.at[block, index], rs_r.at[block, index]
        if index == 1:
            return remote(piece(block, at.far_two), got_a.at[block], sends, recvs, at.second)
        return remote(piece(block, at.at_first), got_b.at[block], sends, recvs, at.first)

    def along_z(block, step):
        index = 4 + step
        return remote(
            w.at[block, at.c, at.own, at.z_to(step)], got_z.at[block, step - 1],
            rs_s.at[block, index], rs_r.at[block, index], at.z_peer(step),
        )

    def to_plane(block, step):
        index = 4 + step
        return remote(
            piece(block, at.own), got_zd.at[step - 1],
            rs_s.at[block, index], rs_r.at[block, index], at.z_peer(step),
        )

    def swap_back(block, tall_one, incoming=False):
        sends, recvs = rs_s.at[block, 4], rs_r.at[block, 4]
        columns = other if incoming else mine
        if tall_one:
            return remote(
                asm_down.at[other_tall, :], red.at[pl.ds(blocks_low, tall), columns],
                sends, recvs, at.core,
            )
        return remote(
            asm.at[slot_of(block), other_rows, :], red.at[red_rows(block), columns],
            sends, recvs, at.core,
        )

    blocks_low = slots * share

    def slot_of(block):
        if isinstance(block, int):
            return block if block <= groups else groups + 1 + (block - groups - 1) // 2
        return jnp.where(block > groups, groups + 1 + (block - groups - 1) // 2, block)

    def red_rows(block):
        return pl.ds(pl.multiple_of(slot_of(block) * share, 8), share)

    def add_piece(block, place, got):
        w[block, at.c, place] = w[block, at.c, place] + got

    def scatter_one(block):
        to_core(block).wait_recv()
        where, side = landing(block, 1 - at.c)
        add_piece(block, at.far_two, w[where, side, at.far_two])
        going(block, 1).start()
        add_piece(block, at.near_two, w[where, side, at.near_two])

    def scatter_two(block):
        going(block, 1).wait_recv()
        add_piece(block, at.at_first, got_a[block, 1 - at.f])
        going(block, 3).start()
        add_piece(block, at.own, got_a[block, at.f])

    def scatter_three(block):
        going(block, 3).wait_recv()
        add_piece(block, at.own, got_b[block])

        def every():
            for step in range(1, depth):
                along_z(block, step).start()

        def one(z):
            @pl.when(at.z != z)
            def _():
                to_plane(block, lax.rem(z - at.z + depth, depth)).start()

        weights.split(block, every, one)

    def scatter_four(block):
        def every():
            total = w[block, at.c, at.own, at.z].astype(f32)
            for step in range(1, depth):
                along_z(block, step).wait_recv()
                total = total + got_z[block, step - 1].astype(f32)
            slot = slot_of(block)
            asm[slot] = total
            squares[...] += total * total
            swap_back(block, False).start()
            red[red_rows(block), mine] = asm[slot, my_rows, :]

        def one(z):
            @pl.when(at.z == z)
            def _():
                for step in range(1, depth):
                    to_plane(block, step).wait_recv()
                total = w[block, at.c, at.own].astype(f32)
                for step in range(1, depth):
                    total = total + got_zd[step - 1].astype(f32)
                asm_down[...] = total.reshape(2 * tall, half)
                squares[...] += jnp.sum(total * total, 0)
                swap_back(block, True).start()
                red[pl.ds(blocks_low, tall), mine] = asm_down[my_tall, :]

        weights.split(block, every, one)

    def scatter_end(block):
        def every():
            swap_back(block, False, True).wait_recv()
            swap_back(block, False).wait_send()
            for step in range(1, depth):
                along_z(block, step).wait_send()

        def one(z):
            @pl.when(at.z == z)
            def _():
                swap_back(block, True, True).wait_recv()
                swap_back(block, True).wait_send()

            @pl.when(at.z != z)
            def _():
                to_plane(block, lax.rem(z - at.z + depth, depth)).wait_send()

        weights.split(block, every, one)
        for index in (1, 3):
            going(block, index).wait_send()

    stages = (scatter_one, scatter_two, scatter_three, scatter_four)

    def scatter_pump(turn):
        for stage, first, pace in zip(stages, (4, 7, 11, 14), (2, 3, 3, 3)):
            if isinstance(turn, int):
                order = (turn - first) // pace
                if (turn - first) % pace == 0 and 0 <= order <= 2 * units:
                    stage(turns[order])
                continue
            late = turn - first
            due = jnp.logical_and(late >= 0, lax.rem(late, pace) == 0)
            pl.when(due)(functools.partial(stage, groups + 1 + lax.div(late, pace)))

    def give(block, gradient, natural=False):
        weights.sent(block)
        if isinstance(block, int) and block <= groups:
            to_core(turns[turns.index(block) - 2]).wait_send()
        else:
            pl.when(block > groups + 2)(lambda: to_core(block - 2).wait_send())
        low = gradient.astype(bf16)
        for side, place, level, start in strips(natural):
            w[block, side, place, level] = low[
                start : start + slab, side * half : (side + 1) * half
            ]
        to_core(block).start()

    squares[...] = jnp.zeros_like(squares)
    out_acc[...] = jnp.zeros_like(out_acc)
    dh2[...] = jnp.zeros_like(dh2)
    gvec[...] = jnp.zeros_like(gvec)

    @pl.loop(0, units)
    def _(unit):
        up, down = groups + 1 + 2 * unit, groups + 2 + 2 * unit
        weights.finish(up)
        weights.finish(down)
        flatten(flat_up, up)
        flatten(flat_down, down, True)

        @pl.loop(0, width // wide)
        def _(step):
            @pl.when(step == 0)
            def _():
                gather_odd(3 * groups + 2 + 2 * unit)
                scatter_pump(4 * unit)

            @pl.when(step == 2)
            def _():
                gather_even(3 * groups + 3 + 2 * unit)
                scatter_pump(4 * unit + 1)

            columns = wide_at(step)
            bias = vec[pl.ds(8 + unit, 1), columns]
            total = jnp.zeros((8, wide), f32)
            for half_rows in chunks_of(rows, rows // 2):
                pre_grad[:, :wide] = dot(h2[half_rows, :], flat_up[:, columns])
                pre_grad[:, wide:] = dot_tr(dy[half_rows, :], flat_down[columns, :])
                for part in chunks_of(rows // 2, CHUNK):
                    here = slice(half_rows.start + part.start, half_rows.start + part.stop)
                    made, slope = gelu_both(pre_grad[part, :wide] + bias)
                    act[here, columns] = made.astype(bf16)
                    du_low = (pre_grad[part, wide:] * slope).astype(bf16)
                    du[here, columns] = du_low
                    total = total + fold(du_low.astype(f32))
            gvec[pl.ds(8 + unit, 1), columns] = column_sum(total)

        @pl.loop(0, width // wide)
        def _(step):
            @pl.when(step == 1)
            def _():
                gather_odd(3 * groups + 3 + 2 * unit)
                scatter_pump(4 * unit + 2)

            columns = wide_at(step)
            out_acc[:, columns] += dot(act[...], flat_down[:, columns])
            dh2[:, columns] += dot_tr(du[...], flat_up[columns, :])

        gather_even(3 * groups + 4 + 2 * unit)
        scatter_pump(4 * unit + 3)
        give(up, dot(h2_tr[...], du[...]))
        give(down, dot_tl(act[...], dy[...]), True)

    sums_two[...] = jnp.zeros_like(sums_two)

    @pl.loop(0, rows // ROWS)
    def _(step):
        for turn in range(rows // ROWS):
            pl.when(step == turn)(functools.partial(scatter_pump, 4 * units + turn))
        for here in row_chunks(step):
            middle_here = middle[here, :]
            out = middle_here + (out_acc[here, :] + vec[7:8, :])
            h2[here, :] = out.astype(bf16)
            dy_here = dy[here, :].astype(f32)
            dh2_here = dh2[here, :]
            unit, inv_std = standardize(middle_here)
            dmiddle = dy_here + norm_back(dh2_here, unit, inv_std, vec[2:3, :])
            dh2[here, :] = dmiddle
            da = dmiddle.astype(bf16)
            act[here, :] = da
            sums_two[0] += fold(dh2_here * unit)
            sums_two[1] += fold(dh2_here)
            sums_two[2] += fold(da.astype(f32))
            sums_two[3] += fold(dy_here)

    for place, line in enumerate((2, 3, 6, 7)):
        gvec[line : line + 1, :] = column_sum(sums_two[place])
    flatten(flat_up, groups)

    @pl.loop(0, width // wide)
    def _(step):
        columns = wide_at(step)
        du[:, columns] = dot_tr(act[...], flat_up[columns, :]).astype(bf16)

    store_out = pltpu.make_async_copy(h2, out_hbm, local_s.at[0])
    store_out.start()
    load_again = pltpu.make_async_copy(x_hbm, dy, local_s.at[2])
    load_again.start()
    give(groups, dot(att[...], act[...]))
    load_again.wait()
    first_norm(h2_tr, False)

    after = 4 * units + rows // ROWS

    @pl.loop(0, groups)
    def _(group):
        long_rows = lambda side: slice(side * 4 * LONG_DEV, (side + 1) * 4 * LONG_DEV)

        def stacked_long(side):
            return (
                stack_heads(qkv[SHORT_DEV:, q_at(group, side)], score_scale),
                stack_heads(du[SHORT_DEV:, pair_lanes(2 * group + side)], None),
            )

        for side in range(2):
            queries, upstream = stacked_long(side)
            here, pair = long_rows(side), 2 * group + side
            out_acc[here, :wide] = dot_tr(far_block(pair, 0), queries)
            out_acc[here, wide : 2 * wide] = dot_tr(far_block(pair, PAIR), upstream)
        for side in range(2):
            queries, upstream = stacked_long(side)
            here, pair = long_rows(side), 2 * group + side
            lanes = slice(side * wide, (side + 1) * wide)
            probs = flat_down.at[: 4 * LONG_DEV, lanes]
            grad_scores = flat_up.at[: 4 * LONG_DEV, lanes]
            softmax_back_into(
                out_acc.at[here, :wide], out_acc.at[here, wide : 2 * wide], allowed_long,
                lse[tiles, pair], probs, grad_scores,
            )
            dk, dv = dot(grad_scores[...], queries), dot(probs[...], upstream)
            dq = unstack_heads(dot(far_block(pair, 0).T, grad_scores[...])) * score_scale
            qkv[SHORT_DEV:, q_at(group, side)] = dq.astype(bf16).T
            far[:, :, far_pair(pair, 0)] = dk.astype(bf16).reshape(4, LONG_DEV, PAIR)
            far[:, :, far_pair(pair, PAIR)] = dv.astype(bf16).reshape(4, LONG_DEV, PAIR)
        for turn in range(groups):
            pl.when(group == turn)(functools.partial(scatter_pump, after + turn))

    flats = (flat_up, act.at[:width, :], att.at[:, :width])

    far_one = remote(far.at[core_blk], far_got.at[0], fg_s.at[0], fg_r.at[0], at.core)
    far_two = remote(far.at[both_blk], far_got.at[1], fg_s.at[1], fg_r.at[1], at.core)
    far_three = remote(far.at[y_blk], far_got.at[2], fg_s.at[2], fg_r.at[2], at.y_peer)
    far_two.start()
    far_one.start()
    store_out.wait()
    lse[tiles + 1] = jnp.full(lse.shape[1:], 1e30, f32)
    flat_down[...] = jnp.zeros_like(flat_down)

    @pl.loop(0, groups)
    def _(group):
        middle[:SHORT_DEV, 0 : 4 * PAIR] = jnp.zeros((SHORT_DEV, 4 * PAIR), f32)
        flat_down[:BAND, 0 : 2 * wide] = jnp.zeros((BAND, 2 * wide), bf16)
        before = group - 1

        def pump(place):
            for now in range(groups):
                turn = after + groups + 5 * now + place
                pl.when(group == now)(functools.partial(scatter_pump, turn))

            @pl.when(group > 0)
            def _():
                if place == 0:
                    pl.when(group > 1)(lambda: scatter_four(group - 2))
                if place == 1:
                    for block in range(groups - 1):
                        pl.when(before == block)(functools.partial(scatter_one, block))
                if place == 3:
                    scatter_two(before)
                if place == 4:
                    scatter_three(before)

        pump(0)
        for side in range(2):
            turned[side * PAIR : (side + 1) * PAIR, :] = qkv[:SHORT_DEV, k_at(group, side)].T

        def tile_rows(tile):
            return pl.ds(pl.multiple_of(tile * TILE, TILE), TILE)

        def slot_rows(slot):
            return slice(slot * BAND, (slot + 1) * BAND)

        def stacked(tile, side):
            here = tile_rows(tile)
            return (
                stack_heads(qkv[here, q_at(group, side)], score_scale),
                stack_heads(du[here, pair_lanes(group * 2 + side)], None),
            )

        def products(tile, side, target):
            queries, upstream = stacked(tile, side)
            band = pl.ds(band_start(tile), BAND)
            probs = flat_down[slot_rows(side), :wide]
            grad_scores = flat_down[slot_rows(side), wide : 2 * wide]
            start = side * 2 * PAIR
            middle[band, start : start + PAIR] += dot(grad_scores, queries)
            middle[band, start + PAIR : start + 2 * PAIR] += dot(probs, upstream)
            keys_tr = turned[side * PAIR : (side + 1) * PAIR, band]
            dq = unstack_heads(dot(keys_tr, grad_scores)) * score_scale
            h2[tile_rows(target), pair_lanes(group * 2 + side)] = dq.astype(bf16).T

        def soften(tile, side, source):
            softmax_back_into(
                middle.at[slot_rows(side), 2 * wide : 3 * wide],
                out_acc.at[slot_rows(side), :wide],
                allowed_short(tile),
                lse[source, group * 2 + side],
                flat_down.at[slot_rows(side), :wide],
                flat_down.at[slot_rows(side), wide : 2 * wide],
            )

        def compare(tile, side):
            queries, upstream = stacked(tile, side)
            band = pl.ds(band_start(tile), BAND)
            middle[slot_rows(side), 2 * wide : 3 * wide] = dot_tr(
                qkv[band, k_at(group, side)], queries
            )
            out_acc[slot_rows(side), :wide] = dot_tr(qkv[band, v_at(group, side)], upstream)

        @pl.loop(0, tiles + 1)
        def _(turn):
            now, last = jnp.minimum(turn, tiles - 1), jnp.maximum(turn - 1, 0)
            target = jnp.where(turn == 0, tiles, last)
            products(last, 0, target)
            soften(last, 1, jnp.where(turn == 0, tiles + 1, last))
            compare(now, 0)
            products(last, 1, target)
            soften(now, 0, now)
            compare(now, 1)

            @pl.when(turn == 1)
            def _():
                pump(1)

                @pl.when(group == 0)
                def _():
                    far_two.wait_recv()
                    far[y_blk] = far[y_blk] + far_got[1]
                    far_three.start()

            pl.when(turn == 3)(lambda: pump(2))
            pl.when(turn == 6)(lambda: pump(3))

        for side in range(2):
            qkv[:SHORT_DEV, q_at(group, side)] = h2[:SHORT_DEV, pair_lanes(group * 2 + side)]

        @pl.when(group == 0)
        def _():
            far_one.wait_recv()
            far_three.wait_recv()

        for side in range(2):
            start = side * 2 * PAIR
            qkv[:SHORT_DEV, kv_at(group, side)] = middle[
                :SHORT_DEV, start : start + 2 * PAIR
            ].astype(bf16)
            near_at = far_columns(group, side)
            near = far[at.blk, :, near_at].astype(f32) + far_got[0, :, near_at].astype(f32)
            near = near + far_got[2, :, near_at].astype(f32)
            qkv[SHORT_DEV:, kv_at(group, side)] = near.astype(bf16)

        for block, target in enumerate(flats):
            pl.when(group == block)(functools.partial(flatten, target, block))
        gradient = dot(h2_tr[...], qkv[:, group_columns(group, 0, width)])
        for block in range(groups):
            pl.when(group == block)(functools.partial(give, block, gradient))

        pump(4)
        sums = column_sum(qkv[:, group_columns(group, 0, width)].astype(f32))
        for side in range(2):
            own = pl.ds(pl.multiple_of((2 * group + side) * PAIR, PAIR), PAIR)
            for part, line in ((0, 4), (2, 5)):
                lane = lane_of(part, side)
                gvec[line : line + 1, own] = sums[:, lane : lane + PAIR]

    def input_rows(step):
        sums_two[0:2] = jnp.zeros((2, 8, width), f32)

        @pl.loop(step * (rows // ROWS // 2), (step + 1) * (rows // ROWS // 2))
        def _(block):
            for here in row_chunks(block):
                unit, inv_std = standardize(dy[here, :].astype(f32))
                dh1 = out_acc[here, :]
                middle[here, :] = dh2[here, :] + norm_back(dh1, unit, inv_std, vec[0:1, :])
                sums_two[0] += fold(dh1 * unit)
                sums_two[1] += fold(dh1)

        return column_sum(sums_two[0]), column_sum(sums_two[1])

    latest = groups - 1
    scatter_one(latest)

    @pl.loop(0, width // wide)
    def _(step):
        columns = wide_at(step)
        made = jnp.zeros((rows, wide), f32)
        for group, flat in enumerate(flats):
            made = made + dot_tr(qkv[:, group * width : (group + 1) * width], flat[columns, :])
        out_acc[:, columns] = made

    gain_low, shift_low = input_rows(0)
    scatter_pump(after + 6 * groups)
    scatter_four(latest - 1)
    gain_high, shift_high = input_rows(1)
    store_grad = pltpu.make_async_copy(middle, grad_hbm, local_s.at[1])
    store_grad.start()
    gvec[0:1, :] = gain_low + gain_high
    gvec[1:2, :] = shift_low + shift_high
    exchange = Exchange(at, v_sent, v_got, v_got_z, ex_s, ex_r, 0)
    exchange.begin(gvec[...])
    scatter_two(latest)
    exchange.step()
    scatter_three(latest)
    exchange.step()
    exchange.step()
    scatter_four(latest)

    weight_square = jnp.sum(squares[...], keepdims=True)
    norms = ShortExchange(at, n_sent, n_got_z, n_got, no_s, no_r)
    norm_copies = norms.along_z(jnp.broadcast_to(weight_square, n_sent.shape[1:]))
    vector_sum = exchange.step()
    device = at.dp * 4 + at.blk
    turn_by = lax.rem(width - device * per, width)
    rvec_ref[...] = pltpu.roll(vector_sum, turn_by, 1)[:, :128]
    vector_square = jnp.sum(vector_sum * vector_sum, keepdims=True)
    norm_copies = norms.in_plane(norms.finish(n_got_z, norm_copies))

    @pl.loop(0, blocks)
    def _(block):
        @pl.when(block > groups)
        def _():
            scatter_end(block)

    for block in range(groups + 1):
        scatter_end(block)
    for block in turns[-2:]:
        to_core(block).wait_send()
    for group in range(groups):
        for side in range(2):
            for part in range(3):
                start = part * width + (2 * group + side) * PAIR
                lane = lane_of(part, side)
                rqkv_ref[:, start : start + PAIR] = red[
                    group * share : (group + 1) * share, lane : lane + PAIR
                ]
    rout_ref[...] = red[groups * share : (groups + 1) * share, :]
    for unit in range(units):
        start = (groups + 1 + unit) * share
        rup_ref[:, unit * width : (unit + 1) * width] = red[start : start + share, :]
    rdown_ref[...] = red[blocks_low : blocks_low + tall, :]
    far_one.wait_send()
    far_two.wait_send()
    far_three.wait_send()
    for swap in swaps:
        swap.wait_send()
    vectors.sent(0)
    norm_ref[...] = jnp.sqrt(norms.finish(n_got, norm_copies) + vector_square)
    store_grad.wait()


def run_fused(depth, patches, cotangent, ends, length, w_qkv, w_out, w_up, w_down, vectors):
    rows, width = patches.shape
    share = w_out.shape[0]
    tall = w_down.shape[0]
    bf16, f32 = jnp.bfloat16, jnp.float32
    slab = 2 * share
    lanes4 = 2 * PAIR
    groups = width // lanes4
    units = w_up.shape[1] // width
    slots = groups + 1 + units
    blocks = slots + units
    half = width // 2
    tiles = SHORT_DEV // TILE
    vmem = lambda shape, kind: pltpu.VMEM(shape, kind)
    dma = pltpu.SemaphoreType.DMA
    copies = depth + 3
    scratch = [
        vmem((blocks + 2, 2, 4, depth, slab, half), bf16),
        vmem((2, 4, depth, 16, 128), bf16),
        vmem((16, 128), f32),
        vmem((slots, share, half), f32),
        vmem((slots, slab, half), f32),
        vmem((2 * tall, half), f32),
        vmem((16, width), f32),
        vmem((rows, 3 * width), bf16),
        vmem((width, rows), bf16),
        vmem((rows, width), f32),
        vmem((rows, width), bf16),
        vmem((rows, width), bf16),
        vmem((rows, width), bf16),
        vmem((rows, width), f32),
        vmem((rows, width), f32),
        vmem((rows, width), bf16),
        vmem((4, LONG_DEV, 2 * width), bf16),
        vmem((3, LONG_DEV, 2 * width), bf16),
        vmem((tiles + 2, width // PAIR, 1, 2 * TILE), f32),
        vmem((SHORT_DEV, TILE), f32),
        vmem((tiles, 1, TILE), f32),
        vmem((lanes4, SHORT_DEV), bf16),
        vmem((width, rows), bf16),
        vmem((width, width), bf16),
        vmem((width, width), bf16),
        vmem((rows // 2, 4 * PAIR), f32),
        vmem((blocks, 2, depth, slab, half), bf16),
        vmem((blocks, depth, slab, half), bf16),
        vmem((blocks, depth - 1, slab, half), bf16),
        vmem((depth - 1, depth, slab, half), bf16),
        vmem((slots * share + tall, width), f32),
        vmem((slab, half), f32),
        vmem((16, width), f32),
        vmem((4, 8, width), f32),
        vmem((4, 16, width), f32),
        vmem((3, 16, width), f32),
        vmem((depth, 16, width), f32),
        vmem((2, 8, 128), f32),
        vmem((8, 8, 128), f32),
        vmem((depth, 8, 128), f32),
    ]
    scratch += [dma((3,))] * 2 + [dma((blocks, copies))] * 2 + [dma((1, copies))] * 2
    scratch += [dma((groups, 3))] * 2 + [dma((3,))] * 2 + [dma((blocks, 4 + depth))] * 2
    scratch += [dma((1, 3 + depth))] * 2 + [dma((depth + 6,))] * 2 + [dma((3,))]
    in_vmem = pl.BlockSpec(memory_space=pltpu.VMEM)
    in_smem = pl.BlockSpec(memory_space=pltpu.SMEM)
    anywhere = pl.BlockSpec(memory_space=pl.ANY)
    return pl.pallas_call(
        functools.partial(fused_kernel, depth),
        out_shape=[
            jax.ShapeDtypeStruct((rows, width), bf16),
            jax.ShapeDtypeStruct((rows, width), f32),
            jax.ShapeDtypeStruct(w_qkv.shape, f32),
            jax.ShapeDtypeStruct(w_out.shape, f32),
            jax.ShapeDtypeStruct(w_up.shape, f32),
            jax.ShapeDtypeStruct(w_down.shape, f32),
            jax.ShapeDtypeStruct((16, 128), f32),
            jax.ShapeDtypeStruct((8, 128), f32),
        ],
        in_specs=[in_smem] * 2 + [in_vmem] * 5 + [anywhere] * 2,
        out_specs=[anywhere] * 2 + [in_vmem] * 6,
        scratch_shapes=scratch,
        compiler_params=pltpu.CompilerParams(
            vmem_limit_bytes=FUSED_VMEM, collective_id=0, has_side_effects=True
        ),
    )(ends, length, w_qkv, w_out, w_up, w_down, vectors, patches, cotangent)


def adamw_kernel(*refs):
    out_in, grad_in, norm_ref, out_out, grad_out, total_ref = *refs[:3], *refs[23:26]
    sources = [refs[3 + 5 * kind : 8 + 5 * kind] for kind in range(4)]
    targets = [refs[26 + 5 * kind : 31 + 5 * kind] for kind in range(4)]
    through, sems = refs[46:48], refs[48]
    loads, stores = [], []
    for place, (source, target) in enumerate(((out_in, out_out), (grad_in, grad_out))):
        loads.append(pltpu.make_async_copy(source, through[place], sems.at[place]))
        stores.append(pltpu.make_async_copy(through[place], target, sems.at[2 + place]))
    for load in loads:
        load.start()
    total_ref[...] = norm_ref[0:1, 0:1]
    factor = 1.0 / jnp.maximum(norm_ref[0:1, 0:1], 1.0)
    for load, store in zip(loads, stores):
        load.wait()
        store.start()
    for place in range(5):
        weight, first, second, gradient = (source[place] for source in sources)
        rate, decay = (rate_vector, 0.0) if place == 4 else (rate_matrix, decay_weight)
        lines, columns = weight.shape
        new = adamw_step(
            weight[...], gradient[:lines, :columns] * factor, first[...], second[...], rate, decay
        )
        for target, value in zip(targets, (*new, new[0])):
            target[place][...] = value.astype(target[place].dtype)
    for store in stores:
        store.wait()


def run_adamw(result, input_grad, norm, weights, firsts, seconds, gradients):
    f32 = jnp.float32
    outs = [jax.ShapeDtypeStruct(part.shape, part.dtype) for part in (result, input_grad)]
    outs.append(jax.ShapeDtypeStruct((1, 1), f32))
    for kind in (f32, f32, f32, jnp.bfloat16):
        outs += [jax.ShapeDtypeStruct(part.shape, kind) for part in weights]
    in_vmem, anywhere = pl.BlockSpec(memory_space=pltpu.VMEM), pl.BlockSpec(memory_space=pl.ANY)
    found = pl.pallas_call(
        adamw_kernel,
        out_shape=outs,
        in_specs=[anywhere] * 2 + [in_vmem] * 21,
        out_specs=[anywhere] * 2 + [in_vmem] * 21,
        scratch_shapes=[
            pltpu.VMEM(result.shape, result.dtype),
            pltpu.VMEM(input_grad.shape, input_grad.dtype),
            pltpu.SemaphoreType.DMA((4,)),
        ],
        compiler_params=pltpu.CompilerParams(vmem_limit_bytes=VMEM_MOST),
    )(result, input_grad, norm, *weights, *firsts, *seconds, *gradients)
    return found[0], found[1], found[2].reshape(()), *found[3:]


def adamw_step(weight, gradient, first_moment, second_moment, rate, decay):
    first_new = beta_first * first_moment + (1.0 - beta_first) * gradient
    second_new = beta_second * second_moment + (1.0 - beta_second) * gradient * gradient
    first_hat = first_new / (1.0 - beta_first**STEP)
    second_hat = second_new / (1.0 - beta_second**STEP)
    weight_new = weight - rate * (first_hat / (jnp.sqrt(second_hat) + eps_adam) + decay * weight)
    return (weight_new, first_new, second_new)


def gather_parameters(weights, vectors):
    low = [w.astype(jnp.bfloat16) for w in weights] + [vectors.astype(jnp.bfloat16)]
    flat = jnp.concatenate([part.reshape(-1) for part in low])
    flat = jnp.pad(flat, (0, -flat.size % 4096)).reshape(-1, 128)
    whole = lax.all_gather(flat, ("dp", "blk"), axis=0, tiled=True)
    whole = whole.reshape(-1, flat.size)
    found, at = [], 0
    for part in low[:-1]:
        piece = whole[:, at : at + part.size]
        found.append(piece.reshape(-1, part.shape[1]))
        at += part.size
    piece = whole[:, at : at + vectors.size].reshape(-1, *vectors.shape)
    found.append(piece.transpose(1, 0, 2).reshape(vectors.shape[0], -1))
    return found


def layer_by_parts(
    patches, cotangent, short_lengths, long_lengths, w_qkv, w_out, w_up, w_down, vectors
):
    rows, width = patches.shape
    bf16, f32 = jnp.bfloat16, jnp.float32
    full_qkv, full_out, full_up, full_down, full_vec = gather_parameters(
        (w_qkv, w_out, w_up, w_down), vectors
    )
    params = full_vec.astype(f32)

    hidden_one, projected = call(
        qkv_phase, [((rows, width), bf16), ((rows, 3 * width), bf16)]
    )(patches, params, full_qkv)
    far = lax.all_gather(projected[SHORT_DEV:, width:], "blk", axis=0, tiled=True)
    tiles, pairs = SHORT_DEV // TILE, width // PAIR
    marks = [pltpu.VMEM((SHORT_DEV, TILE), f32), pltpu.VMEM((tiles, 1, TILE), f32)]
    attended, lse, middle, hidden_two = call(
        forward_kernel,
        [
            ((rows, width), bf16),
            ((tiles + 1, pairs, 1, 2 * TILE), f32),
            ((rows, width), f32),
            ((rows, width), bf16),
        ],
        scratch=marks,
        smem=(0, 1),
    )(short_lengths, long_lengths, patches, params, projected, far, full_out)

    long_place = lax.axis_index("blk") * LONG_DEV + jnp.arange(LONG_DEV, dtype=jnp.int32)
    keep = jnp.concatenate([jnp.ones((SHORT_DEV,), bool), long_place < long_lengths[0]])
    grad_low = jnp.where(keep[:, None], cotangent, jnp.zeros_like(cotangent))
    blocks = full_up.shape[1] // width
    result, grad_hidden_two, grad_up, grad_down, grad_bias_up = run_mlp(
        hidden_two, grad_low, middle, full_up, full_down,
        params[8 : 8 + blocks].reshape(blocks, 1, width), params[7:8],
    )
    scatter = functools.partial(
        lax.psum_scatter, axis_name=("dp", "blk"), scatter_dimension=0, tiled=True
    )
    red_up = scatter(grad_up)
    red_down = scatter(grad_down)

    grad_middle, grad_att, sums_two, grad_out = call(
        middle_back_kernel,
        [
            ((rows, width), f32),
            ((rows, width), bf16),
            ((4, width), f32),
            ((width, width), f32),
        ],
        scratch=[pltpu.VMEM((rows, width), bf16)],
    )(grad_low, middle, grad_hidden_two, params, full_out, attended)
    red_out = scatter(grad_out)

    mixed, far_grad = call(
        attention_back_kernel,
        [((rows, 3 * width), bf16), ((far.shape[0], 2 * width), bf16)],
        scratch=marks + [pltpu.VMEM((SHORT_DEV, 2 * PAIR), f32)] * 2,
        smem=(0, 1),
    )(short_lengths, long_lengths, projected, far, lse, grad_att)
    near = lax.psum_scatter(far_grad, "blk", scatter_dimension=0, tiled=True)
    input_grad, grad_qkv, sums_one = call(
        input_back_kernel,
        [((rows, width), f32), ((width, 3 * width), f32), ((4, width), f32)],
        scratch=[pltpu.VMEM((rows, 3 * width), bf16)],
    )(patches, hidden_one, mixed, near, params, full_qkv, grad_middle)
    red_qkv = scatter(grad_qkv)

    grad_vec = jnp.concatenate(
        [sums_one[0:2], sums_two[0:2], sums_one[2:4], sums_two[2:4], grad_bias_up.reshape(-1, width)], 0
    )
    red_vec = lax.psum_scatter(grad_vec, ("dp", "blk"), scatter_dimension=1, tiled=True)
    reduced = (red_qkv, red_out, red_up, red_down, red_vec)
    grad_norm = jnp.sqrt(
        lax.psum(sum(jnp.sum(part * part) for part in reduced), ("dp", "blk"))
    )
    return result, input_grad, grad_norm, reduced


def fits_one(patches, w_out):
    dp, blk = lax.axis_size("dp"), lax.axis_size("blk")
    share, width = w_out.shape
    return blk == 4 and dp % 2 == 0 and 2 * share % 16 == 0 and dp * blk * share == width


def per_device(
    patches, cotangent, short_lengths, long_lengths,
    w_qkv, w_out, w_up, w_down, vectors,
    first_qkv, first_out, first_up, first_down, first_vectors,
    second_qkv, second_out, second_up, second_down, second_vectors,
):
    layer = (patches, cotangent, short_lengths, long_lengths)
    weights = (w_qkv, w_out, w_up, w_down, vectors)
    if fits_one(patches, w_out):
        depth = lax.axis_size("dp") // 2
        result, input_grad, *gradients, norm = run_fused(depth, *layer, *weights)
    else:
        result, input_grad, grad_norm, gradients = layer_by_parts(*layer, *weights)
        norm = jnp.broadcast_to(grad_norm, (8, 128))
    firsts = (first_qkv, first_out, first_up, first_down, first_vectors)
    seconds = (second_qkv, second_out, second_up, second_down, second_vectors)
    return run_adamw(result, input_grad, norm, weights, firsts, seconds, gradients)


def solution(mesh):
    rows = P(("dp", "blk"), None)
    columns = P(None, ("dp", "blk"))
    group = (rows,) * 4 + (columns,)
    return jax.shard_map(
        per_device,
        mesh=mesh,
        in_specs=(rows, rows, rows, P("dp")) + group * 3,
        out_specs=(rows, rows, P()) + group * 4,
        check_vma=False,
    )
```

```python
import functools

import jax
import jax.numpy as jnp
from jax import lax
from jax.experimental import pallas as pl
from jax.experimental.pallas import tpu as pltpu
from jax.sharding import PartitionSpec as P

HD = 64
SHORT_DEV = 896
LONG_DEV = 128
STEP = 10
TILE = 128
BAND = 3 * TILE
PAIR = 2 * HD
ROWS = 256
CHUNK = 32

eps_norm = 1e-06
far_below = -1000000000.0
rate_matrix = 0.04
rate_vector = 0.5
beta_first = 0.5
beta_second = 0.5
eps_adam = 1e-08
decay_weight = 0.01
score_scale = HD ** (-0.5)
gelu_root = 0.7978845608028654
gelu_cube = 0.044715
VMEM_MOST = 60 * 1024 * 1024
FUSED_VMEM = 63 * 1024 * 1024


def dot(left, right):
    return lax.dot_general(left, right, (((1,), (0,)), ((), ())), preferred_element_type=jnp.float32)


def dot_tr(left, right):
    return lax.dot_general(left, right, (((1,), (1,)), ((), ())), preferred_element_type=jnp.float32)


def dot_tl(left, right):
    return lax.dot_general(left, right, (((0,), (0,)), ((), ())), preferred_element_type=jnp.float32)


def standardize(values):
    centered = values - jnp.mean(values, -1, keepdims=True)
    inv_std = lax.rsqrt(jnp.mean(centered * centered, -1, keepdims=True) + eps_norm)
    return centered * inv_std, inv_std


def norm_back(upstream, standard, inv_std, gain):
    scaled = upstream * gain
    inner = (
        scaled
        - jnp.mean(scaled, -1, keepdims=True)
        - standard * jnp.mean(scaled * standard, -1, keepdims=True)
    )
    return inner * inv_std


def column_sum(values):
    return jnp.sum(values, 0, keepdims=True)


def rows_at(step):
    return pl.ds(pl.multiple_of(step * ROWS, ROWS), ROWS)


def qkv_phase(x_ref, vec_ref, w_ref, h1_ref, qkv_ref):
    width = x_ref.shape[1]

    @pl.loop(0, x_ref.shape[0] // ROWS)
    def _(step):
        here = rows_at(step)
        unit, _ = standardize(x_ref[here, :].astype(jnp.float32))
        hidden = (unit * vec_ref[0:1, :] + vec_ref[1:2, :]).astype(jnp.bfloat16)
        h1_ref[here, :] = hidden
        for part, bias in ((0, 4), (1, None), (2, 5)):
            columns = slice(part * width, (part + 1) * width)
            made = dot(hidden, w_ref[:, columns])
            if bias is not None:
                made = made + vec_ref[bias : bias + 1, :]
            qkv_ref[here, columns] = made.astype(jnp.bfloat16)


def stack_heads(values, scale):
    lane = lax.broadcasted_iota(jnp.int32, values.shape, 1)
    if scale is not None:
        values = values * jnp.asarray(scale, values.dtype)
    zero = jnp.zeros_like(values)
    return jnp.concatenate(
        [jnp.where(lane < HD, values, zero), jnp.where(lane < HD, zero, values)], 0
    )


def unstack_heads(values):
    return jnp.concatenate([values[:HD, :TILE], values[HD:, TILE:]], 0)


def softmax_of(scores, allowed):
    scores = jnp.where(allowed, scores, far_below)
    top = jnp.max(scores, 0, keepdims=True)
    exponent = jnp.exp(scores - top)
    total = jnp.sum(exponent, 0, keepdims=True)
    return (exponent * (1.0 / total)).astype(jnp.bfloat16), top + jnp.log(total)


def attend_forward(queries, keys, values_tr, allowed):
    probs, log_total = softmax_of(dot_tr(keys, stack_heads(queries, score_scale)), allowed)
    return unstack_heads(dot(values_tr, probs)).astype(jnp.bfloat16), log_total


def softmax_back(scores, allowed, log_total, grad_probs):
    probs = jnp.exp(jnp.where(allowed, scores, far_below) - log_total)
    delta = jnp.sum(probs * grad_probs, 0, keepdims=True)
    grad_scores = (probs * (grad_probs - delta)).astype(jnp.bfloat16)
    return probs.astype(jnp.bfloat16), grad_scores


def attend_back(queries, keys, keys_tr, values, allowed, log_total, upstream):
    stacked_q = stack_heads(queries, score_scale)
    stacked_up = stack_heads(upstream, None)
    probs, grad_scores = softmax_back(
        dot_tr(keys, stacked_q), allowed, log_total, dot_tr(values, stacked_up)
    )
    grad_keys = dot(grad_scores, stacked_q)
    grad_values = dot(probs, stacked_up)
    grad_queries = unstack_heads(dot(keys_tr, grad_scores)) * score_scale
    return grad_queries.astype(jnp.bfloat16).T, grad_keys, grad_values


def mark_segments(ends_ref, key_seg, query_seg):
    count = ends_ref.shape[1]
    for tile in range(SHORT_DEV // TILE):
        rows = lax.broadcasted_iota(jnp.int32, (TILE, TILE), 0) + tile * TILE
        lanes = lax.broadcasted_iota(jnp.int32, (1, TILE), 1) + tile * TILE
        by_row = jnp.zeros((TILE, TILE), jnp.float32)
        by_lane = jnp.zeros((1, TILE), jnp.float32)
        end = jnp.int32(0)
        for clip in range(count):
            end = end + ends_ref[0, clip]
            by_row = by_row + jnp.where(rows >= end, 1.0, 0.0)
            by_lane = by_lane + jnp.where(lanes >= end, 1.0, 0.0)
        key_seg[tile * TILE : (tile + 1) * TILE, :] = by_row
        query_seg[tile] = by_lane


def band_start(tile):
    most = SHORT_DEV - BAND
    return pl.multiple_of(jnp.clip((tile - 1) * TILE, 0, most), TILE)


def pair_lanes(pair, offset=0):
    return pl.ds(pl.multiple_of(offset + pair * PAIR, PAIR), PAIR)


def short_mask(tile, key_seg, query_seg):
    band = key_seg[pl.ds(band_start(tile), BAND), :]
    line = query_seg[tile]
    return jnp.concatenate([band, band], 1) == jnp.concatenate([line, line], 1)


def long_mask(length_ref, keys):
    place = lax.broadcasted_iota(jnp.int32, (keys, 2 * TILE), 0)
    return place < length_ref[0]


def attention_forward_phase(qkv_ref, far_ref, length_ref, key_seg, query_seg, out_ref, lse_ref):
    width = out_ref.shape[1]
    pairs = width // PAIR
    tiles = SHORT_DEV // TILE

    @pl.loop(0, tiles)
    def _(tile):
        rows = pl.ds(pl.multiple_of(tile * TILE, TILE), TILE)
        band = pl.ds(band_start(tile), BAND)
        allowed = short_mask(tile, key_seg, query_seg)
        for pair in range(pairs):
            made, lse = attend_forward(
                qkv_ref[rows, pair * PAIR : (pair + 1) * PAIR],
                qkv_ref[band, width + pair * PAIR : width + (pair + 1) * PAIR],
                qkv_ref[band, 2 * width + pair * PAIR : 2 * width + (pair + 1) * PAIR].T,
                allowed,
            )
            out_ref[rows, pair * PAIR : (pair + 1) * PAIR] = made.T
            lse_ref[tile, pair] = lse

    @pl.loop(0, pairs)
    def _(pair):
        allowed = long_mask(length_ref, far_ref.shape[0])
        made, lse = attend_forward(
            qkv_ref[SHORT_DEV:, pair_lanes(pair)],
            far_ref[:, pair_lanes(pair)],
            far_ref[:, pair_lanes(pair, width)].T,
            allowed,
        )
        out_ref[SHORT_DEV:, pair_lanes(pair)] = made.T
        lse_ref[tiles, pair] = lse


def attention_back_long(qkv_ref, far_ref, length_ref, lse_ref, up_ref, dqkv_ref, far_grad):
    width = up_ref.shape[1]
    tiles = SHORT_DEV // TILE

    @pl.loop(0, width // PAIR)
    def _(pair):
        allowed = long_mask(length_ref, far_ref.shape[0])
        dq, dk, dv = attend_back(
            qkv_ref[SHORT_DEV:, pair_lanes(pair)],
            far_ref[:, pair_lanes(pair)],
            far_ref[:, pair_lanes(pair)].T,
            far_ref[:, pair_lanes(pair, width)],
            allowed,
            lse_ref[tiles, pair],
            up_ref[SHORT_DEV:, pair_lanes(pair)],
        )
        dqkv_ref[SHORT_DEV:, pair_lanes(pair)] = dq
        far_grad[:, pair_lanes(pair)] = dk.astype(jnp.bfloat16)
        far_grad[:, pair_lanes(pair, width)] = dv.astype(jnp.bfloat16)


def attention_back_short(qkv_ref, key_seg, query_seg, lse_ref, up_ref, dqkv_ref, dk_acc, dv_acc):
    width = up_ref.shape[1]
    tiles = SHORT_DEV // TILE

    @pl.loop(0, width // (2 * PAIR))
    def _(group):
        dk_acc[...] = jnp.zeros_like(dk_acc)
        dv_acc[...] = jnp.zeros_like(dv_acc)

        @pl.loop(0, tiles)
        def _(tile):
            rows = pl.ds(pl.multiple_of(tile * TILE, TILE), TILE)
            band = pl.ds(band_start(tile), BAND)
            allowed = short_mask(tile, key_seg, query_seg)
            for half in range(2):
                pair = group * 2 + half
                dq, dk, dv = attend_back(
                    qkv_ref[rows, pair_lanes(pair)],
                    qkv_ref[band, pair_lanes(pair, width)],
                    qkv_ref[band, pair_lanes(pair, width)].T,
                    qkv_ref[band, pair_lanes(pair, 2 * width)],
                    allowed,
                    lse_ref[tile, pair],
                    up_ref[rows, pair_lanes(pair)],
                )
                dqkv_ref[rows, pair_lanes(pair)] = dq
                own = slice(half * PAIR, (half + 1) * PAIR)
                dk_acc[band, own] += dk
                dv_acc[band, own] += dv

        lanes = 2 * PAIR
        k_at = pl.ds(pl.multiple_of(width + group * lanes, lanes), lanes)
        v_at = pl.ds(pl.multiple_of(2 * width + group * lanes, lanes), lanes)
        dqkv_ref[:SHORT_DEV, k_at] = dk_acc[...].astype(jnp.bfloat16)
        dqkv_ref[:SHORT_DEV, v_at] = dv_acc[...].astype(jnp.bfloat16)


def middle_phase(x_ref, vec_ref, w_ref, att_ref, middle_ref, h2_ref):
    @pl.loop(0, x_ref.shape[0] // ROWS)
    def _(step):
        here = rows_at(step)
        made = dot(att_ref[here, :], w_ref[...]) + vec_ref[6:7, :]
        middle = x_ref[here, :].astype(jnp.float32) + made
        middle_ref[here, :] = middle
        unit, _ = standardize(middle)
        h2_ref[here, :] = (unit * vec_ref[2:3, :] + vec_ref[3:4, :]).astype(jnp.bfloat16)


def gelu_both(values):
    square = values * values
    inner = values * (gelu_root + (gelu_root * gelu_cube) * square)
    bent = jnp.tanh(inner)
    half_up = 0.5 + 0.5 * bent
    slope = half_up + (0.5 * values) * (1.0 - bent * bent) * (
        gelu_root + (3.0 * gelu_root * gelu_cube) * square
    )
    return values * half_up, slope


def mlp_rows(h2_ref, dy_ref, up_ref, down_ref, bias, act_ref, du_ref, out_acc, dh2_acc, first):
    def body(step, total):
        here = rows_at(step)
        pre = dot(h2_ref[here, :], up_ref[...]) + bias
        grad_act = dot_tr(dy_ref[here, :], down_ref[...])
        act, slope = gelu_both(pre)
        act_low = act.astype(jnp.bfloat16)
        du_low = (grad_act * slope).astype(jnp.bfloat16)
        act_ref[here, :] = act_low
        du_ref[here, :] = du_low
        made = dot(act_low, down_ref[...])
        grad_hidden = dot_tr(du_low, up_ref[...])
        if first is True:
            out_acc[here, :] = made
            dh2_acc[here, :] = grad_hidden
        else:
            out_acc[here, :] += made
            dh2_acc[here, :] += grad_hidden
        return total + column_sum(du_low.astype(jnp.float32))

    width = up_ref.shape[1]
    return lax.fori_loop(0, h2_ref.shape[0] // ROWS, body, jnp.zeros((1, width), jnp.float32))


def middle_back_phase(
    dy_ref, middle_ref, dh2_ref, vec_ref, w_ref, dmiddle_ref, da_ref, datt_ref, gvec_ref
):
    def body(step, totals):
        here = rows_at(step)
        dy_low = dy_ref[here, :].astype(jnp.float32)
        dh2 = dh2_ref[here, :]
        unit, inv_std = standardize(middle_ref[here, :])
        dmiddle = dy_low + norm_back(dh2, unit, inv_std, vec_ref[2:3, :])
        dmiddle_ref[here, :] = dmiddle
        da = dmiddle.astype(jnp.bfloat16)
        da_ref[here, :] = da
        datt_ref[here, :] = dot_tr(da, w_ref[...]).astype(jnp.bfloat16)
        return (
            totals[0] + column_sum(dh2 * unit),
            totals[1] + column_sum(dh2),
            totals[2] + column_sum(da.astype(jnp.float32)),
            totals[3] + column_sum(dy_low),
        )

    zero = jnp.zeros((1, dy_ref.shape[1]), jnp.float32)
    totals = lax.fori_loop(0, dy_ref.shape[0] // ROWS, body, (zero,) * 4)
    for place in range(4):
        gvec_ref[place : place + 1, :] = totals[place]


def input_back_phase(x_ref, dqkv_ref, vec_ref, w_ref, dmiddle_ref, grad_ref, gvec_ref):
    width = x_ref.shape[1]

    def body(step, totals):
        here = rows_at(step)
        dh1 = dot_tr(dqkv_ref[here, :], w_ref[...])
        unit, inv_std = standardize(x_ref[here, :].astype(jnp.float32))
        grad_ref[here, :] = dmiddle_ref[here, :] + norm_back(dh1, unit, inv_std, vec_ref[0:1, :])
        return (
            totals[0] + column_sum(dh1 * unit),
            totals[1] + column_sum(dh1),
            totals[2] + column_sum(dqkv_ref[here, :width].astype(jnp.float32)),
            totals[3] + column_sum(dqkv_ref[here, 2 * width :].astype(jnp.float32)),
        )

    zero = jnp.zeros((1, width), jnp.float32)
    totals = lax.fori_loop(0, x_ref.shape[0] // ROWS, body, (zero,) * 4)
    for place in range(4):
        gvec_ref[place : place + 1, :] = totals[place]


def call(body, outs, scratch=(), smem=()):
    def run(*arrays):
        specs = [
            pl.BlockSpec(memory_space=pltpu.SMEM if place in smem else pltpu.VMEM)
            for place in range(len(arrays))
        ]
        return pl.pallas_call(
            body,
            out_shape=[jax.ShapeDtypeStruct(shape, kind) for shape, kind in outs],
            in_specs=specs,
            out_specs=[pl.BlockSpec(memory_space=pltpu.VMEM)] * len(outs),
            scratch_shapes=list(scratch),
            compiler_params=pltpu.CompilerParams(vmem_limit_bytes=VMEM_MOST),
        )(*arrays)

    return run


def forward_kernel(
    ends_ref, length_ref, x_ref, vec_ref, qkv_ref, far_ref, w_ref,
    att_ref, lse_ref, middle_ref, h2_ref, key_seg, query_seg,
):
    mark_segments(ends_ref, key_seg, query_seg)
    attention_forward_phase(qkv_ref, far_ref, length_ref, key_seg, query_seg, att_ref, lse_ref)
    middle_phase(x_ref, vec_ref, w_ref, att_ref, middle_ref, h2_ref)


def mlp_kernel(
    h2_ref, dy_ref, middle_ref, up_ref, down_ref, bias_ref, last_ref,
    out_ref, dh2_ref, gup_ref, gdown_ref, gbu_ref, act_ref, du_ref, out_acc,
):
    block = pl.program_id(0)

    @pl.when(block == 0)
    def _():
        out_acc[...] = jnp.zeros_like(out_acc)
        dh2_ref[...] = jnp.zeros_like(dh2_ref)

    gbu_ref[0] = mlp_rows(
        h2_ref, dy_ref, up_ref, down_ref, bias_ref[0], act_ref, du_ref, out_acc, dh2_ref, None
    )
    gup_ref[...] = dot_tl(h2_ref[...], du_ref[...])
    gdown_ref[...] = dot_tl(act_ref[...], dy_ref[...])

    @pl.when(block == pl.num_programs(0) - 1)
    def _():
        out_ref[...] = (middle_ref[...] + (out_acc[...] + last_ref[...])).astype(jnp.bfloat16)


def run_mlp(h2, dy, middle, w_up, w_down, bias_up, bias_down):
    rows, width = h2.shape
    units = w_up.shape[1]
    blocks = units // width
    whole = lambda shape: pl.BlockSpec(shape, lambda b: (0, 0))
    return pl.pallas_call(
        mlp_kernel,
        grid=(blocks,),
        out_shape=[
            jax.ShapeDtypeStruct((rows, width), jnp.bfloat16),
            jax.ShapeDtypeStruct((rows, width), jnp.float32),
            jax.ShapeDtypeStruct((width, units), jnp.float32),
            jax.ShapeDtypeStruct((units, width), jnp.float32),
            jax.ShapeDtypeStruct((blocks, 1, width), jnp.float32),
        ],
        in_specs=[
            whole((rows, width)),
            whole((rows, width)),
            whole((rows, width)),
            pl.BlockSpec((width, width), lambda b: (0, b)),
            pl.BlockSpec((width, width), lambda b: (b, 0)),
            pl.BlockSpec((1, 1, width), lambda b: (b, 0, 0)),
            whole((1, width)),
        ],
        out_specs=[
            whole((rows, width)),
            whole((rows, width)),
            pl.BlockSpec((width, width), lambda b: (0, b)),
            pl.BlockSpec((width, width), lambda b: (b, 0)),
            pl.BlockSpec((1, 1, width), lambda b: (b, 0, 0)),
        ],
        scratch_shapes=[
            pltpu.VMEM((rows, width), jnp.bfloat16),
            pltpu.VMEM((rows, width), jnp.bfloat16),
            pltpu.VMEM((rows, width), jnp.float32),
        ],
        compiler_params=pltpu.CompilerParams(vmem_limit_bytes=VMEM_MOST),
    )(h2, dy, middle, w_up, w_down, bias_up, bias_down)


def middle_back_kernel(
    dy_ref, middle_ref, dh2_ref, vec_ref, w_ref, att_ref,
    dmiddle_ref, datt_ref, gvec_ref, gout_ref, da_ref,
):
    middle_back_phase(
        dy_ref, middle_ref, dh2_ref, vec_ref, w_ref, dmiddle_ref, da_ref, datt_ref, gvec_ref
    )
    gout_ref[...] = dot_tl(att_ref[...], da_ref[...])


def attention_back_kernel(
    ends_ref, length_ref, qkv_ref, far_ref, lse_ref, datt_ref,
    dqkv_ref, far_grad, key_seg, query_seg, dk_acc, dv_acc,
):
    mark_segments(ends_ref, key_seg, query_seg)
    attention_back_long(qkv_ref, far_ref, length_ref, lse_ref, datt_ref, dqkv_ref, far_grad)
    width = datt_ref.shape[1]
    dqkv_ref[SHORT_DEV:, width:] = jnp.zeros((LONG_DEV, 2 * width), jnp.bfloat16)
    attention_back_short(
        qkv_ref, key_seg, query_seg, lse_ref, datt_ref, dqkv_ref, dk_acc, dv_acc
    )


def input_back_kernel(
    x_ref, h1_ref, dqkv_ref, near_ref, vec_ref, w_ref, dmiddle_ref,
    grad_ref, gqkv_ref, gvec_ref, mixed_ref,
):
    width = x_ref.shape[1]
    mixed_ref[...] = dqkv_ref[...]
    mixed_ref[SHORT_DEV:, width:] = near_ref[...]
    input_back_phase(x_ref, mixed_ref, vec_ref, w_ref, dmiddle_ref, grad_ref, gvec_ref)
    for part in range(3):
        columns = slice(part * width, (part + 1) * width)
        gqkv_ref[:, columns] = dot_tl(h1_ref[...], mixed_ref[:, columns])


def when(condition, body):
    if isinstance(condition, bool):
        if condition:
            body()
    else:
        pl.when(condition)(body)


def both(left, right):
    if isinstance(left, bool) and isinstance(right, bool):
        return left and right
    return jnp.logical_and(left, right)


def fold(values):
    return jnp.sum(values.reshape(-1, 8, values.shape[1]), 0)


def chunks_of(count, size):
    return [slice(start, start + size) for start in range(0, count, size)]


def softmax_into(scores, allowed_at, probs):
    parts = chunks_of(scores.shape[0], 64)
    top = None
    for part in parts:
        value = jnp.where(allowed_at(part), scores[part, :], far_below)
        scores[part, :] = value
        high = jnp.max(value.reshape(-1, 8, value.shape[1]), 0)
        top = high if top is None else jnp.maximum(top, high)
    top = jnp.max(top, 0, keepdims=True)
    total = None
    for part in parts:
        value = jnp.exp(scores[part, :] - top)
        scores[part, :] = value
        total = fold(value) if total is None else total + fold(value)
    total = jnp.sum(total, 0, keepdims=True)
    scale = 1.0 / total
    for part in parts:
        probs[part, :] = (scores[part, :] * scale).astype(jnp.bfloat16)
    return top + jnp.log(total)


def softmax_back_into(scores, grad_probs, allowed_at, log_total, probs, grad_scores):
    parts = chunks_of(scores.shape[0], 32)
    delta = None
    for part in parts:
        value = jnp.exp(jnp.where(allowed_at(part), scores[part, :], far_below) - log_total)
        scores[part, :] = value
        probs[part, :] = value.astype(jnp.bfloat16)
        share = fold(value * grad_probs[part, :])
        delta = share if delta is None else delta + share
    delta = jnp.sum(delta, 0, keepdims=True)
    for part in parts:
        grad = scores[part, :] * (grad_probs[part, :] - delta)
        grad_scores[part, :] = grad.astype(jnp.bfloat16)


class Places:
    def __init__(self, depth):
        self.depth = depth
        dp, blk = lax.axis_index("dp"), lax.axis_index("blk")
        self.dp, self.blk = dp, blk
        z, x, y, c = dp // 2, lax.rem(dp, 2), blk // 2, lax.rem(blk, 2)
        self.z, self.x, self.y, self.c = z, x, y, c
        flip = lambda value, by: lax.rem(value + by, 2)
        self.core = (dp, y * 2 + 1 - c)
        self.x_peer = (z * 2 + 1 - x, blk)
        self.y_peer = (dp, (1 - y) * 2 + c)
        self.first = (z * 2 + flip(x, 1 - c), flip(y, c) * 2 + c)
        self.second = (z * 2 + flip(x, c), flip(y, 1 - c) * 2 + c)
        self.corner = x * 4 + blk
        self.s, self.f = jnp.where(c == 0, y, x), jnp.where(c == 0, x, y)
        self.own = self.s * 2 + self.f
        self.at_first = self.s * 2 + 1 - self.f
        self.near_two = pl.ds(2 * self.s, 2)
        self.far_two = pl.ds(2 - 2 * self.s, 2)
        self.core_near_two = pl.ds(2 * self.f, 2)
        self.core_far_two = pl.ds(2 - 2 * self.f, 2)

    def z_peer(self, step):
        return (lax.rem(self.z + step, self.depth) * 2 + self.x, self.blk)

    def z_from(self, step):
        return lax.rem(self.z - step + self.depth, self.depth)

    def z_to(self, step):
        return lax.rem(self.z + step, self.depth)

    def plane_from(self, step):
        return lax.rem(self.corner - step + 8, 8)

    def plane_peer(self, step):
        corner = lax.rem(self.corner + step, 8)
        return (self.z * 2 + corner // 4, lax.rem(corner, 4))


def remote(source, target, sends, recvs, device):
    return pltpu.make_async_remote_copy(
        src_ref=source,
        dst_ref=target,
        send_sem=sends,
        recv_sem=recvs,
        device_id=device,
        device_id_type=pl.DeviceIdType.MESH,
    )


class Gather:
    def __init__(self, at, pieces, sends, recvs, plane=None):
        self.at, self.pieces, self.sends, self.recvs, self.plane = at, pieces, sends, recvs, plane
        self.near = at.depth - 1

    def along_z(self, block, step, whole, incoming):
        at = self.at
        source = at.z_from(step) if incoming else at.z
        region = self.pieces(block, None if whole else source, at.own, True)
        index = step - 1
        return remote(
            region, region, self.sends.at[block, index], self.recvs.at[block, index],
            at.z_peer(step),
        )

    def copy(self, block, kind, incoming=False):
        at = self.at
        device = (at.first, at.second, at.core, at.core)[kind]
        going = (at.own, at.near_two, at.near_two, at.far_two)
        coming = (at.at_first, at.far_two, at.core_near_two, at.core_far_two)
        place = (coming if incoming else going)[kind]
        region = self.pieces(block, None, place, not (incoming and kind >= 2))
        index = self.near + kind
        return remote(
            region, region, self.sends.at[block, index], self.recvs.at[block, index], device
        )

    def start(self, block, *kinds):
        for kind in kinds:
            self.copy(block, kind).start()

    def arrive(self, block, *kinds):
        for kind in kinds:
            self.copy(block, kind, True).wait_recv()

    def split(self, block, every, one):
        if self.plane is None:
            every()
            return
        single, z = self.plane(block)
        if isinstance(single, bool):
            one(z) if single else every()
            return
        pl.when(single)(lambda: one(z))
        pl.when(jnp.logical_not(single))(every)

    def push(self, block):
        def every():
            for step in range(1, self.at.depth):
                self.along_z(block, step, False, False).start()

        def one(z):
            @pl.when(self.at.z == z)
            def _():
                for step in range(1, self.at.depth):
                    self.along_z(block, step, True, False).start()

        self.split(block, every, one)

    def stage_two(self, block):
        def every():
            for step in range(1, self.at.depth):
                self.along_z(block, step, False, True).wait_recv()

        def one(z):
            @pl.when(self.at.z != z)
            def _():
                away = lax.rem(self.at.z - z + self.at.depth, self.at.depth)
                self.along_z(block, away, True, True).wait_recv()

        self.split(block, every, one)
        self.start(block, 0)

    def stage_three(self, block):
        self.arrive(block, 0)
        self.start(block, 1, 2)

    def stage_four(self, block):
        self.arrive(block, 1)
        self.start(block, 3)

    def finish(self, block):
        self.arrive(block, 2, 3)

    def sent(self, block):
        def every():
            for step in range(1, self.at.depth):
                self.along_z(block, step, False, False).wait_send()

        def one(z):
            @pl.when(self.at.z == z)
            def _():
                for step in range(1, self.at.depth):
                    self.along_z(block, step, True, False).wait_send()

        self.split(block, every, one)
        for kind in range(4):
            self.copy(block, kind).wait_send()


class Exchange:
    def __init__(self, at, sent, got, got_z, sends, recvs, slot):
        self.at, self.sent, self.got, self.got_z = at, sent, got, got_z
        self.sends, self.recvs, self.slot = sends, recvs, slot
        self.stage, self.copies, self.value = 0, [], None

    def copy(self, source, target, index, device):
        return remote(
            source, target, self.sends.at[self.slot, index], self.recvs.at[self.slot, index], device
        )

    def begin(self, value):
        at, stage = self.at, self.stage
        self.value = value
        self.sent[stage] = value
        peers = (at.core, at.x_peer, at.y_peer)
        if stage < 3:
            copy = self.copy(self.sent.at[stage], self.got.at[stage], stage, peers[stage])
            self.copies = [(copy, copy)]
        else:
            self.got_z[at.z] = value
            self.copies = []
            for step in range(1, at.depth):
                ends = [self.got_z.at[at.z], self.got_z.at[at.z_from(step)]]
                self.copies.append(
                    tuple(self.copy(self.sent.at[3], end, 2 + step, at.z_peer(step)) for end in ends)
                )
        for going, _ in self.copies:
            going.start()

    def step(self):
        for going, coming in self.copies:
            going.wait_send()
            coming.wait_recv()
        if self.stage < 3:
            value = self.value + self.got[self.stage]
            self.stage += 1
            self.begin(value)
            return None
        value = self.got_z[0]
        for place in range(1, self.at.depth):
            value = value + self.got_z[place]
        return value


class ShortExchange:
    def __init__(self, at, sent, got_z, got_plane, sends, recvs):
        self.at, self.sent, self.got_z, self.got_plane = at, sent, got_z, got_plane
        self.sends, self.recvs = sends, recvs

    def start(self, stage, landing, mine, value, others):
        self.sent[stage] = value
        landing[mine] = value
        copies = []
        for device, slot, index in others:
            ends = [landing.at[mine], landing.at[slot]]
            copies.append(
                tuple(
                    remote(self.sent.at[stage], end, self.sends.at[index], self.recvs.at[index], device)
                    for end in ends
                )
            )
        for going, _ in copies:
            going.start()
        return copies

    def finish(self, landing, copies):
        for going, coming in copies:
            going.wait_send()
            coming.wait_recv()
        value = landing[0]
        for place in range(1, landing.shape[0]):
            value = value + landing[place]
        return value

    def along_z(self, value):
        at = self.at
        others = [(at.z_peer(step), at.z_from(step), step - 1) for step in range(1, at.depth)]
        return self.start(0, self.got_z, at.z, value, others)

    def in_plane(self, value):
        at = self.at
        others = [
            (at.plane_peer(step), at.plane_from(step), at.depth - 2 + step) for step in range(1, 8)
        ]
        return self.start(1, self.got_plane, at.corner, value, others)


def fused_kernel(
    depth, ends_ref, length_ref, wqkv_ref, wout_ref, wup_ref, wdown_ref, vectors_ref, x_hbm, cot_hbm,
    out_hbm, grad_hbm, rqkv_ref, rout_ref, rup_ref, rdown_ref, rvec_ref, norm_ref,
    w, vbuf, vpad, give_out, asm, asm_down, vec, qkv, att, middle, h2, act, du, out_acc, dh2, dy,
    far, far_got, lse, key_seg, query_seg, turned, h2_tr, flat_up, flat_down, pre_grad,
    got_a, got_b, got_z, got_zd, red, squares, gvec, sums_two,
    v_sent, v_got, v_got_z, n_sent, n_got, n_got_z,
    swap_s, swap_r, ag_s, ag_r, vg_s, vg_r, kv_s, kv_r, fg_s, fg_r, rs_s, rs_r, ex_s, ex_r, no_s, no_r, local_s,
):
    bf16, f32 = jnp.bfloat16, jnp.float32
    at = Places(depth)
    rows, width = dy.shape
    spare = w.shape[0] - 2
    blocks = spare
    slab = w.shape[4]
    share = slab // 2
    half = width // 2
    lanes4 = 2 * PAIR
    groups = width // lanes4
    units = (blocks - groups - 1) // 2
    tiles = SHORT_DEV // TILE
    mine = pl.ds(pl.multiple_of(at.c * half, 128), half)
    other = pl.ds(pl.multiple_of((1 - at.c) * half, 128), half)
    my_rows = pl.ds(pl.multiple_of(at.c * share, 8), share)
    other_rows = pl.ds(pl.multiple_of((1 - at.c) * share, 8), share)
    tall = units * share
    my_tall = pl.ds(pl.multiple_of(at.c * tall, 8), tall)
    other_tall = pl.ds(pl.multiple_of((1 - at.c) * tall, 8), tall)
    wide = 2 * PAIR
    wide_at = lambda step: pl.ds(pl.multiple_of(step * wide, wide), wide)

    barrier = pltpu.get_barrier_semaphore()
    friends = [at.plane_peer(step) for step in range(1, 8)]
    friends += [at.z_peer(step) for step in range(1, depth)]
    for friend in friends:
        pl.semaphore_signal(barrier, inc=1, device_id=friend, device_id_type=pl.DeviceIdType.MESH)
    load_x = pltpu.make_async_copy(x_hbm, dy, local_s.at[0])
    load_x.start()

    def pair_part(part, pair):
        return pl.ds(pl.multiple_of(part * width + pair * PAIR, PAIR), PAIR)

    def own_slot(slot, side, columns):
        if slot < groups:
            parts = [lax.rem(place + side, 3) for place in range(3)]
            return [wqkv_ref[:, pair_part(part, 2 * slot + side)] for part in parts]
        if slot == groups:
            return [wout_ref[:, columns]]
        start = (slot - groups - 1) * width
        return [wup_ref[:, pl.ds(pl.multiple_of(start + side * half, 128), half)]]

    slots = groups + 1 + units
    for slot in range(slots):
        lane = 0
        for piece in own_slot(slot, 1 - at.c, other):
            give_out[slot, :, lane : lane + piece.shape[1]] = piece
            lane += piece.shape[1]
    vpad[...] = jnp.zeros_like(vpad)
    vpad[: vectors_ref.shape[0], : vectors_ref.shape[1]] = vectors_ref[...]
    vbuf[at.c, at.own, at.z] = vpad[...].astype(bf16)
    pl.semaphore_wait(barrier, len(friends))
    swaps = []
    for index, (low, high) in enumerate(((0, groups), (groups, slots))):
        swaps.append(
            remote(
                give_out.at[low:high], asm.at[low:high, my_rows, :],
                swap_s.at[index], swap_r.at[index], at.core,
            )
        )
    swaps.append(
        remote(wdown_ref.at[:, other], asm_down.at[my_tall, :], swap_s.at[2], swap_r.at[2], at.core)
    )
    for swap in swaps:
        swap.start()
    for slot in range(slots):
        lane = 0
        for piece in own_slot(slot, at.c, mine):
            asm[slot, my_rows, lane : lane + piece.shape[1]] = piece
            lane += piece.shape[1]
    asm_down[my_tall, :] = wdown_ref[:, mine]

    def weight_piece(block, z, place, own_half):
        side = at.c if own_half else 1 - at.c
        if z is None:
            return w.at[block, side, place]
        return w.at[block, side, place, z]

    def vector_piece(block, z, place, own_half):
        core = at.c if own_half else 1 - at.c
        if z is None:
            return vbuf.at[core, place]
        return vbuf.at[core, place, z]

    def plane(block):
        after = block - groups
        if isinstance(block, int):
            return after > 0 and after % 2 == 0, after // 2 - 1
        return jnp.logical_and(after > 0, lax.rem(after, 2) == 0), after // 2 - 1

    weights = Gather(at, weight_piece, ag_s, ag_r, plane)
    vectors = Gather(at, vector_piece, vg_s, vg_r)

    def push(block):
        def every():
            slot = jnp.where(block > groups, groups + 1 + (block - groups - 1) // 2, block)
            w[block, at.c, at.own, at.z] = asm[slot].astype(bf16)

        def one(z):
            @pl.when(at.z == z)
            def _():
                w[block, at.c, at.own] = asm_down[...].reshape(depth, slab, half).astype(bf16)

        weights.split(block, every, one)
        weights.push(block)

    def gather_even(turn):
        last, block = turn - 3, turn
        when(both(last >= 0, last < blocks), lambda: weights.stage_four(last))

        def second():
            weights.stage_two(block)
            when(block + groups < blocks, lambda: push(block + groups))

        when(block < blocks, second)

    def gather_odd(turn):
        block = turn - 1
        when(both(block >= 0, block < blocks), lambda: weights.stage_three(block))

    vectors.push(0)
    swaps[0].wait_recv()
    for block in range(groups):
        push(block)
    mark_segments(ends_ref, key_seg, query_seg)
    swaps[1].wait_recv()
    swaps[2].wait_recv()
    vectors.stage_two(0)
    gather_even(0)
    vectors.stage_three(0)
    gather_even(1)
    gather_odd(1)
    vectors.stage_four(0)
    gather_even(2)
    gather_odd(2)
    vectors.finish(0)
    gather_even(3)

    per = vectors_ref.shape[1]
    lane_inverse = (1 << 16) // per + 1
    spread_row = lax.broadcasted_iota(jnp.int32, (128, width), 0)
    spread_col = lax.broadcasted_iota(jnp.int32, (128, width), 1)
    spread_place = spread_col - ((spread_col * lane_inverse) >> 16) * per
    spread = jnp.where(spread_row == spread_place, 1.0, 0.0).astype(bf16)
    whole = jnp.zeros((16, width), f32)
    row = lax.broadcasted_iota(jnp.int32, (8 * 16, width), 0)
    col = (lax.broadcasted_iota(jnp.int32, (8 * 16, width), 1) * lane_inverse) >> 16
    core, place = row >> 6, (row >> 4) & 3
    place = jnp.where(core == 0, ((place & 1) << 1) | (place >> 1), place)
    device = place * 2 + core
    for level in range(depth):
        values = dot(vbuf[:, :, level].reshape(8 * 16, 128), spread)
        values = jnp.where(col == device + level * 8, values, 0.0).reshape(8, 16, width)
        whole = whole + jnp.sum(values, 0)
    vec[...] = whole

    def row_chunks(step):
        return [
            pl.ds(pl.multiple_of(step * ROWS + start, CHUNK), CHUNK)
            for start in range(0, ROWS, CHUNK)
        ]

    def first_norm(target, first_time):
        @pl.loop(0, rows // ROWS)
        def _(step):
            for here in row_chunks(step):
                value = dy[here, :].astype(f32)
                unit, _ = standardize(value)
                act[here, :] = (unit * vec[0:1, :] + vec[1:2, :]).astype(bf16)
                if first_time:
                    middle[here, :] = value
            if not first_time:
                target[:, rows_at(step)] = act[rows_at(step), :].T

    load_x.wait()
    first_norm(act, True)
    load_dy = pltpu.make_async_copy(cot_hbm, dy, local_s.at[0])
    load_dy.start()

    def allowed_short(tile):
        start, line = band_start(tile), query_seg[tile]

        def allowed(part):
            count = part.stop - part.start
            band = key_seg[pl.ds(pl.multiple_of(start + part.start, 32), count), :]
            return jnp.concatenate([band, band], 1) == jnp.concatenate([line, line], 1)

        return allowed

    def allowed_long(part):
        shape = (part.stop - part.start, 2 * TILE)
        return lax.broadcasted_iota(jnp.int32, shape, 0) + part.start < length_ref[0]

    third = 3 * PAIR

    def group_columns(group, offset, count):
        return pl.ds(pl.multiple_of(group * width + offset, 128), count)

    def lane_of(part, side):
        return side * third + (part - side) % 3 * PAIR

    def q_at(group, side):
        return group_columns(group, lane_of(0, side), PAIR)

    def k_at(group, side):
        return group_columns(group, lane_of(1, side), PAIR)

    def v_at(group, side):
        return group_columns(group, lane_of(2, side), PAIR)

    def kv_at(group, side):
        return group_columns(group, lane_of(1, side), 2 * PAIR)

    def far_columns(group, side):
        return pl.ds(pl.multiple_of((2 * group + side) * 2 * PAIR, 128), 2 * PAIR)

    y_blk, core_blk = (1 - at.y) * 2 + at.c, at.y * 2 + 1 - at.c
    both_blk = 3 - at.blk

    def keys_copy(group, role, incoming=False):
        columns = pl.ds(pl.multiple_of(group * 4 * PAIR, 128), 4 * PAIR)
        device = (at.y_peer, at.core, at.core)[role]
        if incoming:
            source = target = far.at[(y_blk, core_blk, both_blk)[role], :, columns]
        elif role == 2:
            source = target = far.at[y_blk, :, columns]
        else:
            source = qkv.at[SHORT_DEV:, group_columns(group, PAIR, 4 * PAIR)]
            target = far.at[at.blk, :, columns]
        return remote(source, target, kv_s.at[group, role], kv_r.at[group, role], device)

    def strips(natural):
        for side in range(2):
            for place in range(4):
                high, low = place // 2, place % 2
                chip = (low * 2 + high) if side == 0 else place
                for level in range(depth):
                    order = chip * depth + level if natural else level * 4 + chip
                    yield side, place, level, order * slab

    def flatten(target, block, natural=False):
        for side, place, level, start in strips(natural):
            target[start : start + slab, side * half : (side + 1) * half] = w[
                block, side, place, level
            ]

    @pl.loop(0, groups)
    def _(group):
        weights.finish(group)
        bias = []
        for side in range(2):
            lanes = pl.ds(pl.multiple_of((2 * group + side) * PAIR, PAIR), PAIR)
            three = [vec[4:5, lanes], jnp.zeros((1, PAIR), f32), vec[5:6, lanes]]
            bias += three[side:] + three[:side]
        flat_down[0:1, :] = jnp.concatenate(bias, 1).astype(bf16)
        flatten(flat_up, group)

        @pl.loop(0, width // wide)
        def _(step):
            made = dot(act[...], flat_up[:, wide_at(step)])
            made = made + flat_down[0:1, wide_at(step)].astype(f32)
            qkv[:, group_columns(group, step * wide, wide)] = made.astype(bf16)

        keys_copy(group, 0).start()
        keys_copy(group, 1).start()
        for side in range(2):
            far[at.blk, :, far_columns(group, side)] = qkv[SHORT_DEV:, kv_at(group, side)]
            turned[side * PAIR : (side + 1) * PAIR, :] = qkv[:SHORT_DEV, v_at(group, side)].T

        gather_odd(groups + 2 * group)

        def tile_rows(tile):
            return pl.ds(pl.multiple_of(tile * TILE, TILE), TILE)

        def slot_rows(slot):
            return slice(slot * BAND, (slot + 1) * BAND)

        def products(tile, side):
            made = unstack_heads(
                dot(
                    turned[side * PAIR : (side + 1) * PAIR, pl.ds(band_start(tile), BAND)],
                    flat_down[slot_rows(side), :wide],
                )
            )
            att[pair_lanes(group * 2 + side), tile_rows(tile)] = made.astype(bf16)

        def soften(tile, side):
            lse[tile, group * 2 + side] = softmax_into(
                out_acc.at[slot_rows(side), :wide],
                allowed_short(tile),
                flat_down.at[slot_rows(side), :wide],
            )

        def compare(tile, side):
            queries = stack_heads(qkv[tile_rows(tile), q_at(group, side)], score_scale)
            keys = qkv[pl.ds(band_start(tile), BAND), k_at(group, side)]
            out_acc[slot_rows(side), :wide] = dot_tr(keys, queries)

        @pl.loop(0, tiles + 1)
        def _(turn):
            now, last = jnp.minimum(turn, tiles - 1), jnp.maximum(turn - 1, 0)
            products(last, 0)
            soften(last, 1)
            compare(now, 0)
            products(last, 1)
            soften(now, 0)
            compare(now, 1)
            pl.when(turn == 1)(lambda: gather_even(groups + 1 + 2 * group))

            @pl.when(turn == 3)
            def _():
                gather_odd(groups + 1 + 2 * group)
                keys_copy(group, 0, True).wait_recv()
                keys_copy(group, 2).start()

            pl.when(turn == 6)(lambda: gather_even(groups + 2 + 2 * group))

    def far_pair(pair, offset):
        return pl.ds(pl.multiple_of(pair * 2 * PAIR + offset, PAIR), PAIR)

    def far_block(pair, offset):
        return far[:, :, far_pair(pair, offset)].reshape(4 * LONG_DEV, PAIR)

    gather_odd(3 * groups)
    for group in range(groups):
        keys_copy(group, 1, True).wait_recv()
        keys_copy(group, 2, True).wait_recv()

    @pl.loop(0, groups)
    def _(group):
        long_rows = lambda side: slice(side * 4 * LONG_DEV, (side + 1) * 4 * LONG_DEV)
        for side in range(2):
            queries = stack_heads(qkv[SHORT_DEV:, q_at(group, side)], score_scale)
            out_acc[long_rows(side), :wide] = dot_tr(far_block(2 * group + side, 0), queries)
        for side in range(2):
            pair = 2 * group + side
            probs = flat_down.at[: 4 * LONG_DEV, side * wide : (side + 1) * wide]
            lse[tiles, pair] = softmax_into(
                out_acc.at[long_rows(side), :wide], allowed_long, probs
            )
            made = unstack_heads(dot(far_block(pair, PAIR).T, probs[...]))
            att[pair_lanes(pair), SHORT_DEV:] = made.astype(bf16)
        pl.when(group == 0)(lambda: gather_even(3 * groups + 1))
        pl.when(group == groups - 1)(lambda: gather_odd(3 * groups + 1))

    weights.finish(groups)
    for group in range(groups):
        for role in range(3):
            keys_copy(group, role).wait_send()

    load_dy.wait()
    place = lax.broadcasted_iota(jnp.int32, (LONG_DEV, width), 0) + at.blk * LONG_DEV
    keep = place < length_ref[0]
    dy[SHORT_DEV:, :] = jnp.where(keep, dy[SHORT_DEV:, :].astype(f32), 0.0).astype(bf16)

    act[...] = att[...].T
    flatten(flat_up, groups)
    gather_even(3 * groups + 2)

    @pl.loop(0, width // wide)
    def _(step):
        columns = wide_at(step)
        made = dot(act[...], flat_up[:, columns]) + vec[6:7, columns]
        middle[:, columns] = middle[:, columns] + made

    @pl.loop(0, rows // ROWS)
    def _(step):
        for here in row_chunks(step):
            unit, _ = standardize(middle[here, :])
            h2[here, :] = (unit * vec[2:3, :] + vec[3:4, :]).astype(bf16)
        h2_tr[:, rows_at(step)] = h2[rows_at(step), :].T

    def piece(block, place):
        return w.at[block, at.c, place]

    turns = [*range(groups + 1, blocks), groups, *range(groups)]

    def landing(block, side):
        if isinstance(block, int) and block <= groups:
            return turns[turns.index(block) - 4], side
        order = block - groups - 1
        odd = jnp.logical_and(order < 4, lax.rem(order, 2) == 1)
        return (
            jnp.where(order < 4, spare + order // 2, block - 4),
            jnp.where(odd, 1 - side, side),
        )

    def to_core(block):
        place, side = landing(block, at.c)
        return remote(
            w.at[block, 1 - at.c], w.at[place, side], rs_s.at[block, 0], rs_r.at[block, 0], at.core
        )

    def going(block, index):
        sends, recvs = rs_s.at[block, index], rs_r.at[block, index]
        if index == 1:
            return remote(piece(block, at.far_two), got_a.at[block], sends, recvs, at.second)
        return remote(piece(block, at.at_first), got_b.at[block], sends, recvs, at.first)

    def along_z(block, step):
        index = 4 + step
        return remote(
            w.at[block, at.c, at.own, at.z_to(step)], got_z.at[block, step - 1],
            rs_s.at[block, index], rs_r.at[block, index], at.z_peer(step),
        )

    def to_plane(block, step):
        index = 4 + step
        return remote(
            piece(block, at.own), got_zd.at[step - 1],
            rs_s.at[block, index], rs_r.at[block, index], at.z_peer(step),
        )

    def swap_back(block, tall_one, incoming=False):
        sends, recvs = rs_s.at[block, 4], rs_r.at[block, 4]
        columns = other if incoming else mine
        if tall_one:
            return remote(
                asm_down.at[other_tall, :], red.at[pl.ds(blocks_low, tall), columns],
                sends, recvs, at.core,
            )
        return remote(
            asm.at[slot_of(block), other_rows, :], red.at[red_rows(block), columns],
            sends, recvs, at.core,
        )

    blocks_low = slots * share

    def slot_of(block):
        if isinstance(block, int):
            return block if block <= groups else groups + 1 + (block - groups - 1) // 2
        return jnp.where(block > groups, groups + 1 + (block - groups - 1) // 2, block)

    def red_rows(block):
        return pl.ds(pl.multiple_of(slot_of(block) * share, 8), share)

    def add_piece(block, place, got):
        w[block, at.c, place] = w[block, at.c, place] + got

    def scatter_one(block):
        to_core(block).wait_recv()
        where, side = landing(block, 1 - at.c)
        add_piece(block, at.far_two, w[where, side, at.far_two])
        going(block, 1).start()
        add_piece(block, at.near_two, w[where, side, at.near_two])

    def scatter_two(block):
        going(block, 1).wait_recv()
        add_piece(block, at.at_first, got_a[block, 1 - at.f])
        going(block, 3).start()
        add_piece(block, at.own, got_a[block, at.f])

    def scatter_three(block):
        going(block, 3).wait_recv()
        add_piece(block, at.own, got_b[block])

        def every():
            for step in range(1, depth):
                along_z(block, step).start()

        def one(z):
            @pl.when(at.z != z)
            def _():
                to_plane(block, lax.rem(z - at.z + depth, depth)).start()

        weights.split(block, every, one)

    def scatter_four(block):
        def every():
            total = w[block, at.c, at.own, at.z].astype(f32)
            for step in range(1, depth):
                along_z(block, step).wait_recv()
                total = total + got_z[block, step - 1].astype(f32)
            slot = slot_of(block)
            asm[slot] = total
            squares[...] += total * total
            swap_back(block, False).start()
            red[red_rows(block), mine] = asm[slot, my_rows, :]

        def one(z):
            @pl.when(at.z == z)
            def _():
                for step in range(1, depth):
                    to_plane(block, step).wait_recv()
                total = w[block, at.c, at.own].astype(f32)
                for step in range(1, depth):
                    total = total + got_zd[step - 1].astype(f32)
                asm_down[...] = total.reshape(2 * tall, half)
                squares[...] += jnp.sum(total * total, 0)
                swap_back(block, True).start()
                red[pl.ds(blocks_low, tall), mine] = asm_down[my_tall, :]

        weights.split(block, every, one)

    def scatter_end(block):
        def every():
            swap_back(block, False, True).wait_recv()
            swap_back(block, False).wait_send()
            for step in range(1, depth):
                along_z(block, step).wait_send()

        def one(z):
            @pl.when(at.z == z)
            def _():
                swap_back(block, True, True).wait_recv()
                swap_back(block, True).wait_send()

            @pl.when(at.z != z)
            def _():
                to_plane(block, lax.rem(z - at.z + depth, depth)).wait_send()

        weights.split(block, every, one)
        for index in (1, 3):
            going(block, index).wait_send()

    stages = (scatter_one, scatter_two, scatter_three, scatter_four)

    def scatter_pump(turn):
        for stage, first, pace in zip(stages, (4, 7, 11, 14), (2, 3, 3, 3)):
            if isinstance(turn, int):
                order = (turn - first) // pace
                if (turn - first) % pace == 0 and 0 <= order <= 2 * units:
                    stage(turns[order])
                continue
            late = turn - first
            due = jnp.logical_and(late >= 0, lax.rem(late, pace) == 0)
            pl.when(due)(functools.partial(stage, groups + 1 + lax.div(late, pace)))

    def give(block, gradient, natural=False):
        weights.sent(block)
        if isinstance(block, int) and block <= groups:
            to_core(turns[turns.index(block) - 2]).wait_send()
        else:
            pl.when(block > groups + 2)(lambda: to_core(block - 2).wait_send())
        low = gradient.astype(bf16)
        for side, place, level, start in strips(natural):
            w[block, side, place, level] = low[
                start : start + slab, side * half : (side + 1) * half
            ]
        to_core(block).start()

    squares[...] = jnp.zeros_like(squares)
    out_acc[...] = jnp.zeros_like(out_acc)
    dh2[...] = jnp.zeros_like(dh2)
    gvec[...] = jnp.zeros_like(gvec)

    @pl.loop(0, units)
    def _(unit):
        up, down = groups + 1 + 2 * unit, groups + 2 + 2 * unit
        weights.finish(up)
        weights.finish(down)
        flatten(flat_up, up)
        flatten(flat_down, down, True)

        @pl.loop(0, width // wide)
        def _(step):
            @pl.when(step == 0)
            def _():
                gather_odd(3 * groups + 2 + 2 * unit)
                scatter_pump(4 * unit)

            @pl.when(step == 2)
            def _():
                gather_even(3 * groups + 3 + 2 * unit)
                scatter_pump(4 * unit + 1)

            columns = wide_at(step)
            bias = vec[pl.ds(8 + unit, 1), columns]
            total = jnp.zeros((8, wide), f32)
            for half_rows in chunks_of(rows, rows // 2):
                pre_grad[:, :wide] = dot(h2[half_rows, :], flat_up[:, columns])
                pre_grad[:, wide:] = dot_tr(dy[half_rows, :], flat_down[columns, :])
                for part in chunks_of(rows // 2, CHUNK):
                    here = slice(half_rows.start + part.start, half_rows.start + part.stop)
                    made, slope = gelu_both(pre_grad[part, :wide] + bias)
                    act[here, columns] = made.astype(bf16)
                    du_low = (pre_grad[part, wide:] * slope).astype(bf16)
                    du[here, columns] = du_low
                    total = total + fold(du_low.astype(f32))
            gvec[pl.ds(8 + unit, 1), columns] = column_sum(total)

        @pl.loop(0, width // wide)
        def _(step):
            @pl.when(step == 1)
            def _():
                gather_odd(3 * groups + 3 + 2 * unit)
                scatter_pump(4 * unit + 2)

            columns = wide_at(step)
            out_acc[:, columns] += dot(act[...], flat_down[:, columns])
            dh2[:, columns] += dot_tr(du[...], flat_up[columns, :])

        gather_even(3 * groups + 4 + 2 * unit)
        scatter_pump(4 * unit + 3)
        give(up, dot(h2_tr[...], du[...]))
        give(down, dot_tl(act[...], dy[...]), True)

    sums_two[...] = jnp.zeros_like(sums_two)

    @pl.loop(0, rows // ROWS)
    def _(step):
        for turn in range(rows // ROWS):
            pl.when(step == turn)(functools.partial(scatter_pump, 4 * units + turn))
        for here in row_chunks(step):
            middle_here = middle[here, :]
            out = middle_here + (out_acc[here, :] + vec[7:8, :])
            h2[here, :] = out.astype(bf16)
            dy_here = dy[here, :].astype(f32)
            dh2_here = dh2[here, :]
            unit, inv_std = standardize(middle_here)
            dmiddle = dy_here + norm_back(dh2_here, unit, inv_std, vec[2:3, :])
            dh2[here, :] = dmiddle
            da = dmiddle.astype(bf16)
            act[here, :] = da
            sums_two[0] += fold(dh2_here * unit)
            sums_two[1] += fold(dh2_here)
            sums_two[2] += fold(da.astype(f32))
            sums_two[3] += fold(dy_here)

    for place, line in enumerate((2, 3, 6, 7)):
        gvec[line : line + 1, :] = column_sum(sums_two[place])
    flatten(flat_up, groups)

    @pl.loop(0, width // wide)
    def _(step):
        columns = wide_at(step)
        du[:, columns] = dot_tr(act[...], flat_up[columns, :]).astype(bf16)

    store_out = pltpu.make_async_copy(h2, out_hbm, local_s.at[0])
    store_out.start()
    load_again = pltpu.make_async_copy(x_hbm, dy, local_s.at[2])
    load_again.start()
    give(groups, dot(att[...], act[...]))
    load_again.wait()
    first_norm(h2_tr, False)

    after = 4 * units + rows // ROWS

    @pl.loop(0, groups)
    def _(group):
        long_rows = lambda side: slice(side * 4 * LONG_DEV, (side + 1) * 4 * LONG_DEV)

        def stacked_long(side):
            return (
                stack_heads(qkv[SHORT_DEV:, q_at(group, side)], score_scale),
                stack_heads(du[SHORT_DEV:, pair_lanes(2 * group + side)], None),
            )

        for side in range(2):
            queries, upstream = stacked_long(side)
            here, pair = long_rows(side), 2 * group + side
            out_acc[here, :wide] = dot_tr(far_block(pair, 0), queries)
            out_acc[here, wide : 2 * wide] = dot_tr(far_block(pair, PAIR), upstream)
        for side in range(2):
            queries, upstream = stacked_long(side)
            here, pair = long_rows(side), 2 * group + side
            lanes = slice(side * wide, (side + 1) * wide)
            probs = flat_down.at[: 4 * LONG_DEV, lanes]
            grad_scores = flat_up.at[: 4 * LONG_DEV, lanes]
            softmax_back_into(
                out_acc.at[here, :wide], out_acc.at[here, wide : 2 * wide], allowed_long,
                lse[tiles, pair], probs, grad_scores,
            )
            dk, dv = dot(grad_scores[...], queries), dot(probs[...], upstream)
            dq = unstack_heads(dot(far_block(pair, 0).T, grad_scores[...])) * score_scale
            qkv[SHORT_DEV:, q_at(group, side)] = dq.astype(bf16).T
            far[:, :, far_pair(pair, 0)] = dk.astype(bf16).reshape(4, LONG_DEV, PAIR)
            far[:, :, far_pair(pair, PAIR)] = dv.astype(bf16).reshape(4, LONG_DEV, PAIR)
        for turn in range(groups):
            pl.when(group == turn)(functools.partial(scatter_pump, after + turn))

    flats = (flat_up, act.at[:width, :], att.at[:, :width])

    far_one = remote(far.at[core_blk], far_got.at[0], fg_s.at[0], fg_r.at[0], at.core)
    far_two = remote(far.at[both_blk], far_got.at[1], fg_s.at[1], fg_r.at[1], at.core)
    far_three = remote(far.at[y_blk], far_got.at[2], fg_s.at[2], fg_r.at[2], at.y_peer)
    far_two.start()
    far_one.start()
    store_out.wait()
    lse[tiles + 1] = jnp.full(lse.shape[1:], 1e30, f32)
    flat_down[...] = jnp.zeros_like(flat_down)

    @pl.loop(0, groups)
    def _(group):
        middle[:SHORT_DEV, 0 : 4 * PAIR] = jnp.zeros((SHORT_DEV, 4 * PAIR), f32)
        flat_down[:BAND, 0 : 2 * wide] = jnp.zeros((BAND, 2 * wide), bf16)
        before = group - 1

        def pump(place):
            for now in range(groups):
                turn = after + groups + 5 * now + place
                pl.when(group == now)(functools.partial(scatter_pump, turn))

            @pl.when(group > 0)
            def _():
                if place == 0:
                    pl.when(group > 1)(lambda: scatter_three(group - 2))
                if place == 2:
                    pl.when(group > 1)(lambda: scatter_four(group - 2))
                if place == 1:
                    for block in range(groups - 1):
                        pl.when(before == block)(functools.partial(scatter_one, block))
                if place == 3:
                    scatter_two(before)

        pump(0)
        for side in range(2):
            turned[side * PAIR : (side + 1) * PAIR, :] = qkv[:SHORT_DEV, k_at(group, side)].T

        def tile_rows(tile):
            return pl.ds(pl.multiple_of(tile * TILE, TILE), TILE)

        def slot_rows(slot):
            return slice(slot * BAND, (slot + 1) * BAND)

        def stacked(tile, side):
            here = tile_rows(tile)
            return (
                stack_heads(qkv[here, q_at(group, side)], score_scale),
                stack_heads(du[here, pair_lanes(group * 2 + side)], None),
            )

        def products(tile, side, target):
            queries, upstream = stacked(tile, side)
            band = pl.ds(band_start(tile), BAND)
            probs = flat_down[slot_rows(side), :wide]
            grad_scores = flat_down[slot_rows(side), wide : 2 * wide]
            start = side * 2 * PAIR
            middle[band, start : start + PAIR] += dot(grad_scores, queries)
            middle[band, start + PAIR : start + 2 * PAIR] += dot(probs, upstream)
            keys_tr = turned[side * PAIR : (side + 1) * PAIR, band]
            dq = unstack_heads(dot(keys_tr, grad_scores)) * score_scale
            h2[tile_rows(target), pair_lanes(group * 2 + side)] = dq.astype(bf16).T

        def soften(tile, side, source):
            softmax_back_into(
                middle.at[slot_rows(side), 2 * wide : 3 * wide],
                out_acc.at[slot_rows(side), :wide],
                allowed_short(tile),
                lse[source, group * 2 + side],
                flat_down.at[slot_rows(side), :wide],
                flat_down.at[slot_rows(side), wide : 2 * wide],
            )

        def compare(tile, side):
            queries, upstream = stacked(tile, side)
            band = pl.ds(band_start(tile), BAND)
            middle[slot_rows(side), 2 * wide : 3 * wide] = dot_tr(
                qkv[band, k_at(group, side)], queries
            )
            out_acc[slot_rows(side), :wide] = dot_tr(qkv[band, v_at(group, side)], upstream)

        @pl.loop(0, tiles + 1)
        def _(turn):
            now, last = jnp.minimum(turn, tiles - 1), jnp.maximum(turn - 1, 0)
            target = jnp.where(turn == 0, tiles, last)
            products(last, 0, target)
            soften(last, 1, jnp.where(turn == 0, tiles + 1, last))
            compare(now, 0)
            products(last, 1, target)
            soften(now, 0, now)
            compare(now, 1)

            @pl.when(turn == 1)
            def _():
                pump(1)

                @pl.when(group == 0)
                def _():
                    far_two.wait_recv()
                    far[y_blk] = far[y_blk] + far_got[1]
                    far_three.start()

            pl.when(turn == 3)(lambda: pump(2))
            pl.when(turn == 6)(lambda: pump(3))

        for side in range(2):
            qkv[:SHORT_DEV, q_at(group, side)] = h2[:SHORT_DEV, pair_lanes(group * 2 + side)]

        @pl.when(group == 0)
        def _():
            far_one.wait_recv()
            far_three.wait_recv()

        for side in range(2):
            start = side * 2 * PAIR
            qkv[:SHORT_DEV, kv_at(group, side)] = middle[
                :SHORT_DEV, start : start + 2 * PAIR
            ].astype(bf16)
            near_at = far_columns(group, side)
            near = far[at.blk, :, near_at].astype(f32) + far_got[0, :, near_at].astype(f32)
            near = near + far_got[2, :, near_at].astype(f32)
            qkv[SHORT_DEV:, kv_at(group, side)] = near.astype(bf16)

        for block, target in enumerate(flats):
            pl.when(group == block)(functools.partial(flatten, target, block))
        gradient = dot(h2_tr[...], qkv[:, group_columns(group, 0, width)])
        for block in range(groups):
            pl.when(group == block)(functools.partial(give, block, gradient))

        pump(4)
        sums = column_sum(qkv[:, group_columns(group, 0, width)].astype(f32))
        for side in range(2):
            own = pl.ds(pl.multiple_of((2 * group + side) * PAIR, PAIR), PAIR)
            for part, line in ((0, 4), (2, 5)):
                lane = lane_of(part, side)
                gvec[line : line + 1, own] = sums[:, lane : lane + PAIR]

    def input_rows(step):
        sums_two[0:2] = jnp.zeros((2, 8, width), f32)

        @pl.loop(step * (rows // ROWS // 2), (step + 1) * (rows // ROWS // 2))
        def _(block):
            for here in row_chunks(block):
                unit, inv_std = standardize(dy[here, :].astype(f32))
                dh1 = out_acc[here, :]
                middle[here, :] = dh2[here, :] + norm_back(dh1, unit, inv_std, vec[0:1, :])
                sums_two[0] += fold(dh1 * unit)
                sums_two[1] += fold(dh1)

        return column_sum(sums_two[0]), column_sum(sums_two[1])

    latest = groups - 1
    scatter_three(latest - 1)
    scatter_one(latest)

    @pl.loop(0, width // wide)
    def _(step):
        columns = wide_at(step)
        made = jnp.zeros((rows, wide), f32)
        for group, flat in enumerate(flats):
            made = made + dot_tr(qkv[:, group * width : (group + 1) * width], flat[columns, :])
        out_acc[:, columns] = made

    gain_low, shift_low = input_rows(0)
    scatter_pump(after + 6 * groups)
    scatter_four(latest - 1)
    gain_high, shift_high = input_rows(1)
    store_grad = pltpu.make_async_copy(middle, grad_hbm, local_s.at[1])
    store_grad.start()
    gvec[0:1, :] = gain_low + gain_high
    gvec[1:2, :] = shift_low + shift_high
    exchange = Exchange(at, v_sent, v_got, v_got_z, ex_s, ex_r, 0)
    exchange.begin(gvec[...])
    scatter_two(latest)
    exchange.step()
    scatter_three(latest)
    exchange.step()
    exchange.step()
    scatter_four(latest)

    weight_square = jnp.sum(squares[...], keepdims=True)
    norms = ShortExchange(at, n_sent, n_got_z, n_got, no_s, no_r)
    norm_copies = norms.along_z(jnp.broadcast_to(weight_square, n_sent.shape[1:]))
    vector_sum = exchange.step()
    device = at.dp * 4 + at.blk
    turn_by = lax.rem(width - device * per, width)
    rvec_ref[...] = pltpu.roll(vector_sum, turn_by, 1)[:, :128]
    vector_square = jnp.sum(vector_sum * vector_sum, keepdims=True)
    norm_copies = norms.in_plane(norms.finish(n_got_z, norm_copies))

    @pl.loop(0, blocks)
    def _(block):
        @pl.when(block > groups)
        def _():
            scatter_end(block)

    for block in range(groups + 1):
        scatter_end(block)
    for block in turns[-2:]:
        to_core(block).wait_send()
    for group in range(groups):
        for side in range(2):
            for part in range(3):
                start = part * width + (2 * group + side) * PAIR
                lane = lane_of(part, side)
                rqkv_ref[:, start : start + PAIR] = red[
                    group * share : (group + 1) * share, lane : lane + PAIR
                ]
    rout_ref[...] = red[groups * share : (groups + 1) * share, :]
    for unit in range(units):
        start = (groups + 1 + unit) * share
        rup_ref[:, unit * width : (unit + 1) * width] = red[start : start + share, :]
    rdown_ref[...] = red[blocks_low : blocks_low + tall, :]
    far_one.wait_send()
    far_two.wait_send()
    far_three.wait_send()
    for swap in swaps:
        swap.wait_send()
    vectors.sent(0)
    norm_ref[...] = jnp.sqrt(norms.finish(n_got, norm_copies) + vector_square)
    store_grad.wait()


def run_fused(depth, patches, cotangent, ends, length, w_qkv, w_out, w_up, w_down, vectors):
    rows, width = patches.shape
    share = w_out.shape[0]
    tall = w_down.shape[0]
    bf16, f32 = jnp.bfloat16, jnp.float32
    slab = 2 * share
    lanes4 = 2 * PAIR
    groups = width // lanes4
    units = w_up.shape[1] // width
    slots = groups + 1 + units
    blocks = slots + units
    half = width // 2
    tiles = SHORT_DEV // TILE
    vmem = lambda shape, kind: pltpu.VMEM(shape, kind)
    dma = pltpu.SemaphoreType.DMA
    copies = depth + 3
    scratch = [
        vmem((blocks + 2, 2, 4, depth, slab, half), bf16),
        vmem((2, 4, depth, 16, 128), bf16),
        vmem((16, 128), f32),
        vmem((slots, share, half), f32),
        vmem((slots, slab, half), f32),
        vmem((2 * tall, half), f32),
        vmem((16, width), f32),
        vmem((rows, 3 * width), bf16),
        vmem((width, rows), bf16),
        vmem((rows, width), f32),
        vmem((rows, width), bf16),
        vmem((rows, width), bf16),
        vmem((rows, width), bf16),
        vmem((rows, width), f32),
        vmem((rows, width), f32),
        vmem((rows, width), bf16),
        vmem((4, LONG_DEV, 2 * width), bf16),
        vmem((3, LONG_DEV, 2 * width), bf16),
        vmem((tiles + 2, width // PAIR, 1, 2 * TILE), f32),
        vmem((SHORT_DEV, TILE), f32),
        vmem((tiles, 1, TILE), f32),
        vmem((lanes4, SHORT_DEV), bf16),
        vmem((width, rows), bf16),
        vmem((width, width), bf16),
        vmem((width, width), bf16),
        vmem((rows // 2, 4 * PAIR), f32),
        vmem((blocks, 2, depth, slab, half), bf16),
        vmem((blocks, depth, slab, half), bf16),
        vmem((blocks, depth - 1, slab, half), bf16),
        vmem((depth - 1, depth, slab, half), bf16),
        vmem((slots * share + tall, width), f32),
        vmem((slab, half), f32),
        vmem((16, width), f32),
        vmem((4, 8, width), f32),
        vmem((4, 16, width), f32),
        vmem((3, 16, width), f32),
        vmem((depth, 16, width), f32),
        vmem((2, 8, 128), f32),
        vmem((8, 8, 128), f32),
        vmem((depth, 8, 128), f32),
    ]
    scratch += [dma((3,))] * 2 + [dma((blocks, copies))] * 2 + [dma((1, copies))] * 2
    scratch += [dma((groups, 3))] * 2 + [dma((3,))] * 2 + [dma((blocks, 4 + depth))] * 2
    scratch += [dma((1, 3 + depth))] * 2 + [dma((depth + 6,))] * 2 + [dma((3,))]
    in_vmem = pl.BlockSpec(memory_space=pltpu.VMEM)
    in_smem = pl.BlockSpec(memory_space=pltpu.SMEM)
    anywhere = pl.BlockSpec(memory_space=pl.ANY)
    return pl.pallas_call(
        functools.partial(fused_kernel, depth),
        out_shape=[
            jax.ShapeDtypeStruct((rows, width), bf16),
            jax.ShapeDtypeStruct((rows, width), f32),
            jax.ShapeDtypeStruct(w_qkv.shape, f32),
            jax.ShapeDtypeStruct(w_out.shape, f32),
            jax.ShapeDtypeStruct(w_up.shape, f32),
            jax.ShapeDtypeStruct(w_down.shape, f32),
            jax.ShapeDtypeStruct((16, 128), f32),
            jax.ShapeDtypeStruct((8, 128), f32),
        ],
        in_specs=[in_smem] * 2 + [in_vmem] * 5 + [anywhere] * 2,
        out_specs=[anywhere] * 2 + [in_vmem] * 6,
        scratch_shapes=scratch,
        compiler_params=pltpu.CompilerParams(
            vmem_limit_bytes=FUSED_VMEM, collective_id=0, has_side_effects=True
        ),
    )(ends, length, w_qkv, w_out, w_up, w_down, vectors, patches, cotangent)


def adamw_kernel(*refs):
    out_in, grad_in, norm_ref, out_out, grad_out, total_ref = *refs[:3], *refs[23:26]
    sources = [refs[3 + 5 * kind : 8 + 5 * kind] for kind in range(4)]
    targets = [refs[26 + 5 * kind : 31 + 5 * kind] for kind in range(4)]
    through, sems = refs[46:48], refs[48]
    loads, stores = [], []
    for place, (source, target) in enumerate(((out_in, out_out), (grad_in, grad_out))):
        loads.append(pltpu.make_async_copy(source, through[place], sems.at[place]))
        stores.append(pltpu.make_async_copy(through[place], target, sems.at[2 + place]))
    for load in loads:
        load.start()
    total_ref[...] = norm_ref[0:1, 0:1]
    factor = 1.0 / jnp.maximum(norm_ref[0:1, 0:1], 1.0)
    for load, store in zip(loads, stores):
        load.wait()
        store.start()
    for place in range(5):
        weight, first, second, gradient = (source[place] for source in sources)
        rate, decay = (rate_vector, 0.0) if place == 4 else (rate_matrix, decay_weight)
        lines, columns = weight.shape
        new = adamw_step(
            weight[...], gradient[:lines, :columns] * factor, first[...], second[...], rate, decay
        )
        for target, value in zip(targets, (*new, new[0])):
            target[place][...] = value.astype(target[place].dtype)
    for store in stores:
        store.wait()


def run_adamw(result, input_grad, norm, weights, firsts, seconds, gradients):
    f32 = jnp.float32
    outs = [jax.ShapeDtypeStruct(part.shape, part.dtype) for part in (result, input_grad)]
    outs.append(jax.ShapeDtypeStruct((1, 1), f32))
    for kind in (f32, f32, f32, jnp.bfloat16):
        outs += [jax.ShapeDtypeStruct(part.shape, kind) for part in weights]
    in_vmem, anywhere = pl.BlockSpec(memory_space=pltpu.VMEM), pl.BlockSpec(memory_space=pl.ANY)
    found = pl.pallas_call(
        adamw_kernel,
        out_shape=outs,
        in_specs=[anywhere] * 2 + [in_vmem] * 21,
        out_specs=[anywhere] * 2 + [in_vmem] * 21,
        scratch_shapes=[
            pltpu.VMEM(result.shape, result.dtype),
            pltpu.VMEM(input_grad.shape, input_grad.dtype),
            pltpu.SemaphoreType.DMA((4,)),
        ],
        compiler_params=pltpu.CompilerParams(vmem_limit_bytes=VMEM_MOST),
    )(result, input_grad, norm, *weights, *firsts, *seconds, *gradients)
    return found[0], found[1], found[2].reshape(()), *found[3:]


def adamw_step(weight, gradient, first_moment, second_moment, rate, decay):
    first_new = beta_first * first_moment + (1.0 - beta_first) * gradient
    second_new = beta_second * second_moment + (1.0 - beta_second) * gradient * gradient
    first_hat = first_new / (1.0 - beta_first**STEP)
    second_hat = second_new / (1.0 - beta_second**STEP)
    weight_new = weight - rate * (first_hat / (jnp.sqrt(second_hat) + eps_adam) + decay * weight)
    return (weight_new, first_new, second_new)


def gather_parameters(weights, vectors):
    low = [w.astype(jnp.bfloat16) for w in weights] + [vectors.astype(jnp.bfloat16)]
    flat = jnp.concatenate([part.reshape(-1) for part in low])
    flat = jnp.pad(flat, (0, -flat.size % 4096)).reshape(-1, 128)
    whole = lax.all_gather(flat, ("dp", "blk"), axis=0, tiled=True)
    whole = whole.reshape(-1, flat.size)
    found, at = [], 0
    for part in low[:-1]:
        piece = whole[:, at : at + part.size]
        found.append(piece.reshape(-1, part.shape[1]))
        at += part.size
    piece = whole[:, at : at + vectors.size].reshape(-1, *vectors.shape)
    found.append(piece.transpose(1, 0, 2).reshape(vectors.shape[0], -1))
    return found


def layer_by_parts(
    patches, cotangent, short_lengths, long_lengths, w_qkv, w_out, w_up, w_down, vectors
):
    rows, width = patches.shape
    bf16, f32 = jnp.bfloat16, jnp.float32
    full_qkv, full_out, full_up, full_down, full_vec = gather_parameters(
        (w_qkv, w_out, w_up, w_down), vectors
    )
    params = full_vec.astype(f32)

    hidden_one, projected = call(
        qkv_phase, [((rows, width), bf16), ((rows, 3 * width), bf16)]
    )(patches, params, full_qkv)
    far = lax.all_gather(projected[SHORT_DEV:, width:], "blk", axis=0, tiled=True)
    tiles, pairs = SHORT_DEV // TILE, width // PAIR
    marks = [pltpu.VMEM((SHORT_DEV, TILE), f32), pltpu.VMEM((tiles, 1, TILE), f32)]
    attended, lse, middle, hidden_two = call(
        forward_kernel,
        [
            ((rows, width), bf16),
            ((tiles + 1, pairs, 1, 2 * TILE), f32),
            ((rows, width), f32),
            ((rows, width), bf16),
        ],
        scratch=marks,
        smem=(0, 1),
    )(short_lengths, long_lengths, patches, params, projected, far, full_out)

    long_place = lax.axis_index("blk") * LONG_DEV + jnp.arange(LONG_DEV, dtype=jnp.int32)
    keep = jnp.concatenate([jnp.ones((SHORT_DEV,), bool), long_place < long_lengths[0]])
    grad_low = jnp.where(keep[:, None], cotangent, jnp.zeros_like(cotangent))
    blocks = full_up.shape[1] // width
    result, grad_hidden_two, grad_up, grad_down, grad_bias_up = run_mlp(
        hidden_two, grad_low, middle, full_up, full_down,
        params[8 : 8 + blocks].reshape(blocks, 1, width), params[7:8],
    )
    scatter = functools.partial(
        lax.psum_scatter, axis_name=("dp", "blk"), scatter_dimension=0, tiled=True
    )
    red_up = scatter(grad_up)
    red_down = scatter(grad_down)

    grad_middle, grad_att, sums_two, grad_out = call(
        middle_back_kernel,
        [
            ((rows, width), f32),
            ((rows, width), bf16),
            ((4, width), f32),
            ((width, width), f32),
        ],
        scratch=[pltpu.VMEM((rows, width), bf16)],
    )(grad_low, middle, grad_hidden_two, params, full_out, attended)
    red_out = scatter(grad_out)

    mixed, far_grad = call(
        attention_back_kernel,
        [((rows, 3 * width), bf16), ((far.shape[0], 2 * width), bf16)],
        scratch=marks + [pltpu.VMEM((SHORT_DEV, 2 * PAIR), f32)] * 2,
        smem=(0, 1),
    )(short_lengths, long_lengths, projected, far, lse, grad_att)
    near = lax.psum_scatter(far_grad, "blk", scatter_dimension=0, tiled=True)
    input_grad, grad_qkv, sums_one = call(
        input_back_kernel,
        [((rows, width), f32), ((width, 3 * width), f32), ((4, width), f32)],
        scratch=[pltpu.VMEM((rows, 3 * width), bf16)],
    )(patches, hidden_one, mixed, near, params, full_qkv, grad_middle)
    red_qkv = scatter(grad_qkv)

    grad_vec = jnp.concatenate(
        [sums_one[0:2], sums_two[0:2], sums_one[2:4], sums_two[2:4], grad_bias_up.reshape(-1, width)], 0
    )
    red_vec = lax.psum_scatter(grad_vec, ("dp", "blk"), scatter_dimension=1, tiled=True)
    reduced = (red_qkv, red_out, red_up, red_down, red_vec)
    grad_norm = jnp.sqrt(
        lax.psum(sum(jnp.sum(part * part) for part in reduced), ("dp", "blk"))
    )
    return result, input_grad, grad_norm, reduced


def fits_one(patches, w_out):
    dp, blk = lax.axis_size("dp"), lax.axis_size("blk")
    share, width = w_out.shape
    return blk == 4 and dp % 2 == 0 and 2 * share % 16 == 0 and dp * blk * share == width


def per_device(
    patches, cotangent, short_lengths, long_lengths,
    w_qkv, w_out, w_up, w_down, vectors,
    first_qkv, first_out, first_up, first_down, first_vectors,
    second_qkv, second_out, second_up, second_down, second_vectors,
):
    layer = (patches, cotangent, short_lengths, long_lengths)
    weights = (w_qkv, w_out, w_up, w_down, vectors)
    if fits_one(patches, w_out):
        depth = lax.axis_size("dp") // 2
        result, input_grad, *gradients, norm = run_fused(depth, *layer, *weights)
    else:
        result, input_grad, grad_norm, gradients = layer_by_parts(*layer, *weights)
        norm = jnp.broadcast_to(grad_norm, (8, 128))
    firsts = (first_qkv, first_out, first_up, first_down, first_vectors)
    seconds = (second_qkv, second_out, second_up, second_down, second_vectors)
    return run_adamw(result, input_grad, norm, weights, firsts, seconds, gradients)


def solution(mesh):
    rows = P(("dp", "blk"), None)
    columns = P(None, ("dp", "blk"))
    group = (rows,) * 4 + (columns,)
    return jax.shard_map(
        per_device,
        mesh=mesh,
        in_specs=(rows, rows, rows, P("dp")) + group * 3,
        out_specs=(rows, rows, P()) + group * 4,
        check_vma=False,
    )
```
